32 devices in a mesh: groups: 2 (over x), owner: 16 (over z, y, core).
Axes of the slice: x: 2, y: 2, z: 4, core: 2. Of those that a mesh axis runs over, the one named last changes fastest.
Arguments:
- features: bfloat16 [256, 384, 256], P(('groups', 'owner')), parts along dimension 0, may hold values from -8 to 8
- pairs: int32 [1280, 2], P(('groups', 'owner')), parts along dimension 0, may hold values from 0 to 127, as said below
Outputs:
- confidence: bfloat16 [256, 384], P(('groups', 'owner')), parts along dimension 0
The draws below stay inside these ranges and needn't reach their ends.
There are 2 independent parts, one for each index of `groups`. The reference program is written for one: setup_inputs(seed, part) draws one part's arguments, and reference() takes and returns one part's arrays. A program takes and returns all parts, laid end to end along the dimension named above; each array names one. Nothing has to cross between parts.
Inputs may be any that keep to these rules, and one draw needn't show every extreme that they name: View v is held by owner index v // 8; pair row p is held by owner index p // 40. The 40 pairs of one device name exactly 40 distinct views, each in exactly two of its pairs and never twice in one pair. Among the views named by one device's pairs, the count held by any one owner is at most 3, and for one owner it equals 3 at every device.
All inputs are finite; a program needn't handle non-finite values.
Results may differ from the reference program's by a relative error of at most 0.001.
Values may be sent and summed in bfloat16 or wider, within the bound.
No kernel may reach another device: no remote copies, remote signals or barrier semaphores. Data moves between devices by JAX's collectives and lax.ppermute only.
A program may use at most 128 MiB of HBM per device.

```python
import jax
import jax.numpy as jnp
from jax import lax

C = 256
L = 384
VIEWS_DEV = 8
PAIRS_DEV = 40
VIEWS = 128
PAIRS = 640
N_OWNER = 16


def draw_features(key, part):
    key = jax.random.fold_in(key, 11)
    key_base = jax.random.fold_in(key, 0)
    base = jnp.clip(2.2 * jax.random.normal(key_base, (VIEWS, L, C), jnp.float32), -8.0, 8.0)
    return base.astype(jnp.bfloat16)


def draw_pairs(key, part):
    key = jax.random.fold_in(key, 23)
    key_hub, key_rest = jax.random.split(key)
    busiest = jax.random.randint(key_hub, (), 0, N_OWNER)
    worker_keys = jax.random.split(key_rest, N_OWNER)

    def worker_pairs(worker_key):
        key_perm, key_first, key_second, key_shift, key_flip, key_order = jax.random.split(worker_key, 6)
        shuffled = jax.random.permutation(key_perm, N_OWNER)
        located = jnp.argmax(shuffled == busiest)
        shuffled = shuffled.at[located].set(shuffled[0]).at[0].set(busiest)
        first_pick = jax.random.randint(key_first, (N_OWNER,), 0, VIEWS_DEV)
        second_pick = jax.random.randint(key_second, (N_OWNER,), 0, VIEWS_DEV)
        offsets = jnp.minimum(first_pick, second_pick)
        position = jnp.arange(PAIRS_DEV)
        holder = shuffled[position % N_OWNER]
        local_view = (offsets[holder] + position // N_OWNER) % VIEWS_DEV
        view_ids = holder * VIEWS_DEV + local_view
        offset_pair = jax.random.randint(key_shift, (), 1, PAIRS_DEV)
        partner = view_ids[(position + offset_pair) % PAIRS_DEV]
        flipped = jax.random.randint(key_flip, (PAIRS_DEV,), 0, 2)
        left_ids = jnp.where(flipped == 1, partner, view_ids)
        right_ids = jnp.where(flipped == 1, view_ids, partner)
        ordering = jax.random.permutation(key_order, PAIRS_DEV)
        return jnp.stack([left_ids, right_ids], axis=1)[ordering]
    return jax.vmap(worker_pairs)(worker_keys).reshape(PAIRS, 2).astype(jnp.int32)


def setup_inputs(seed: int = 0, part: int = 0) -> dict:
    streams_of = jax.random.split(jax.random.key(seed), 3)
    part_keys = jax.random.split(jax.random.fold_in(streams_of[2], part), 3)
    features = draw_features(jax.random.fold_in(jax.random.fold_in(streams_of[2], part), 71), part)
    pairs = draw_pairs(jax.random.fold_in(jax.random.fold_in(streams_of[2], part), 71), part)
    return dict(features=features, pairs=pairs)


def dual_confidence(left_tokens, right_tokens, score_scale):
    scores = jnp.dot(left_tokens, right_tokens.T, preferred_element_type=jnp.float32) * score_scale
    row_peak = jnp.max(scores, axis=1, keepdims=True)
    row_total = row_peak + jnp.log(jnp.sum(jnp.exp(scores - row_peak), axis=1, keepdims=True))
    col_peak = jnp.max(scores, axis=0, keepdims=True)
    col_total = col_peak + jnp.log(jnp.sum(jnp.exp(scores - col_peak), axis=0, keepdims=True))
    joint = jnp.exp((scores - row_total) + (scores - col_total))
    return jnp.max(joint, axis=1).astype(jnp.bfloat16), jnp.max(joint, axis=0).astype(jnp.bfloat16)


def reference(features, pairs):
    score_scale = 10.0 / C
    initial = jnp.zeros((VIEWS, L), jnp.bfloat16)

    def advance(current, pair_row):
        left_view = pair_row[0]
        right_view = pair_row[1]
        row_conf, col_conf = dual_confidence(features[left_view], features[right_view], score_scale)
        current = current.at[left_view].max(row_conf)
        current = current.at[right_view].max(col_conf)
        return current, None

    result, unused = lax.scan(advance, initial, pairs)
    return result
```

```python
import functools
import math

import jax
import jax.numpy as jnp
import numpy as np
from jax import lax
from jax.experimental import pallas as pl
from jax.experimental.pallas import tpu as pltpu
from jax.sharding import PartitionSpec as P

LANES = 128
SUM_LOW, SUM_HIGH = 1e-28, 1e36


def small_slice_flows():
    at = lambda z, y, c: (z * 2 + y) * 2 + c
    yc = [(y, c) for y in range(2) for c in range(2)]
    to_two = [(at(1, y, c), at(2, y, c)) for y, c in yc] + [(at(0, y, c), at(1, y, c)) for y, c in yc]
    far_to_two = [(at(0, y, c), at(2, y, c)) for y, c in yc]
    swap_y = [(at(z, y, c), at(z, 1 - y, c)) for z in range(4) for y, c in yc]
    swap_high = [(at(3, y, c), at(2, y, c)) for y, c in yc] + [(at(2, y, c), at(3, y, c)) for y, c in yc]
    cross_high = [(at(3, 1 - y, c), at(2, y, c)) for y, c in yc]
    swap_core = [(i, i ^ 1) for i in range(16)]
    return [
        (0, to_two),
        (0, swap_high),
        (0, swap_y),
        (0, far_to_two),
        (0, cross_high),
        (1, swap_core),
        (2, swap_core),
        (3, swap_core),
        (4, swap_core),
    ]


def cyclic_flows(owners):
    step = max(1, math.isqrt(owners // 2))
    reach = set(range(step))
    top = step - 1
    while top < owners // 2:
        top += step
        reach.add(top)
    reach = sorted(d % owners for d in reach if d % owners)
    return [(0, [((i + d) % owners, i) for i in range(owners)]) for d in dict.fromkeys(reach)]


@functools.lru_cache(None)
def make_plan(owners):
    flows = small_slice_flows() if owners == 16 else cyclic_flows(owners)
    held = [[d] for d in range(owners)]
    for source, perm in flows:
        arrived = {t: held[s][source] for s, t in perm}
        for d in range(owners):
            held[d].append(arrived.get(d, -1))
    first = [{} for _ in range(owners)]
    for d in range(owners):
        for k, o in enumerate(held[d]):
            if o >= 0:
                first[d].setdefault(o, k)
    table = np.zeros((owners, owners, owners), np.int32)
    load = np.zeros(owners)
    choices = []
    for a in range(owners):
        for b in range(a, owners):
            at = [d for d in range(owners) if a in first[d] and b in first[d]]
            assert at
            choices.append((len(at), a, b, at))
    for _, a, b, at in sorted(choices):
        d = min(at, key=lambda d: (load[d], d))
        load[d] += 1 if a == b else 2
        table[d, a, b] = first[d][a] * 64 + first[d][b] + 1
        table[d, b, a] = first[d][b] * 64 + first[d][a] + 1
    return flows, table


def pair_lists(pairs, mine, views_dev):
    count, owners = pairs.shape[0], mine.shape[0]
    left, right = pairs[:, 0], pairs[:, 1]
    is_left = (left // views_dev)[:, None] == jnp.arange(owners)[None, :]
    is_right = (right // views_dev)[:, None] == jnp.arange(owners)[None, :]
    row = jnp.dot(is_left.astype(jnp.float32), mine.astype(jnp.float32), precision=lax.Precision.HIGHEST)
    found = jnp.sum(jnp.where(is_right, row, 0.0), axis=1).astype(jnp.int32)
    chosen = found > 0
    buffers = jnp.maximum(found - 1, 0)
    left_slot = (buffers // 64) * views_dev + left % views_dev
    right_slot = (buffers % 64) * views_dev + right % views_dev
    place = jnp.arange(count)
    rank = jnp.sum((place[None, :] < place[:, None]) & chosen[None, :], axis=1)
    picker = (rank[None, :] == place[:, None]) & chosen[None, :]
    slots = jnp.sum(jnp.where(picker, (left_slot * 1024 + right_slot)[None, :], 0), axis=1)
    views = jnp.sum(jnp.where(picker, (left * 1024 + right)[None, :], 0), axis=1)
    return jnp.sum(chosen.astype(jnp.int32)).reshape(1), slots, views


def kernel(views_dev, score_scale, count_ref, slots_ref, views_ref, *refs):
    sources = refs[:-9]
    out_ref, left_buf, right_buf, scores, by_row, by_col, low, high, sems = refs[-9:]
    length = left_buf.shape[1]
    total = count_ref[0]

    def start(slot, dst, sem):
        def branch(lo, hi, buffer):
            if hi - lo == 1:
                pltpu.make_async_copy(sources[lo].at[lax.rem(slot, views_dev)], dst, sem).start()
                return
            mid = (lo + hi) // 2
            pl.when(buffer < mid)(lambda: branch(lo, mid, buffer))
            pl.when(buffer >= mid)(lambda: branch(mid, hi, buffer))

        branch(0, len(sources), lax.div(slot, views_dev))

    def fetch(p):
        packed = slots_ref[p]
        half = lax.rem(p, 2)
        start(lax.shift_right_logical(packed, 10), left_buf.at[half], sems.at[half])
        start(lax.bitwise_and(packed, 1023), right_buf.at[half], sems.at[half])

    def arrive(half):
        pltpu.make_async_copy(sources[0].at[0], left_buf.at[half], sems.at[half]).wait()
        pltpu.make_async_copy(sources[0].at[0], right_buf.at[half], sems.at[half]).wait()

    def record(p, row_conf, col_conf):
        packed = views_ref[p]
        left, right = lax.shift_right_logical(packed, 10), lax.bitwise_and(packed, 1023)
        for tile in range(by_row.shape[1] // LANES):
            lane = lax.broadcasted_iota(jnp.int32, (length, LANES), 1) + tile * LANES
            at = (slice(None), slice(tile * LANES, (tile + 1) * LANES))
            by_row[at] = jnp.maximum(by_row[at], jnp.where(lane == left, row_conf, 0.0))
        by_col[pl.ds(right, 1), :] = jnp.maximum(by_col[pl.ds(right, 1), :], col_conf)

    def product(half):
        return lax.dot_general(
            left_buf[half],
            right_buf[half],
            (((1,), (1,)), ((), ())),
            preferred_element_type=jnp.float32,
        )

    def plain(p, half):
        weight = jnp.exp2(product(half) * (score_scale / math.log(2.0)))
        row_sum = jnp.sum(weight, axis=1, keepdims=True)
        col_sum = jnp.sum(weight, axis=0, keepdims=True)
        low[...] = jnp.minimum(low[...], jnp.minimum(jnp.min(row_sum), jnp.min(col_sum)))
        high[...] = jnp.maximum(high[...], jnp.maximum(jnp.max(row_sum), jnp.max(col_sum)))
        row_inv, col_inv = lax.rsqrt(row_sum), lax.rsqrt(col_sum)
        row_top = jnp.max(weight * col_inv, axis=1, keepdims=True) * row_inv
        col_top = jnp.max(weight * row_inv, axis=0, keepdims=True) * col_inv
        record(p, row_top * row_top, col_top * col_top)

    def shifted(p, half):
        scores[...] = product(half) * score_scale
        value = scores[...]
        row_peak = jnp.max(value, axis=1, keepdims=True)
        row_total = row_peak + jnp.log(jnp.sum(jnp.exp(value - row_peak), axis=1, keepdims=True))
        col_peak = jnp.max(value, axis=0, keepdims=True)
        col_total = col_peak + jnp.log(jnp.sum(jnp.exp(value - col_peak), axis=0, keepdims=True))
        value = (value - row_total) + (value - col_total)
        record(p, jnp.exp(jnp.max(value, axis=1, keepdims=True)), jnp.exp(jnp.max(value, axis=0, keepdims=True)))

    def sweep(work):
        by_row[...] = jnp.zeros_like(by_row)
        by_col[...] = jnp.zeros_like(by_col)
        pl.when(total > 0)(lambda: fetch(0))

        def body(p, carry):
            half = lax.rem(p, 2)
            pl.when(p + 1 < total)(lambda: fetch(p + 1))
            arrive(half)
            work(p, half)
            return carry

        lax.fori_loop(0, total, body, 0)

    low[...] = jnp.ones_like(low)
    high[...] = jnp.ones_like(high)
    sweep(plain)
    fine = (jnp.min(low[...]) >= SUM_LOW) & (jnp.max(high[...]) <= SUM_HIGH)
    pl.when(jnp.logical_not(fine))(lambda: sweep(shifted))
    out_ref[...] = jnp.maximum(by_row[...].T, by_col[...]).astype(jnp.bfloat16)


def confidences(count, slots, views, sources, score_scale, views_all):
    views_dev, length, width = sources[0].shape
    padded = (views_all + LANES - 1) // LANES * LANES
    smem = pl.BlockSpec(memory_space=pltpu.SMEM)
    return pl.pallas_call(
        functools.partial(kernel, views_dev, score_scale),
        out_shape=jax.ShapeDtypeStruct((padded, length), jnp.bfloat16),
        in_specs=[smem] * 3 + [pl.BlockSpec(memory_space=pl.ANY)] * len(sources),
        out_specs=pl.BlockSpec(memory_space=pltpu.VMEM),
        scratch_shapes=[
            pltpu.VMEM((2, length, width), jnp.bfloat16),
            pltpu.VMEM((2, length, width), jnp.bfloat16),
            pltpu.VMEM((length, length), jnp.float32),
            pltpu.VMEM((length, padded), jnp.float32),
            pltpu.VMEM((padded, length), jnp.float32),
            pltpu.VMEM((8, LANES), jnp.float32),
            pltpu.VMEM((8, LANES), jnp.float32),
            pltpu.SemaphoreType.DMA((2,)),
        ],
        compiler_params=pltpu.CompilerParams(vmem_limit_bytes=16 * 1024 * 1024),
    )(count, slots, views, *sources)[:views_all]


def everyones_pairs(pairs, owners):
    if owners != 16:
        return lax.all_gather(pairs, "owner", axis=0, tiled=True)
    flat = pairs.reshape(1, -1)
    shift = lambda s: [(i, (i + 4 * s) % 16) for i in range(16)]
    flat = jnp.concatenate([flat] + [lax.ppermute(flat, "owner", shift(s)) for s in (1, 2, 3)])
    flat = jnp.concatenate([flat, lax.ppermute(flat, "owner", [(i, i ^ 2) for i in range(16)])])
    flat = jnp.concatenate([flat, lax.ppermute(flat, "owner", [(i, i ^ 1) for i in range(16)])])
    return flat.reshape(-1, 2)


def local(features, pairs):
    owners = lax.axis_size("owner")
    views_dev, length, width = features.shape
    flows, table = make_plan(owners)
    everyone = everyones_pairs(pairs, owners)
    features, everyone = lax.optimization_barrier((features, everyone))
    mine = jnp.asarray(table)[lax.axis_index("owner")]
    count, slots, views = pair_lists(everyone, mine, views_dev)
    buffers = [features]
    for source, perm in flows:
        buffers.append(lax.ppermute(buffers[source], "owner", perm))
    outgoing = confidences(count, slots, views, buffers, 10.0 / width, owners * views_dev)
    returned = lax.all_to_all(
        outgoing.reshape(owners, views_dev, length), "owner", split_axis=0, concat_axis=0, tiled=True
    )
    return jnp.max(returned, axis=0)


def solution(mesh):
    placed = (P(("groups", "owner"), None, None), P(("groups", "owner"), None))
    return jax.shard_map(
        local, mesh=mesh, in_specs=placed, out_specs=P(("groups", "owner"), None), check_vma=False
    )
```

```python
import functools
import math

import jax
import jax.numpy as jnp
import numpy as np
from jax import lax
from jax.experimental import pallas as pl
from jax.experimental.pallas import tpu as pltpu
from jax.sharding import PartitionSpec as P

LANES = 128
SUM_LOW, SUM_HIGH = 1e-28, 1e36


PIECES = 2
GROUP = 2


def small_slice_moves():
    at = lambda z, y, c: (z * 2 + y) * 2 + c
    yc = [(y, c) for y in range(2) for c in range(2)]
    step = lambda z, t: [(at(z, y, c), at(t, y, c)) for y, c in yc]
    return dict(
        near=step(1, 2) + step(0, 1),
        high=step(3, 2) + step(2, 3),
        side=[(at(z, y, c), at(z, 1 - y, c)) for z in range(4) for y, c in yc],
        far=step(0, 2),
        cross=[(at(3, 1 - y, c), at(2, y, c)) for y, c in yc],
        core=[(i, i ^ 1) for i in range(16)],
    )


SMALL_FLOWS = [
    (0, "near"),
    (0, "high"),
    (0, "side"),
    (0, "far"),
    (0, "cross"),
    (1, "core"),
    (2, "core"),
    (3, "core"),
    (4, "core"),
]
EARLY = [(0, 0), (0, 1), (3, 0), (3, 1), (8, 0), (8, 1), (2, 0), (2, 1), (7, 0), (7, 1), (1, 0), (1, 1), (6, 0), (6, 1)]
SMALL_PHASES = [
    EARLY + [(5, 0), (4, 0), (9, 0)],
    [(4, 1), (9, 1)] + EARLY + [(5, 0), (5, 1), (4, 0), (9, 0)],
]


def cyclic_distances(owners):
    step = max(1, math.isqrt(owners // 2))
    reach = set(range(step))
    top = step - 1
    while top < owners // 2:
        top += step
        reach.add(top)
    return sorted({d % owners for d in reach} - {0})


@functools.lru_cache(None)
def make_plan(owners):
    if owners == 16:
        moves = small_slice_moves()
        flows = [(source, moves[name]) for source, name in SMALL_FLOWS]
        phases = SMALL_PHASES
    else:
        flows = [(0, [((i + d) % owners, i) for i in range(owners)]) for d in cyclic_distances(owners)]
        phases = [[(k, piece) for k in range(len(flows) + 1) for piece in range(PIECES)]]
    held = [[d] for d in range(owners)]
    for source, perm in flows:
        arrived = {t: held[s][source] for s, t in perm}
        for d in range(owners):
            held[d].append(arrived.get(d, -1))
    first = [{} for _ in range(owners)]
    for d in range(owners):
        for k, o in enumerate(held[d]):
            if o >= 0:
                first[d].setdefault(o, k)
    table = np.zeros((owners, owners, owners), np.int32)
    load = np.zeros(owners)
    choices = []
    for a in range(owners):
        for b in range(a, owners):
            at = [d for d in range(owners) if a in first[d] and b in first[d]]
            assert at
            choices.append((len(at), a, b, at))
    for _, a, b, at in sorted(choices):
        d = min(at, key=lambda d: (load[d], d))
        load[d] += 1 if a == b else 2
        table[d, a, b] = first[d][a] * 64 + first[d][b] + 1
        table[d, b, a] = first[d][b] * 64 + first[d][a] + 1
    order = np.full((len(phases), (len(flows) + 1) * PIECES), -1, np.int32)
    for phase, pieces in enumerate(phases):
        for place, (k, piece) in enumerate(pieces):
            order[phase, k * PIECES + piece] = place
    return flows, phases, table, order


def pair_lists(pairs, mine, order, views_dev):
    count, owners = pairs.shape[0], mine.shape[0]
    left, right = pairs[:, 0], pairs[:, 1]
    is_left = (left // views_dev)[:, None] == jnp.arange(owners)[None, :]
    is_right = (right // views_dev)[:, None] == jnp.arange(owners)[None, :]
    row = jnp.dot(is_left.astype(jnp.float32), mine.astype(jnp.float32), precision=lax.Precision.HIGHEST)
    found = jnp.sum(jnp.where(is_right, row, 0.0), axis=1).astype(jnp.int32)
    buffers = jnp.maximum(found - 1, 0)
    deep = views_dev // PIECES
    left_piece = (buffers // 64) * PIECES + (left % views_dev) // deep
    right_piece = (buffers % 64) * PIECES + (right % views_dev) // deep
    place = jnp.arange(count)
    free = found > 0
    lists = []
    for phase in range(order.shape[0]):
        where = jnp.asarray(order[phase])[None, :]
        names = jnp.arange(order.shape[1])[None, :]
        left_at = jnp.sum(jnp.where(left_piece[:, None] == names, where, 0), axis=1)
        right_at = jnp.sum(jnp.where(right_piece[:, None] == names, where, 0), axis=1)
        chosen = free & (left_at >= 0) & (right_at >= 0)
        free = free & jnp.logical_not(chosen)
        key = jnp.maximum(left_at, right_at) * count + place
        rank = jnp.sum((key[None, :] < key[:, None]) & chosen[None, :], axis=1)
        picker = (rank[None, :] == place[:, None]) & chosen[None, :]
        slots = (left_at * deep + left % deep) * 1024 + right_at * deep + right % deep
        slots = jnp.sum(jnp.where(picker, slots[None, :], 0), axis=1)
        views = jnp.sum(jnp.where(picker, (left * 1024 + right)[None, :], 0), axis=1)
        lists.append((jnp.sum(chosen.astype(jnp.int32)).reshape(1), slots, views))
    return lists


def kernel(pieces, score_scale, count_ref, slots_ref, views_ref, before_ref, *refs):
    sources = refs[:-7]
    out_ref, arena, held, by_row, by_col, bounds, sems = refs[-7:]
    length = arena.shape[1]
    deep = arena.shape[0] // len(pieces)
    total = count_ref[0]
    limit = slots_ref.shape[0] - 1

    def slots_of(p):
        packed = slots_ref[jnp.minimum(p, limit)]
        return lax.shift_right_logical(packed, 10), lax.bitwise_and(packed, 1023)

    def wait_until(needed, waited):
        def wait(k, carry):
            part = arena.at[pl.ds(0, deep)]
            pltpu.make_async_copy(part, part, sems.at[k]).wait()
            return carry

        lax.fori_loop(waited, needed, wait, 0)
        return jnp.maximum(waited, needed)

    def product(p):
        left, right = slots_of(p)
        return lax.dot_general(
            arena[left], arena[right], (((1,), (1,)), ((), ())), preferred_element_type=jnp.float32
        )

    def record(p, row_conf, col_conf):
        packed = views_ref[jnp.minimum(p, limit)]
        real = p < total
        left = jnp.where(real, lax.shift_right_logical(packed, 10), -1)
        right = jnp.where(real, lax.bitwise_and(packed, 1023), by_row.shape[1])
        for tile in range(by_row.shape[1] // LANES):
            lane = lax.broadcasted_iota(jnp.int32, (length, LANES), 1) + tile * LANES
            at = (slice(None), slice(tile * LANES, (tile + 1) * LANES))
            by_row[at] = jnp.maximum(by_row[at], jnp.where(lane == left, row_conf, 0.0))
        by_col[pl.ds(right, 1), :] = jnp.maximum(by_col[pl.ds(right, 1), :], col_conf)

    def plain(p, scores):
        weight = jnp.exp2(scores[...] * (score_scale / math.log(2.0)))
        row_sum = jnp.sum(weight, axis=1, keepdims=True)
        col_sum = jnp.sum(weight, axis=0, keepdims=True)
        least = jnp.minimum(jnp.min(row_sum, axis=0, keepdims=True), jnp.min(col_sum, axis=1, keepdims=True))
        most = jnp.maximum(jnp.max(row_sum, axis=0, keepdims=True), jnp.max(col_sum, axis=1, keepdims=True))
        bounds[0] = jnp.minimum(bounds[0], jnp.where(p < total, least, 1.0))
        bounds[1] = jnp.maximum(bounds[1], jnp.where(p < total, most, 1.0))
        row_inv, col_inv = lax.rsqrt(row_sum), lax.rsqrt(col_sum)
        row_top = jnp.max(weight * col_inv, axis=1, keepdims=True) * row_inv
        col_top = jnp.max(weight * row_inv, axis=0, keepdims=True) * col_inv
        record(p, row_top * row_top, col_top * col_top)

    def shifted(p, carry):
        held[0] = product(p) * score_scale
        value = held[0]
        row_peak = jnp.max(value, axis=1, keepdims=True)
        row_total = row_peak + jnp.log(jnp.sum(jnp.exp(value - row_peak), axis=1, keepdims=True))
        col_peak = jnp.max(value, axis=0, keepdims=True)
        col_total = col_peak + jnp.log(jnp.sum(jnp.exp(value - col_peak), axis=0, keepdims=True))
        value = (value - row_total) + (value - col_total)
        record(p, jnp.exp(jnp.max(value, axis=1, keepdims=True)), jnp.exp(jnp.max(value, axis=0, keepdims=True)))
        return carry

    def clear():
        by_row[...] = jnp.zeros_like(by_row)
        by_col[...] = jnp.zeros_like(by_col)

    for place, (source, first) in enumerate(pieces):
        pltpu.make_async_copy(
            sources[source].at[pl.ds(first, deep)], arena.at[pl.ds(place * deep, deep)], sems.at[place]
        ).start()
    clear()
    bounds[...] = jnp.ones_like(bounds)

    def load(first, at, waited):
        needed = 1
        for g in range(GROUP):
            left, right = slots_of(first + g)
            needed = jnp.maximum(needed, lax.div(jnp.maximum(left, right), deep) + 1)
        waited = wait_until(needed, waited)
        for g in range(GROUP):
            held[at * GROUP + g] = product(first + g)
        return waited

    def rounds(k, waited):
        first = 2 * GROUP * k
        for at in range(2):
            waited = load(first + (at + 1) * GROUP, 1 - at, waited)
            for g in range(GROUP):
                plain(first + at * GROUP + g, held.at[at * GROUP + g])
        return waited

    waited = load(0, 0, jnp.int32(0))
    waited = lax.fori_loop(0, lax.div(total + 2 * GROUP - 1, 2 * GROUP), rounds, waited)
    wait_until(jnp.int32(len(pieces)), waited)
    fine = (jnp.min(bounds[0]) >= SUM_LOW) & (jnp.max(bounds[1]) <= SUM_HIGH)

    @pl.when(jnp.logical_not(fine))
    def again():
        clear()
        lax.fori_loop(0, total, shifted, 0)

    result = jnp.maximum(by_row[...].T, by_col[: by_row.shape[1], :]).astype(jnp.bfloat16)
    out_ref[...] = jnp.maximum(result, before_ref[...])


def confidences(lists, before, sources, pieces, deep, score_scale, work):
    count, slots, views = lists
    padded, length = before.shape
    width = sources[0].shape[2]
    smem = pl.BlockSpec(memory_space=pltpu.SMEM)
    vmem = pl.BlockSpec(memory_space=pltpu.VMEM)
    return pl.pallas_call(
        functools.partial(kernel, pieces, score_scale),
        out_shape=jax.ShapeDtypeStruct(before.shape, jnp.bfloat16),
        in_specs=[smem] * 3 + [vmem] + [pl.BlockSpec(memory_space=pl.ANY)] * len(sources),
        out_specs=vmem,
        scratch_shapes=[
            pltpu.VMEM((len(pieces) * deep, length, width), jnp.bfloat16),
            pltpu.VMEM((2 * GROUP, length, length), jnp.float32),
            pltpu.VMEM((length, padded), jnp.float32),
            pltpu.VMEM((padded + 8, length), jnp.float32),
            pltpu.VMEM((2, 1, 1), jnp.float32),
            pltpu.SemaphoreType.DMA((len(pieces),)),
        ],
        compiler_params=pltpu.CompilerParams(vmem_limit_bytes=56 * 1024 * 1024),
        cost_estimate=pl.CostEstimate(flops=work, bytes_accessed=0, transcendentals=0),
    )(count, slots, views, before, *sources)


def gather_small_slice(features, pairs, moves):
    send = lambda x, name: lax.ppermute(x, "owner", moves[name])
    tie = lax.optimization_barrier
    half = features.shape[0] // PIECES
    halves = [features[:half], features[half:]]
    flat = pairs.reshape(1, -1)
    shift = lambda s: [(i, (i + 4 * s) % 16) for i in range(16)]
    flat = jnp.concatenate([flat] + [lax.ppermute(flat, "owner", shift(s)) for s in (1, 2, 3)])
    halves, flat = tie((halves, flat))
    near, high = [send(x, "near") for x in halves], [send(x, "high") for x in halves]
    flat = jnp.concatenate([flat, send(flat, "side")])
    own, flat = tie((features, flat))
    side = send(own, "side")
    flat = jnp.concatenate([flat, send(flat, "core")])
    far, cross = [], []
    for k in range(PIECES):
        mine, near[k], high[k] = tie((halves[k], near[k], high[k]))
        far.append(send(mine, "far"))
        cross.append(send(mine, "cross"))
    swapped = lambda parts: [send(x, "core") for x in parts]
    buffers = [[features], near, high, [side], far, cross, swapped(near), swapped(high), swapped([side]), swapped(far[:1]) + far[1:]]
    return flat.reshape(-1, 2), buffers


def local(features, pairs):
    owners = lax.axis_size("owner")
    views_dev, length, width = features.shape
    flows, phases, table, order = make_plan(owners)
    if owners == 16:
        everyone, buffers = gather_small_slice(features, pairs, small_slice_moves())
    else:
        everyone = lax.all_gather(pairs, "owner", axis=0, tiled=True)
        buffers = [[features]] + [[lax.ppermute(features, "owner", perm)] for _, perm in flows]
    mine = jnp.asarray(table)[lax.axis_index("owner")]
    lists = pair_lists(everyone, mine, order, views_dev)
    deep = views_dev // PIECES
    padded = (owners * views_dev + LANES - 1) // LANES * LANES
    best = jnp.zeros((padded, length), jnp.bfloat16)
    for phase, (listed, wanted) in enumerate(zip(lists, phases)):
        sources, pieces = [], []
        if phase > 0:
            far, best = lax.optimization_barrier((buffers[4][1], best))
            buffers[9][1] = lax.ppermute(far, "owner", small_slice_moves()["core"])
        for k, piece in wanted:
            part = buffers[k][piece] if len(buffers[k]) > 1 else buffers[k][0]
            if not any(part is x for x in sources):
                sources.append(part)
            at = [part is x for x in sources].index(True)
            pieces.append((at, 0 if len(buffers[k]) > 1 else piece * deep))
        best = confidences(listed, best, sources, tuple(pieces), deep, 10.0 / width, 10**8)
    outgoing = best[: owners * views_dev].reshape(owners, views_dev, length)
    returned = lax.all_to_all(outgoing, "owner", split_axis=0, concat_axis=0, tiled=True)
    return jnp.max(returned, axis=0)


def solution(mesh):
    placed = (P(("groups", "owner"), None, None), P(("groups", "owner"), None))
    return jax.shard_map(
        local, mesh=mesh, in_specs=placed, out_specs=P(("groups", "owner"), None), check_vma=False
    )
```

```python
import functools
import math

import jax
import jax.numpy as jnp
import numpy as np
from jax import lax
from jax.experimental import pallas as pl
from jax.experimental.pallas import tpu as pltpu
from jax.sharding import PartitionSpec as P

LANES = 128
SUM_LOW, SUM_HIGH = 1e-28, 1e36


PIECES = 2
GROUP = 2


def small_slice_moves():
    at = lambda z, y, c: (z * 2 + y) * 2 + c
    yc = [(y, c) for y in range(2) for c in range(2)]
    step = lambda z, t: [(at(z, y, c), at(t, y, c)) for y, c in yc]
    return dict(
        near=step(1, 2) + step(0, 1),
        high=step(3, 2) + step(2, 3),
        side=[(at(z, y, c), at(z, 1 - y, c)) for z in range(4) for y, c in yc],
        far=step(0, 2),
        cross=[(at(3, 1 - y, c), at(2, y, c)) for y, c in yc],
        core=[(i, i ^ 1) for i in range(16)],
    )


SMALL_FLOWS = [
    (0, "near"),
    (0, "high"),
    (0, "side"),
    (0, "far"),
    (0, "cross"),
    (1, "core"),
    (2, "core"),
    (3, "core"),
    (4, "core"),
]
EARLY = [(0, 0), (0, 1), (3, 0), (3, 1), (8, 0), (8, 1), (2, 0), (2, 1), (7, 0), (7, 1), (1, 0), (1, 1), (6, 0), (6, 1)]
SMALL_PHASES = [
    EARLY,
    [(4, 0), (9, 0)] + EARLY + [(5, 0)],
    [(4, 1), (9, 1)] + EARLY + [(5, 0), (5, 1), (4, 0), (9, 0)],
]


def cyclic_distances(owners):
    step = max(1, math.isqrt(owners // 2))
    reach = set(range(step))
    top = step - 1
    while top < owners // 2:
        top += step
        reach.add(top)
    return sorted({d % owners for d in reach} - {0})


@functools.lru_cache(None)
def make_plan(owners):
    if owners == 16:
        moves = small_slice_moves()
        flows = [(source, moves[name]) for source, name in SMALL_FLOWS]
        phases = SMALL_PHASES
    else:
        flows = [(0, [((i + d) % owners, i) for i in range(owners)]) for d in cyclic_distances(owners)]
        phases = [[(k, piece) for k in range(len(flows) + 1) for piece in range(PIECES)]]
    held = [[d] for d in range(owners)]
    for source, perm in flows:
        arrived = {t: held[s][source] for s, t in perm}
        for d in range(owners):
            held[d].append(arrived.get(d, -1))
    first = [{} for _ in range(owners)]
    for d in range(owners):
        for k, o in enumerate(held[d]):
            if o >= 0:
                first[d].setdefault(o, k)
    table = np.zeros((owners, owners, owners), np.int32)
    load = np.zeros(owners)
    choices = []
    for a in range(owners):
        for b in range(a, owners):
            at = [d for d in range(owners) if a in first[d] and b in first[d]]
            assert at
            choices.append((len(at), a, b, at))
    for _, a, b, at in sorted(choices):
        d = min(at, key=lambda d: (load[d], d))
        load[d] += 1 if a == b else 2
        table[d, a, b] = first[d][a] * 64 + first[d][b] + 1
        table[d, b, a] = first[d][b] * 64 + first[d][a] + 1
    order = np.full((len(phases), (len(flows) + 1) * PIECES), -1, np.int32)
    for phase, pieces in enumerate(phases):
        for place, (k, piece) in enumerate(pieces):
            order[phase, k * PIECES + piece] = place
    return flows, phases, table, order


def pair_lists(pairs, mine, order, views_dev):
    count, owners = pairs.shape[0], mine.shape[0]
    left, right = pairs[:, 0], pairs[:, 1]
    is_left = (left // views_dev)[:, None] == jnp.arange(owners)[None, :]
    is_right = (right // views_dev)[:, None] == jnp.arange(owners)[None, :]
    row = jnp.dot(is_left.astype(jnp.float32), mine.astype(jnp.float32), precision=lax.Precision.HIGHEST)
    found = jnp.sum(jnp.where(is_right, row, 0.0), axis=1).astype(jnp.int32)
    buffers = jnp.maximum(found - 1, 0)
    deep = views_dev // PIECES
    left_piece = (buffers // 64) * PIECES + (left % views_dev) // deep
    right_piece = (buffers % 64) * PIECES + (right % views_dev) // deep
    place = jnp.arange(count)
    free = found > 0
    lists = []
    for phase in range(order.shape[0]):
        where = jnp.asarray(order[phase])[None, :]
        names = jnp.arange(order.shape[1])[None, :]
        left_at = jnp.sum(jnp.where(left_piece[:, None] == names, where, 0), axis=1)
        right_at = jnp.sum(jnp.where(right_piece[:, None] == names, where, 0), axis=1)
        chosen = free & (left_at >= 0) & (right_at >= 0)
        free = free & jnp.logical_not(chosen)
        key = jnp.maximum(left_at, right_at) * count + place
        rank = jnp.sum((key[None, :] < key[:, None]) & chosen[None, :], axis=1)
        picker = (rank[None, :] == place[:, None]) & chosen[None, :]
        slots = (left_at * deep + left % deep) * 1024 + right_at * deep + right % deep
        slots = jnp.sum(jnp.where(picker, slots[None, :], 0), axis=1)
        views = jnp.sum(jnp.where(picker, (left * 1024 + right)[None, :], 0), axis=1)
        used = ((left_at[:, None] == names) | (right_at[:, None] == names)) & chosen[:, None]
        counts = jnp.concatenate([jnp.sum(chosen.astype(jnp.int32)).reshape(1), jnp.any(used, axis=0).astype(jnp.int32)])
        lists.append((counts, slots, views))
    return lists


def kernel(pieces, score_scale, count_ref, slots_ref, views_ref, before_ref, *refs):
    sources = refs[:-7]
    out_ref, arena, held, by_row, by_col, bounds, sems = refs[-7:]
    length = arena.shape[1]
    deep = arena.shape[0] // len(pieces)
    total = count_ref[0]
    limit = slots_ref.shape[0] - 1

    def slots_of(p):
        packed = slots_ref[jnp.minimum(p, limit)]
        return lax.shift_right_logical(packed, 10), lax.bitwise_and(packed, 1023)

    def wait_until(needed, waited):
        def wait(k, carry):
            part = arena.at[pl.ds(0, deep)]
            pl.when(count_ref[k + 1] > 0)(lambda: pltpu.make_async_copy(part, part, sems.at[k]).wait())
            return carry

        lax.fori_loop(waited, needed, wait, 0)
        return jnp.maximum(waited, needed)

    def product(p):
        left, right = slots_of(p)
        return lax.dot_general(
            arena[left], arena[right], (((1,), (1,)), ((), ())), preferred_element_type=jnp.float32
        )

    def record(p, row_conf, col_conf):
        packed = views_ref[jnp.minimum(p, limit)]
        real = p < total
        left = jnp.where(real, lax.shift_right_logical(packed, 10), -1)
        right = jnp.where(real, lax.bitwise_and(packed, 1023), by_row.shape[1])
        for tile in range(by_row.shape[1] // LANES):
            lane = lax.broadcasted_iota(jnp.int32, (length, LANES), 1) + tile * LANES
            at = (slice(None), slice(tile * LANES, (tile + 1) * LANES))
            by_row[at] = jnp.maximum(by_row[at], jnp.where(lane == left, row_conf, 0.0))
        by_col[pl.ds(right, 1), :] = jnp.maximum(by_col[pl.ds(right, 1), :], col_conf)

    def plain(p, scores):
        weight = jnp.exp2(scores[...] * (score_scale / math.log(2.0)))
        row_sum = jnp.sum(weight, axis=1, keepdims=True)
        col_sum = jnp.sum(weight, axis=0, keepdims=True)
        least = jnp.minimum(jnp.min(row_sum, axis=0, keepdims=True), jnp.min(col_sum, axis=1, keepdims=True))
        most = jnp.maximum(jnp.max(row_sum, axis=0, keepdims=True), jnp.max(col_sum, axis=1, keepdims=True))
        bounds[0] = jnp.minimum(bounds[0], jnp.where(p < total, least, 1.0))
        bounds[1] = jnp.maximum(bounds[1], jnp.where(p < total, most, 1.0))
        row_inv, col_inv = lax.rsqrt(row_sum), lax.rsqrt(col_sum)
        row_top = jnp.max(weight * col_inv, axis=1, keepdims=True) * row_inv
        col_top = jnp.max(weight * row_inv, axis=0, keepdims=True) * col_inv
        record(p, row_top * row_top, col_top * col_top)

    def shifted(p, carry):
        held[0] = product(p) * score_scale
        value = held[0]
        row_peak = jnp.max(value, axis=1, keepdims=True)
        row_total = row_peak + jnp.log(jnp.sum(jnp.exp(value - row_peak), axis=1, keepdims=True))
        col_peak = jnp.max(value, axis=0, keepdims=True)
        col_total = col_peak + jnp.log(jnp.sum(jnp.exp(value - col_peak), axis=0, keepdims=True))
        value = (value - row_total) + (value - col_total)
        record(p, jnp.exp(jnp.max(value, axis=1, keepdims=True)), jnp.exp(jnp.max(value, axis=0, keepdims=True)))
        return carry

    def clear():
        by_row[...] = jnp.zeros_like(by_row)
        by_col[...] = jnp.zeros_like(by_col)

    for place, (source, first) in enumerate(pieces):
        piece = pltpu.make_async_copy(
            sources[source].at[pl.ds(first, deep)], arena.at[pl.ds(place * deep, deep)], sems.at[place]
        )
        pl.when(count_ref[place + 1] > 0)(piece.start)
    clear()
    bounds[...] = jnp.ones_like(bounds)

    def load(first, at, waited):
        needed = 1
        for g in range(GROUP):
            left, right = slots_of(first + g)
            needed = jnp.maximum(needed, lax.div(jnp.maximum(left, right), deep) + 1)
        waited = wait_until(needed, waited)
        for g in range(GROUP):
            held[at * GROUP + g] = product(first + g)
        return waited

    def rounds(k, waited):
        first = 2 * GROUP * k
        for at in range(2):
            waited = load(first + (at + 1) * GROUP, 1 - at, waited)
            for g in range(GROUP):
                plain(first + at * GROUP + g, held.at[at * GROUP + g])
        return waited

    @pl.when(total > 0)
    def all_pairs():
        waited = load(0, 0, jnp.int32(0))
        waited = lax.fori_loop(0, lax.div(total + 2 * GROUP - 1, 2 * GROUP), rounds, waited)
        wait_until(jnp.int32(len(pieces)), waited)

    fine = (jnp.min(bounds[0]) >= SUM_LOW) & (jnp.max(bounds[1]) <= SUM_HIGH)

    @pl.when(jnp.logical_not(fine))
    def again():
        clear()
        lax.fori_loop(0, total, shifted, 0)

    result = jnp.maximum(by_row[...].T, by_col[: by_row.shape[1], :]).astype(jnp.bfloat16)
    out_ref[...] = jnp.maximum(result, before_ref[...])


def confidences(lists, before, sources, pieces, deep, score_scale, work):
    count, slots, views = lists
    padded, length = before.shape
    width = sources[0].shape[2]
    smem = pl.BlockSpec(memory_space=pltpu.SMEM)
    vmem = pl.BlockSpec(memory_space=pltpu.VMEM)
    return pl.pallas_call(
        functools.partial(kernel, pieces, score_scale),
        out_shape=jax.ShapeDtypeStruct(before.shape, jnp.bfloat16),
        in_specs=[smem] * 3 + [vmem] + [pl.BlockSpec(memory_space=pl.ANY)] * len(sources),
        out_specs=vmem,
        scratch_shapes=[
            pltpu.VMEM((len(pieces) * deep, length, width), jnp.bfloat16),
            pltpu.VMEM((2 * GROUP, length, length), jnp.float32),
            pltpu.VMEM((length, padded), jnp.float32),
            pltpu.VMEM((padded + 8, length), jnp.float32),
            pltpu.VMEM((2, 1, 1), jnp.float32),
            pltpu.SemaphoreType.DMA((len(pieces),)),
        ],
        compiler_params=pltpu.CompilerParams(vmem_limit_bytes=56 * 1024 * 1024),
        cost_estimate=pl.CostEstimate(flops=work, bytes_accessed=0, transcendentals=0),
    )(count, slots, views, before, *sources)


def gather_small_slice(features, pairs, moves):
    send = lambda x, name: lax.ppermute(x, "owner", moves[name])
    tie = lax.optimization_barrier
    half = features.shape[0] // PIECES
    halves = [features[:half], features[half:]]
    near, high = [send(halves[0], "near")], [send(halves[0], "high")]
    flat = pairs.reshape(1, -1)
    flat = jnp.concatenate([flat, send(flat, "side")])
    own, flat = tie((features, flat))
    side = send(own, "side")
    flat = jnp.concatenate([flat, send(flat, "core")])
    mine, flat = tie((halves[1], flat))
    shift = lambda s: [(i, (i + 4 * s) % 16) for i in range(16)]
    flat = jnp.concatenate([flat] + [lax.ppermute(flat, "owner", shift(s)) for s in (1, 2, 3)])
    flat, near[0], high[0] = tie((flat, near[0], high[0]))
    near.append(send(mine, "near"))
    high.append(send(mine, "high"))
    far, cross = [], []
    for k in range(PIECES):
        mine, near[k], high[k] = tie((halves[k], near[k], high[k]))
        far.append(send(mine, "far"))
        cross.append(send(mine, "cross"))
    swapped = lambda parts: [send(x, "core") for x in parts]
    buffers = [[features], near, high, [side], far, cross, swapped(near), swapped(high), swapped([side]), list(far)]
    return flat.reshape(-1, 2), buffers


def local(features, pairs):
    owners = lax.axis_size("owner")
    views_dev, length, width = features.shape
    flows, phases, table, order = make_plan(owners)
    if owners == 16:
        everyone, buffers = gather_small_slice(features, pairs, small_slice_moves())
    else:
        everyone = lax.all_gather(pairs, "owner", axis=0, tiled=True)
        buffers = [[features]] + [[lax.ppermute(features, "owner", perm)] for _, perm in flows]
    mine = jnp.asarray(table)[lax.axis_index("owner")]
    lists = pair_lists(everyone, mine, order, views_dev)
    deep = views_dev // PIECES
    padded = (owners * views_dev + LANES - 1) // LANES * LANES
    best = jnp.zeros((padded, length), jnp.bfloat16)
    for phase, (listed, wanted) in enumerate(zip(lists, phases)):
        sources, pieces = [], []
        if phase > 0:
            far, best = lax.optimization_barrier((buffers[4][phase - 1], best))
            buffers[9][phase - 1] = lax.ppermute(far, "owner", small_slice_moves()["core"])
        for k, piece in wanted:
            part = buffers[k][piece] if len(buffers[k]) > 1 else buffers[k][0]
            if not any(part is x for x in sources):
                sources.append(part)
            at = [part is x for x in sources].index(True)
            pieces.append((at, 0 if len(buffers[k]) > 1 else piece * deep))
        best = confidences(listed, best, sources, tuple(pieces), deep, 10.0 / width, 10**8)
    outgoing = best[: owners * views_dev].reshape(owners, views_dev, length)
    returned = lax.all_to_all(outgoing, "owner", split_axis=0, concat_axis=0, tiled=True)
    return jnp.max(returned, axis=0)


def solution(mesh):
    placed = (P(("groups", "owner"), None, None), P(("groups", "owner"), None))
    return jax.shard_map(
        local, mesh=mesh, in_specs=placed, out_specs=P(("groups", "owner"), None), check_vma=False
    )
```

```python
import functools
import math

import jax
import jax.numpy as jnp
import numpy as np
from jax import lax
from jax.experimental import pallas as pl
from jax.experimental.pallas import tpu as pltpu
from jax.sharding import PartitionSpec as P

LANES = 128
SUM_LOW, SUM_HIGH = 1e-28, 1e36


PIECES = 2
GROUP = 2


def small_slice_moves():
    at = lambda z, y, c: (z * 2 + y) * 2 + c
    yc = [(y, c) for y in range(2) for c in range(2)]
    step = lambda z, t: [(at(z, y, c), at(t, y, c)) for y, c in yc]
    return dict(
        near=step(1, 2) + step(0, 1),
        high=step(3, 2) + step(2, 3),
        side=[(at(z, y, c), at(z, 1 - y, c)) for z in range(4) for y, c in yc],
        far=step(0, 2),
        cross=[(at(3, 1 - y, c), at(2, y, c)) for y, c in yc],
        core=[(i, i ^ 1) for i in range(16)],
    )


SMALL_FLOWS = [
    (0, "near"),
    (0, "high"),
    (0, "side"),
    (0, "far"),
    (0, "cross"),
    (1, "core"),
    (2, "core"),
    (3, "core"),
    (4, "core"),
]
EARLY = [(0, 0), (0, 1), (3, 0), (3, 1), (8, 0), (8, 1), (2, 0), (2, 1), (7, 0), (7, 1), (1, 0), (1, 1), (6, 0), (6, 1)]
SMALL_PHASES = [
    EARLY,
    [(4, 0), (9, 0), (4, 1), (9, 1)] + EARLY + [(5, 0), (5, 1)],
]


def cyclic_distances(owners):
    step = max(1, math.isqrt(owners // 2))
    reach = set(range(step))
    top = step - 1
    while top < owners // 2:
        top += step
        reach.add(top)
    return sorted({d % owners for d in reach} - {0})


@functools.lru_cache(None)
def make_plan(owners):
    if owners == 16:
        moves = small_slice_moves()
        flows = [(source, moves[name]) for source, name in SMALL_FLOWS]
        phases = SMALL_PHASES
    else:
        flows = [(0, [((i + d) % owners, i) for i in range(owners)]) for d in cyclic_distances(owners)]
        phases = [[(k, piece) for k in range(len(flows) + 1) for piece in range(PIECES)]]
    held = [[d] for d in range(owners)]
    for source, perm in flows:
        arrived = {t: held[s][source] for s, t in perm}
        for d in range(owners):
            held[d].append(arrived.get(d, -1))
    first = [{} for _ in range(owners)]
    for d in range(owners):
        for k, o in enumerate(held[d]):
            if o >= 0:
                first[d].setdefault(o, k)
    table = np.zeros((owners, owners, owners), np.int32)
    load = np.zeros(owners)
    choices = []
    for a in range(owners):
        for b in range(a, owners):
            at = [d for d in range(owners) if a in first[d] and b in first[d]]
            assert at
            choices.append((len(at), a, b, at))
    for _, a, b, at in sorted(choices):
        d = min(at, key=lambda d: (load[d], d))
        load[d] += 1 if a == b else 2
        table[d, a, b] = first[d][a] * 64 + first[d][b] + 1
        table[d, b, a] = first[d][b] * 64 + first[d][a] + 1
    order = np.full((len(phases), (len(flows) + 1) * PIECES), -1, np.int32)
    for phase, pieces in enumerate(phases):
        for place, (k, piece) in enumerate(pieces):
            order[phase, k * PIECES + piece] = place
    return flows, phases, table, order


def pair_lists(pairs, mine, order, views_dev):
    count, owners = pairs.shape[0], mine.shape[0]
    left, right = pairs[:, 0], pairs[:, 1]
    is_left = (left // views_dev)[:, None] == jnp.arange(owners)[None, :]
    is_right = (right // views_dev)[:, None] == jnp.arange(owners)[None, :]
    row = jnp.dot(is_left.astype(jnp.float32), mine.astype(jnp.float32), precision=lax.Precision.HIGHEST)
    found = jnp.sum(jnp.where(is_right, row, 0.0), axis=1).astype(jnp.int32)
    buffers = jnp.maximum(found - 1, 0)
    deep = views_dev // PIECES
    left_piece = (buffers // 64) * PIECES + (left % views_dev) // deep
    right_piece = (buffers % 64) * PIECES + (right % views_dev) // deep
    place = jnp.arange(count)
    free = found > 0
    lists = []
    for phase in range(order.shape[0]):
        where = jnp.asarray(order[phase])[None, :]
        names = jnp.arange(order.shape[1])[None, :]
        left_at = jnp.sum(jnp.where(left_piece[:, None] == names, where, 0), axis=1)
        right_at = jnp.sum(jnp.where(right_piece[:, None] == names, where, 0), axis=1)
        chosen = free & (left_at >= 0) & (right_at >= 0)
        free = free & jnp.logical_not(chosen)
        key = jnp.maximum(left_at, right_at) * count + place
        rank = jnp.sum((key[None, :] < key[:, None]) & chosen[None, :], axis=1)
        picker = (rank[None, :] == place[:, None]) & chosen[None, :]
        slots = (left_at * deep + left % deep) * 1024 + right_at * deep + right % deep
        slots = jnp.sum(jnp.where(picker, slots[None, :], 0), axis=1)
        views = jnp.sum(jnp.where(picker, (left * 1024 + right)[None, :], 0), axis=1)
        used = ((left_at[:, None] == names) | (right_at[:, None] == names)) & chosen[:, None]
        counts = jnp.concatenate([jnp.sum(chosen.astype(jnp.int32)).reshape(1), jnp.any(used, axis=0).astype(jnp.int32)])
        lists.append((counts, slots, views))
    return lists


def kernel(pieces, score_scale, count_ref, slots_ref, views_ref, before_ref, *refs):
    sources = refs[:-7]
    out_ref, arena, held, by_row, by_col, bounds, sems = refs[-7:]
    length = arena.shape[1]
    deep = arena.shape[0] // len(pieces)
    total = count_ref[0]
    limit = slots_ref.shape[0] - 1

    def slots_of(p):
        packed = slots_ref[jnp.minimum(p, limit)]
        return lax.shift_right_logical(packed, 10), lax.bitwise_and(packed, 1023)

    def wait_until(needed, waited):
        def wait(k, carry):
            part = arena.at[pl.ds(0, deep)]
            pl.when(count_ref[k + 1] > 0)(lambda: pltpu.make_async_copy(part, part, sems.at[k]).wait())
            return carry

        lax.fori_loop(waited, needed, wait, 0)
        return jnp.maximum(waited, needed)

    def product(p):
        left, right = slots_of(p)
        return lax.dot_general(
            arena[left], arena[right], (((1,), (1,)), ((), ())), preferred_element_type=jnp.float32
        )

    def record(p, row_conf, col_conf):
        packed = views_ref[jnp.minimum(p, limit)]
        real = p < total
        left = jnp.where(real, lax.shift_right_logical(packed, 10), -1)
        right = jnp.where(real, lax.bitwise_and(packed, 1023), by_row.shape[1])
        for tile in range(by_row.shape[1] // LANES):
            lane = lax.broadcasted_iota(jnp.int32, (length, LANES), 1) + tile * LANES
            at = (slice(None), slice(tile * LANES, (tile + 1) * LANES))
            by_row[at] = jnp.maximum(by_row[at], jnp.where(lane == left, row_conf, 0.0))
        by_col[pl.ds(right, 1), :] = jnp.maximum(by_col[pl.ds(right, 1), :], col_conf)

    def plain(p, scores):
        weight = jnp.exp2(scores[...] * (score_scale / math.log(2.0)))
        row_sum = jnp.sum(weight, axis=1, keepdims=True)
        col_sum = jnp.sum(weight, axis=0, keepdims=True)
        least = jnp.minimum(jnp.min(row_sum, axis=0, keepdims=True), jnp.min(col_sum, axis=1, keepdims=True))
        most = jnp.maximum(jnp.max(row_sum, axis=0, keepdims=True), jnp.max(col_sum, axis=1, keepdims=True))
        bounds[0] = jnp.minimum(bounds[0], jnp.where(p < total, least, 1.0))
        bounds[1] = jnp.maximum(bounds[1], jnp.where(p < total, most, 1.0))
        row_inv, col_inv = lax.rsqrt(row_sum), lax.rsqrt(col_sum)
        row_top = jnp.max(weight * col_inv, axis=1, keepdims=True) * row_inv
        col_top = jnp.max(weight * row_inv, axis=0, keepdims=True) * col_inv
        record(p, row_top * row_top, col_top * col_top)

    def shifted(p, carry):
        held[0] = product(p) * score_scale
        value = held[0]
        row_peak = jnp.max(value, axis=1, keepdims=True)
        row_total = row_peak + jnp.log(jnp.sum(jnp.exp(value - row_peak), axis=1, keepdims=True))
        col_peak = jnp.max(value, axis=0, keepdims=True)
        col_total = col_peak + jnp.log(jnp.sum(jnp.exp(value - col_peak), axis=0, keepdims=True))
        value = (value - row_total) + (value - col_total)
        record(p, jnp.exp(jnp.max(value, axis=1, keepdims=True)), jnp.exp(jnp.max(value, axis=0, keepdims=True)))
        return carry

    def clear():
        by_row[...] = jnp.zeros_like(by_row)
        by_col[...] = jnp.zeros_like(by_col)

    for place, (source, first) in enumerate(pieces):
        piece = pltpu.make_async_copy(
            sources[source].at[pl.ds(first, deep)], arena.at[pl.ds(place * deep, deep)], sems.at[place]
        )
        pl.when(count_ref[place + 1] > 0)(piece.start)
    clear()
    bounds[...] = jnp.ones_like(bounds)

    def load(first, at, waited):
        needed = 1
        for g in range(GROUP):
            left, right = slots_of(first + g)
            needed = jnp.maximum(needed, lax.div(jnp.maximum(left, right), deep) + 1)
        waited = wait_until(needed, waited)
        for g in range(GROUP):
            held[at * GROUP + g] = product(first + g)
        return waited

    def rounds(k, waited):
        first = 2 * GROUP * k
        for at in range(2):
            waited = load(first + (at + 1) * GROUP, 1 - at, waited)
            for g in range(GROUP):
                plain(first + at * GROUP + g, held.at[at * GROUP + g])
        return waited

    @pl.when(total > 0)
    def all_pairs():
        waited = load(0, 0, jnp.int32(0))
        waited = lax.fori_loop(0, lax.div(total + 2 * GROUP - 1, 2 * GROUP), rounds, waited)
        wait_until(jnp.int32(len(pieces)), waited)

    fine = (jnp.min(bounds[0]) >= SUM_LOW) & (jnp.max(bounds[1]) <= SUM_HIGH)

    @pl.when(jnp.logical_not(fine))
    def again():
        clear()
        lax.fori_loop(0, total, shifted, 0)

    result = jnp.maximum(by_row[...].T, by_col[: by_row.shape[1], :]).astype(jnp.bfloat16)
    out_ref[...] = jnp.maximum(result, before_ref[...])


def confidences(lists, before, sources, pieces, deep, score_scale, work):
    count, slots, views = lists
    padded, length = before.shape
    width = sources[0].shape[2]
    smem = pl.BlockSpec(memory_space=pltpu.SMEM)
    vmem = pl.BlockSpec(memory_space=pltpu.VMEM)
    return pl.pallas_call(
        functools.partial(kernel, pieces, score_scale),
        out_shape=jax.ShapeDtypeStruct(before.shape, jnp.bfloat16),
        in_specs=[smem] * 3 + [vmem] + [pl.BlockSpec(memory_space=pl.ANY)] * len(sources),
        out_specs=vmem,
        scratch_shapes=[
            pltpu.VMEM((len(pieces) * deep, length, width), jnp.bfloat16),
            pltpu.VMEM((2 * GROUP, length, length), jnp.float32),
            pltpu.VMEM((length, padded), jnp.float32),
            pltpu.VMEM((padded + 8, length), jnp.float32),
            pltpu.VMEM((2, 1, 1), jnp.float32),
            pltpu.SemaphoreType.DMA((len(pieces),)),
        ],
        compiler_params=pltpu.CompilerParams(vmem_limit_bytes=56 * 1024 * 1024),
        cost_estimate=pl.CostEstimate(flops=work, bytes_accessed=0, transcendentals=0),
    )(count, slots, views, before, *sources)


def gather_small_slice(features, pairs, moves):
    send = lambda x, name: lax.ppermute(x, "owner", moves[name])
    tie = lax.optimization_barrier
    near, high = send(features, "near"), send(features, "high")
    flat = pairs.reshape(1, -1)
    flat = jnp.concatenate([flat, send(flat, "side")])
    own, flat = tie((features, flat))
    side = send(own, "side")
    flat = jnp.concatenate([flat, send(flat, "core")])
    shift = lambda s: [(i, (i + 4 * s) % 16) for i in range(16)]
    flat = jnp.concatenate([flat] + [lax.ppermute(flat, "owner", shift(s)) for s in (1, 2, 3)])
    flat, near, high = tie((flat, near, high))
    own, near, high = tie((features, near, high))
    far, cross = send(own, "far"), send(own, "cross")
    swapped = [send(x, "core") for x in (near, high, side)]
    return flat.reshape(-1, 2), [features, near, high, side, far, cross, *swapped]


def local(features, pairs):
    owners = lax.axis_size("owner")
    views_dev, length, width = features.shape
    flows, phases, table, order = make_plan(owners)
    if owners == 16:
        everyone, buffers = gather_small_slice(features, pairs, small_slice_moves())
    else:
        everyone = lax.all_gather(pairs, "owner", axis=0, tiled=True)
        buffers = [features] + [lax.ppermute(features, "owner", perm) for _, perm in flows]
    mine = jnp.asarray(table)[lax.axis_index("owner")]
    lists = pair_lists(everyone, mine, order, views_dev)
    deep = views_dev // PIECES
    padded = (owners * views_dev + LANES - 1) // LANES * LANES
    best = jnp.zeros((padded, length), jnp.bfloat16)
    for phase, (listed, wanted) in enumerate(zip(lists, phases)):
        if phase > 0:
            far, best = lax.optimization_barrier((buffers[4], best))
            buffers.append(lax.ppermute(far, "owner", small_slice_moves()["core"]))
        names = sorted({k for k, _ in wanted})
        sources = [buffers[k] for k in names]
        pieces = tuple((names.index(k), piece * deep) for k, piece in wanted)
        best = confidences(listed, best, sources, pieces, deep, 10.0 / width, 10**8)
    outgoing = best[: owners * views_dev].reshape(owners, views_dev, length)
    returned = lax.all_to_all(outgoing, "owner", split_axis=0, concat_axis=0, tiled=True)
    return jnp.max(returned, axis=0)


def solution(mesh):
    placed = (P(("groups", "owner"), None, None), P(("groups", "owner"), None))
    return jax.shard_map(
        local, mesh=mesh, in_specs=placed, out_specs=P(("groups", "owner"), None), check_vma=False
    )
```

```python
import functools
import math

import jax
import jax.numpy as jnp
import numpy as np
from jax import lax
from jax.experimental import pallas as pl
from jax.experimental.pallas import tpu as pltpu
from jax.sharding import PartitionSpec as P

LANES = 128
SUM_LOW, SUM_HIGH = 1e-28, 1e36


PIECES = 2
GROUP = 2


def small_slice_moves():
    at = lambda z, y, c: (z * 2 + y) * 2 + c
    yc = [(y, c) for y in range(2) for c in range(2)]
    step = lambda z, t: [(at(z, y, c), at(t, y, c)) for y, c in yc]
    return dict(
        near=step(1, 2) + step(0, 1),
        high=step(3, 2) + step(2, 3),
        side=[(at(z, y, c), at(z, 1 - y, c)) for z in range(4) for y, c in yc],
        far=step(0, 2),
        cross=[(at(3, 1 - y, c), at(2, y, c)) for y, c in yc],
        core=[(i, i ^ 1) for i in range(16)],
    )


SMALL_FLOWS = [
    (0, "near"),
    (0, "high"),
    (0, "side"),
    (0, "far"),
    (0, "cross"),
    (1, "core"),
    (2, "core"),
    (3, "core"),
    (4, "core"),
    (0, "core"),
]
LATE_BUFFER = 9
EARLY = [(k, piece) for k in (0, 10, 3, 8, 2, 7, 1, 6) for piece in range(PIECES)]
SMALL_PHASES = [
    EARLY,
    [(4, 0)] + EARLY + [(5, 0)],
    [(4, 1)] + EARLY + [(5, 0), (5, 1), (4, 0), (9, 0), (9, 1)],
]


def cyclic_distances(owners):
    step = max(1, math.isqrt(owners // 2))
    reach = set(range(step))
    top = step - 1
    while top < owners // 2:
        top += step
        reach.add(top)
    return sorted({d % owners for d in reach} - {0})


@functools.lru_cache(None)
def make_plan(owners):
    if owners == 16:
        moves = small_slice_moves()
        flows = [(source, moves[name]) for source, name in SMALL_FLOWS]
        phases = SMALL_PHASES
    else:
        flows = [(0, [((i + d) % owners, i) for i in range(owners)]) for d in cyclic_distances(owners)]
        phases = [[(k, piece) for k in range(len(flows) + 1) for piece in range(PIECES)]]
    held = [[d] for d in range(owners)]
    for source, perm in flows:
        arrived = {t: held[s][source] for s, t in perm}
        for d in range(owners):
            held[d].append(arrived.get(d, -1))
    first = [{} for _ in range(owners)]
    for d in range(owners):
        for k, o in enumerate(held[d]):
            if o >= 0:
                first[d].setdefault(o, k)
    table = np.zeros((owners, owners, owners), np.int32)
    load = np.zeros(owners)
    choices = []
    for a in range(owners):
        for b in range(a, owners):
            at = [d for d in range(owners) if a in first[d] and b in first[d]]
            assert at
            choices.append((len(at), a, b, at))
    for _, a, b, at in sorted(choices):
        late = lambda d: owners == 16 and LATE_BUFFER in (first[d][a], first[d][b])
        d = min(at, key=lambda d: (late(d), load[d], d))
        load[d] += 1 if a == b else 2
        table[d, a, b] = first[d][a] * 64 + first[d][b] + 1
        table[d, b, a] = first[d][b] * 64 + first[d][a] + 1
    order = np.full((len(phases), (len(flows) + 1) * PIECES), -1, np.int32)
    for phase, pieces in enumerate(phases):
        for place, (k, piece) in enumerate(pieces):
            order[phase, k * PIECES + piece] = place
    return flows, phases, table, order


def pair_lists(pairs, mine, order, views_dev):
    count, owners = pairs.shape[0], mine.shape[0]
    left, right = pairs[:, 0], pairs[:, 1]
    is_left = (left // views_dev)[:, None] == jnp.arange(owners)[None, :]
    is_right = (right // views_dev)[:, None] == jnp.arange(owners)[None, :]
    row = jnp.dot(is_left.astype(jnp.float32), mine.astype(jnp.float32), precision=lax.Precision.HIGHEST)
    found = jnp.sum(jnp.where(is_right, row, 0.0), axis=1).astype(jnp.int32)
    buffers = jnp.maximum(found - 1, 0)
    deep = views_dev // PIECES
    left_piece = (buffers // 64) * PIECES + (left % views_dev) // deep
    right_piece = (buffers % 64) * PIECES + (right % views_dev) // deep
    place = jnp.arange(count)
    free = found > 0
    lists = []
    for phase in range(order.shape[0]):
        where = jnp.asarray(order[phase])[None, :]
        names = jnp.arange(order.shape[1])[None, :]
        left_at = jnp.sum(jnp.where(left_piece[:, None] == names, where, 0), axis=1)
        right_at = jnp.sum(jnp.where(right_piece[:, None] == names, where, 0), axis=1)
        chosen = free & (left_at >= 0) & (right_at >= 0)
        free = free & jnp.logical_not(chosen)
        key = jnp.maximum(left_at, right_at) * count + place
        rank = jnp.sum((key[None, :] < key[:, None]) & chosen[None, :], axis=1)
        picker = (rank[None, :] == place[:, None]) & chosen[None, :]
        slots = (left_at * deep + left % deep) * 1024 + right_at * deep + right % deep
        slots = jnp.sum(jnp.where(picker, slots[None, :], 0), axis=1)
        views = jnp.sum(jnp.where(picker, (left * 1024 + right)[None, :], 0), axis=1)
        used = ((left_at[:, None] == names) | (right_at[:, None] == names)) & chosen[:, None]
        counts = jnp.concatenate([jnp.sum(chosen.astype(jnp.int32)).reshape(1), jnp.any(used, axis=0).astype(jnp.int32)])
        lists.append((counts, slots, views))
    return lists


def kernel(pieces, score_scale, count_ref, slots_ref, views_ref, before_ref, *refs):
    sources = refs[:-7]
    out_ref, arena, held, by_row, by_col, bounds, sems = refs[-7:]
    length = arena.shape[1]
    deep = arena.shape[0] // len(pieces)
    total = count_ref[0]
    limit = slots_ref.shape[0] - 1

    def slots_of(p):
        packed = slots_ref[jnp.minimum(p, limit)]
        return lax.shift_right_logical(packed, 10), lax.bitwise_and(packed, 1023)

    def wait_until(needed, waited):
        def wait(k, carry):
            part = arena.at[pl.ds(0, deep)]
            pl.when(count_ref[k + 1] > 0)(lambda: pltpu.make_async_copy(part, part, sems.at[k]).wait())
            return carry

        lax.fori_loop(waited, needed, wait, 0)
        return jnp.maximum(waited, needed)

    def product(p):
        left, right = slots_of(p)
        return lax.dot_general(
            arena[left], arena[right], (((1,), (1,)), ((), ())), preferred_element_type=jnp.float32
        )

    def record(p, row_conf, col_conf):
        packed = views_ref[jnp.minimum(p, limit)]
        real = p < total
        left = jnp.where(real, lax.shift_right_logical(packed, 10), -1)
        right = jnp.where(real, lax.bitwise_and(packed, 1023), by_row.shape[1])
        for tile in range(by_row.shape[1] // LANES):
            lane = lax.broadcasted_iota(jnp.int32, (length, LANES), 1) + tile * LANES
            at = (slice(None), slice(tile * LANES, (tile + 1) * LANES))
            by_row[at] = jnp.maximum(by_row[at], jnp.where(lane == left, row_conf, 0.0))
        by_col[pl.ds(right, 1), :] = jnp.maximum(by_col[pl.ds(right, 1), :], col_conf)

    def plain(p, scores):
        weight = jnp.exp2(scores[...] * (score_scale / math.log(2.0)))
        row_sum = jnp.sum(weight, axis=1, keepdims=True)
        col_sum = jnp.sum(weight, axis=0, keepdims=True)
        least = jnp.minimum(jnp.min(row_sum, axis=0, keepdims=True), jnp.min(col_sum, axis=1, keepdims=True))
        most = jnp.maximum(jnp.max(row_sum, axis=0, keepdims=True), jnp.max(col_sum, axis=1, keepdims=True))
        bounds[0] = jnp.minimum(bounds[0], jnp.where(p < total, least, 1.0))
        bounds[1] = jnp.maximum(bounds[1], jnp.where(p < total, most, 1.0))
        row_inv, col_inv = lax.rsqrt(row_sum), lax.rsqrt(col_sum)
        row_top = jnp.max(weight * col_inv, axis=1, keepdims=True) * row_inv
        col_top = jnp.max(weight * row_inv, axis=0, keepdims=True) * col_inv
        record(p, row_top * row_top, col_top * col_top)

    def shifted(p, carry):
        held[0] = product(p) * score_scale
        value = held[0]
        row_peak = jnp.max(value, axis=1, keepdims=True)
        row_total = row_peak + jnp.log(jnp.sum(jnp.exp(value - row_peak), axis=1, keepdims=True))
        col_peak = jnp.max(value, axis=0, keepdims=True)
        col_total = col_peak + jnp.log(jnp.sum(jnp.exp(value - col_peak), axis=0, keepdims=True))
        value = (value - row_total) + (value - col_total)
        record(p, jnp.exp(jnp.max(value, axis=1, keepdims=True)), jnp.exp(jnp.max(value, axis=0, keepdims=True)))
        return carry

    def clear():
        by_row[...] = jnp.zeros_like(by_row)
        by_col[...] = jnp.zeros_like(by_col)

    for place, (source, first) in enumerate(pieces):
        piece = pltpu.make_async_copy(
            sources[source].at[pl.ds(first, deep)], arena.at[pl.ds(place * deep, deep)], sems.at[place]
        )
        pl.when(count_ref[place + 1] > 0)(piece.start)
    clear()
    bounds[...] = jnp.ones_like(bounds)

    def load(first, at, waited):
        needed = 1
        for g in range(GROUP):
            left, right = slots_of(first + g)
            needed = jnp.maximum(needed, lax.div(jnp.maximum(left, right), deep) + 1)
        waited = wait_until(needed, waited)
        for g in range(GROUP):
            held[at * GROUP + g] = product(first + g)
        return waited

    def rounds(k, waited):
        first = 2 * GROUP * k
        for at in range(2):
            waited = load(first + (at + 1) * GROUP, 1 - at, waited)
            for g in range(GROUP):
                plain(first + at * GROUP + g, held.at[at * GROUP + g])
        return waited

    @pl.when(total > 0)
    def all_pairs():
        waited = load(0, 0, jnp.int32(0))
        waited = lax.fori_loop(0, lax.div(total + 2 * GROUP - 1, 2 * GROUP), rounds, waited)
        wait_until(jnp.int32(len(pieces)), waited)

    fine = (jnp.min(bounds[0]) >= SUM_LOW) & (jnp.max(bounds[1]) <= SUM_HIGH)

    @pl.when(jnp.logical_not(fine))
    def again():
        clear()
        lax.fori_loop(0, total, shifted, 0)

    result = jnp.maximum(by_row[...].T, by_col[: by_row.shape[1], :]).astype(jnp.bfloat16)
    out_ref[...] = jnp.maximum(result, before_ref[...])


def confidences(lists, before, sources, pieces, deep, score_scale, work):
    count, slots, views = lists
    padded, length = before.shape
    width = sources[0].shape[2]
    smem = pl.BlockSpec(memory_space=pltpu.SMEM)
    vmem = pl.BlockSpec(memory_space=pltpu.VMEM)
    return pl.pallas_call(
        functools.partial(kernel, pieces, score_scale),
        out_shape=jax.ShapeDtypeStruct(before.shape, jnp.bfloat16),
        in_specs=[smem] * 3 + [vmem] + [pl.BlockSpec(memory_space=pl.ANY)] * len(sources),
        out_specs=vmem,
        scratch_shapes=[
            pltpu.VMEM((len(pieces) * deep, length, width), jnp.bfloat16),
            pltpu.VMEM((2 * GROUP, length, length), jnp.float32),
            pltpu.VMEM((length, padded), jnp.float32),
            pltpu.VMEM((padded + 8, length), jnp.float32),
            pltpu.VMEM((2, 1, 1), jnp.float32),
            pltpu.SemaphoreType.DMA((len(pieces),)),
        ],
        compiler_params=pltpu.CompilerParams(vmem_limit_bytes=56 * 1024 * 1024),
        cost_estimate=pl.CostEstimate(flops=work, bytes_accessed=0, transcendentals=0),
    )(count, slots, views, before, *sources)


def gather_small_slice(features, pairs, moves):
    send = lambda x, name: lax.ppermute(x, "owner", moves[name])
    tie = lax.optimization_barrier
    near, high = send(features, "near"), send(features, "high")
    flat = pairs.reshape(1, -1)
    flat = jnp.concatenate([flat, send(flat, "side")])
    own, flat = tie((features, flat))
    side = send(own, "side")
    flat = jnp.concatenate([flat, send(flat, "core")])
    shift = lambda s: [(i, (i + 4 * s) % 16) for i in range(16)]
    flat = jnp.concatenate([flat] + [lax.ppermute(flat, "owner", shift(s)) for s in (1, 2, 3)])
    flat, near, high = tie((flat, near, high))
    half = features.shape[0] // PIECES
    own, near, high = tie((features, near, high))
    far, cross = [send(own[:half], "far")], [send(own[:half], "cross")]
    swapped = [send(x, "core") for x in (near, high)]
    own, swapped[0], swapped[1] = tie((own, swapped[0], swapped[1]))
    far.append(send(own[half:], "far"))
    cross.append(send(own[half:], "cross"))
    swapped.append(send(side, "core"))
    return flat.reshape(-1, 2), [features, near, high, side, far, cross, *swapped, [], send(features, "core")]


def local(features, pairs):
    owners = lax.axis_size("owner")
    views_dev, length, width = features.shape
    flows, phases, table, order = make_plan(owners)
    if owners == 16:
        everyone, buffers = gather_small_slice(features, pairs, small_slice_moves())
    else:
        everyone = lax.all_gather(pairs, "owner", axis=0, tiled=True)
        buffers = [features] + [lax.ppermute(features, "owner", perm) for _, perm in flows]
    mine = jnp.asarray(table)[lax.axis_index("owner")]
    lists = pair_lists(everyone, mine, order, views_dev)
    deep = views_dev // PIECES
    padded = (owners * views_dev + LANES - 1) // LANES * LANES
    best = jnp.zeros((padded, length), jnp.bfloat16)
    for phase, (listed, wanted) in enumerate(zip(lists, phases)):
        if phase > 1:
            *far, best = lax.optimization_barrier((*buffers[4], best))
            buffers[LATE_BUFFER] = [lax.ppermute(x, "owner", small_slice_moves()["core"]) for x in far]
        sources, pieces = [], []
        for k, piece in wanted:
            cut = isinstance(buffers[k], list)
            part = buffers[k][piece] if cut else buffers[k]
            if not any(part is x for x in sources):
                sources.append(part)
            pieces.append(([part is x for x in sources].index(True), 0 if cut else piece * deep))
        best = confidences(listed, best, sources, tuple(pieces), deep, 10.0 / width, 10**8)
    outgoing = best[: owners * views_dev].reshape(owners, views_dev, length)
    returned = lax.all_to_all(outgoing, "owner", split_axis=0, concat_axis=0, tiled=True)
    return jnp.max(returned, axis=0)


def solution(mesh):
    placed = (P(("groups", "owner"), None, None), P(("groups", "owner"), None))
    return jax.shard_map(
        local, mesh=mesh, in_specs=placed, out_specs=P(("groups", "owner"), None), check_vma=False
    )
```

```python
import functools
import math

import jax
import jax.numpy as jnp
import numpy as np
from jax import lax
from jax.experimental import pallas as pl
from jax.experimental.pallas import tpu as pltpu
from jax.sharding import PartitionSpec as P

LANES = 128
SUM_LOW, SUM_HIGH = 1e-28, 1e36


PIECES = 2
GROUP = 2


def small_slice_moves():
    at = lambda z, y, c: (z * 2 + y) * 2 + c
    yc = [(y, c) for y in range(2) for c in range(2)]
    step = lambda z, t: [(at(z, y, c), at(t, y, c)) for y, c in yc]
    return dict(
        near=step(1, 2) + step(0, 1),
        high=step(3, 2) + step(2, 3),
        side=[(at(z, y, c), at(z, 1 - y, c)) for z in range(4) for y, c in yc],
        far=step(0, 2),
        cross=[(at(3, 1 - y, c), at(2, y, c)) for y, c in yc],
        core=[(i, i ^ 1) for i in range(16)],
    )


SMALL_FLOWS = [
    (0, "near"),
    (0, "high"),
    (0, "side"),
    (0, "far"),
    (0, "cross"),
    (1, "core"),
    (2, "core"),
    (3, "core"),
    (4, "core"),
    (0, "core"),
]
LATE_BUFFER = 9
EARLY = [(k, piece) for k in (0, 10, 3, 8, 2, 7, 1, 6) for piece in range(PIECES)]
SMALL_PHASES = [
    EARLY,
    [(4, 0)] + EARLY + [(5, 0)],
    [(4, 1)] + EARLY + [(5, 0), (5, 1), (4, 0), (9, 0), (9, 1)],
]


def cyclic_distances(owners):
    step = max(1, math.isqrt(owners // 2))
    reach = set(range(step))
    top = step - 1
    while top < owners // 2:
        top += step
        reach.add(top)
    return sorted({d % owners for d in reach} - {0})


@functools.lru_cache(None)
def make_plan(owners):
    if owners == 16:
        moves = small_slice_moves()
        flows = [(source, moves[name]) for source, name in SMALL_FLOWS]
        phases = SMALL_PHASES
    else:
        flows = [(0, [((i + d) % owners, i) for i in range(owners)]) for d in cyclic_distances(owners)]
        phases = [[(k, piece) for k in range(len(flows) + 1) for piece in range(PIECES)]]
    held = [[d] for d in range(owners)]
    for source, perm in flows:
        arrived = {t: held[s][source] for s, t in perm}
        for d in range(owners):
            held[d].append(arrived.get(d, -1))
    first = [{} for _ in range(owners)]
    for d in range(owners):
        for k, o in enumerate(held[d]):
            if o >= 0:
                first[d].setdefault(o, k)
    table = np.zeros((owners, owners, owners), np.int32)
    load = np.zeros(owners)
    choices = []
    for a in range(owners):
        for b in range(a, owners):
            at = [d for d in range(owners) if a in first[d] and b in first[d]]
            assert at
            choices.append((len(at), a, b, at))
    for _, a, b, at in sorted(choices):
        late = lambda d: owners == 16 and LATE_BUFFER in (first[d][a], first[d][b])
        d = min(at, key=lambda d: (late(d), load[d], d))
        load[d] += 1 if a == b else 2
        table[d, a, b] = first[d][a] * 64 + first[d][b] + 1
        table[d, b, a] = first[d][b] * 64 + first[d][a] + 1
    order = np.full((len(phases), (len(flows) + 1) * PIECES), -1, np.int32)
    for phase, pieces in enumerate(phases):
        for place, (k, piece) in enumerate(pieces):
            order[phase, k * PIECES + piece] = place
    return flows, phases, table, order


def pair_lists(pairs, mine, order, views_dev):
    count, owners = pairs.shape[0], mine.shape[0]
    left, right = pairs[:, 0], pairs[:, 1]
    is_left = (left // views_dev)[:, None] == jnp.arange(owners)[None, :]
    is_right = (right // views_dev)[:, None] == jnp.arange(owners)[None, :]
    row = jnp.dot(is_left.astype(jnp.float32), mine.astype(jnp.float32), precision=lax.Precision.HIGHEST)
    found = jnp.sum(jnp.where(is_right, row, 0.0), axis=1).astype(jnp.int32)
    buffers = jnp.maximum(found - 1, 0)
    deep = views_dev // PIECES
    left_piece = (buffers // 64) * PIECES + (left % views_dev) // deep
    right_piece = (buffers % 64) * PIECES + (right % views_dev) // deep
    place = jnp.arange(count)
    free = found > 0
    lists = []
    for phase in range(order.shape[0]):
        where = jnp.asarray(order[phase])[None, :]
        names = jnp.arange(order.shape[1])[None, :]
        left_at = jnp.sum(jnp.where(left_piece[:, None] == names, where, 0), axis=1)
        right_at = jnp.sum(jnp.where(right_piece[:, None] == names, where, 0), axis=1)
        chosen = free & (left_at >= 0) & (right_at >= 0)
        free = free & jnp.logical_not(chosen)
        key = jnp.maximum(left_at, right_at) * count + place
        rank = jnp.sum((key[None, :] < key[:, None]) & chosen[None, :], axis=1)
        picker = (rank[None, :] == place[:, None]) & chosen[None, :]
        slots = (left_at * deep + left % deep) * 1024 + right_at * deep + right % deep
        slots = jnp.sum(jnp.where(picker, slots[None, :], 0), axis=1)
        views = jnp.sum(jnp.where(picker, (left * 1024 + right)[None, :], 0), axis=1)
        used = ((left_at[:, None] == names) | (right_at[:, None] == names)) & chosen[:, None]
        counts = jnp.concatenate([jnp.sum(chosen.astype(jnp.int32)).reshape(1), jnp.any(used, axis=0).astype(jnp.int32)])
        lists.append((counts[None], slots[None], views[None]))
    return lists


def list_kernel(order, views_dev, mine_ref, pairs_ref, *outs):
    owners, count = mine_ref.shape[0], pairs_ref.shape[1]
    deep = views_dev // PIECES
    far_off = float(2**23)
    place = lax.broadcasted_iota(jnp.int32, (1, count), 1).astype(jnp.float32)
    steps = lambda x, width, most: sum((x >= k * width).astype(jnp.int32) for k in range(1, most))
    left, right = pairs_ref[0:1, :], pairs_ref[1:2, :]
    left_owner, right_owner = steps(left, views_dev, owners), steps(right, views_dev, owners)
    right_is = [right_owner == b for b in range(owners)]
    found = jnp.zeros((1, count), jnp.int32)
    for a in range(owners):
        row = jnp.zeros((1, count), jnp.int32)
        for b in range(owners):
            row = jnp.where(right_is[b], mine_ref[a, b], row)
        found = jnp.where(left_owner == a, row, found)
    buffers = jnp.maximum(found - 1, 0)
    left_view, right_view = left - left_owner * views_dev, right - right_owner * views_dev
    left_part, right_part = steps(left_view, deep, PIECES), steps(right_view, deep, PIECES)
    left_piece = lax.shift_right_logical(buffers, 6) * PIECES + left_part
    right_piece = lax.bitwise_and(buffers, 63) * PIECES + right_part
    column = lambda x: jnp.broadcast_to(x, (LANES, count)).T[:, 0:1]
    views = column((left * 1024 + right).astype(jnp.float32))
    free = found > 0
    for phase, where in enumerate(order):
        counts_ref, slots_out, views_out = outs[3 * phase : 3 * phase + 3]
        left_at, right_at = jnp.full((1, count), -1, jnp.int32), jnp.full((1, count), -1, jnp.int32)
        for name, at in enumerate(where):
            if at >= 0:
                left_at = jnp.where(left_piece == name, at, left_at)
                right_at = jnp.where(right_piece == name, at, right_at)
        chosen = free & (left_at >= 0) & (right_at >= 0)
        free = free & jnp.logical_not(chosen)
        key = jnp.where(chosen, jnp.maximum(left_at, right_at).astype(jnp.float32) * count + place, far_off)
        slots = (left_at * deep + left_view - left_part * deep) * 1024
        slots = (slots + right_at * deep + right_view - right_part * deep).astype(jnp.float32)
        own_key = column(key)
        rank = jnp.sum(jnp.where(key < own_key, 1.0, 0.0), axis=1, keepdims=True)
        rank = jnp.where(own_key < far_off, rank, -1.0)
        hit = rank == place
        slots_out[...] = jnp.sum(jnp.where(hit, column(slots), 0.0), axis=0, keepdims=True).astype(jnp.int32)
        views_out[...] = jnp.sum(jnp.where(hit, views, 0.0), axis=0, keepdims=True).astype(jnp.int32)
        picked = jnp.where(chosen, 1.0, 0.0)
        lane = lax.broadcasted_iota(jnp.int32, (1, LANES), 1)
        counts = jnp.where(lane == 0, jnp.sum(picked, axis=1, keepdims=True), 0.0)
        for at in range(sum(x >= 0 for x in where)):
            uses = jnp.where((left_at == at) | (right_at == at), picked, 0.0)
            counts = jnp.where(lane == at + 1, jnp.max(uses, axis=1, keepdims=True), counts)
        counts_ref[...] = counts.astype(jnp.int32)


def quick_lists(pairs, mine, order, views_dev):
    count = pairs.shape[1]
    vmem = pl.BlockSpec(memory_space=pltpu.VMEM)
    shape = lambda n: jax.ShapeDtypeStruct((1, n), jnp.int32)
    flat = pl.pallas_call(
        functools.partial(list_kernel, order.tolist(), views_dev),
        out_shape=[shape(LANES), shape(count), shape(count)] * len(order),
        in_specs=[pl.BlockSpec(memory_space=pltpu.SMEM), vmem],
        out_specs=[vmem] * (3 * len(order)),
        compiler_params=pltpu.CompilerParams(vmem_limit_bytes=32 * 1024 * 1024),
        cost_estimate=pl.CostEstimate(flops=1, bytes_accessed=0, transcendentals=0),
    )(mine, pairs)
    return [tuple(flat[k : k + 3]) for k in range(0, len(flat), 3)]


def kernel(pieces, score_scale, count_ref, slots_ref, views_ref, before_ref, *refs):
    sources = refs[:-7]
    out_ref, arena, held, by_row, by_col, bounds, sems = refs[-7:]
    length = arena.shape[1]
    deep = arena.shape[0] // len(pieces)
    total = count_ref[0, 0]
    limit = slots_ref.shape[1] - 1

    def slots_of(p):
        packed = slots_ref[0, jnp.minimum(p, limit)]
        return lax.shift_right_logical(packed, 10), lax.bitwise_and(packed, 1023)

    def wait_until(needed, waited):
        def wait(k, carry):
            part = arena.at[pl.ds(0, deep)]
            pl.when(count_ref[0, k + 1] > 0)(lambda: pltpu.make_async_copy(part, part, sems.at[k]).wait())
            return carry

        lax.fori_loop(waited, needed, wait, 0)
        return jnp.maximum(waited, needed)

    def product(p):
        left, right = slots_of(p)
        return lax.dot_general(
            arena[left], arena[right], (((1,), (1,)), ((), ())), preferred_element_type=jnp.float32
        )

    def record(p, row_conf, col_conf):
        packed = views_ref[0, jnp.minimum(p, limit)]
        real = p < total
        left = jnp.where(real, lax.shift_right_logical(packed, 10), -1)
        right = jnp.where(real, lax.bitwise_and(packed, 1023), by_row.shape[1])
        for tile in range(by_row.shape[1] // LANES):
            lane = lax.broadcasted_iota(jnp.int32, (length, LANES), 1) + tile * LANES
            at = (slice(None), slice(tile * LANES, (tile + 1) * LANES))
            by_row[at] = jnp.maximum(by_row[at], jnp.where(lane == left, row_conf, 0.0))
        by_col[pl.ds(right, 1), :] = jnp.maximum(by_col[pl.ds(right, 1), :], col_conf)

    def plain(p, scores):
        weight = jnp.exp2(scores[...] * (score_scale / math.log(2.0)))
        row_sum = jnp.sum(weight, axis=1, keepdims=True)
        col_sum = jnp.sum(weight, axis=0, keepdims=True)
        least = jnp.minimum(jnp.min(row_sum, axis=0, keepdims=True), jnp.min(col_sum, axis=1, keepdims=True))
        most = jnp.maximum(jnp.max(row_sum, axis=0, keepdims=True), jnp.max(col_sum, axis=1, keepdims=True))
        bounds[0] = jnp.minimum(bounds[0], jnp.where(p < total, least, 1.0))
        bounds[1] = jnp.maximum(bounds[1], jnp.where(p < total, most, 1.0))
        row_inv, col_inv = lax.rsqrt(row_sum), lax.rsqrt(col_sum)
        row_top = jnp.max(weight * col_inv, axis=1, keepdims=True) * row_inv
        col_top = jnp.max(weight * row_inv, axis=0, keepdims=True) * col_inv
        record(p, row_top * row_top, col_top * col_top)

    def shifted(p, carry):
        held[0] = product(p) * score_scale
        value = held[0]
        row_peak = jnp.max(value, axis=1, keepdims=True)
        row_total = row_peak + jnp.log(jnp.sum(jnp.exp(value - row_peak), axis=1, keepdims=True))
        col_peak = jnp.max(value, axis=0, keepdims=True)
        col_total = col_peak + jnp.log(jnp.sum(jnp.exp(value - col_peak), axis=0, keepdims=True))
        value = (value - row_total) + (value - col_total)
        record(p, jnp.exp(jnp.max(value, axis=1, keepdims=True)), jnp.exp(jnp.max(value, axis=0, keepdims=True)))
        return carry

    def clear():
        by_row[...] = jnp.zeros_like(by_row)
        by_col[...] = jnp.zeros_like(by_col)

    for place, (source, first) in enumerate(pieces):
        piece = pltpu.make_async_copy(
            sources[source].at[pl.ds(first, deep)], arena.at[pl.ds(place * deep, deep)], sems.at[place]
        )
        pl.when(count_ref[0, place + 1] > 0)(piece.start)
    clear()
    bounds[...] = jnp.ones_like(bounds)

    def load(first, at, waited):
        needed = 1
        for g in range(GROUP):
            left, right = slots_of(first + g)
            needed = jnp.maximum(needed, lax.div(jnp.maximum(left, right), deep) + 1)
        waited = wait_until(needed, waited)
        for g in range(GROUP):
            held[at * GROUP + g] = product(first + g)
        return waited

    def rounds(k, waited):
        first = 2 * GROUP * k
        for at in range(2):
            waited = load(first + (at + 1) * GROUP, 1 - at, waited)
            for g in range(GROUP):
                plain(first + at * GROUP + g, held.at[at * GROUP + g])
        return waited

    @pl.when(total > 0)
    def all_pairs():
        waited = load(0, 0, jnp.int32(0))
        waited = lax.fori_loop(0, lax.div(total + 2 * GROUP - 1, 2 * GROUP), rounds, waited)
        wait_until(jnp.int32(len(pieces)), waited)

    fine = (jnp.min(bounds[0]) >= SUM_LOW) & (jnp.max(bounds[1]) <= SUM_HIGH)

    @pl.when(jnp.logical_not(fine))
    def again():
        clear()
        lax.fori_loop(0, total, shifted, 0)

    result = jnp.maximum(by_row[...].T, by_col[: by_row.shape[1], :]).astype(jnp.bfloat16)
    out_ref[...] = jnp.maximum(result, before_ref[...])


def confidences(lists, before, sources, pieces, deep, score_scale, work):
    count, slots, views = lists
    padded, length = before.shape
    width = sources[0].shape[2]
    smem = pl.BlockSpec(memory_space=pltpu.SMEM)
    vmem = pl.BlockSpec(memory_space=pltpu.VMEM)
    return pl.pallas_call(
        functools.partial(kernel, pieces, score_scale),
        out_shape=jax.ShapeDtypeStruct(before.shape, jnp.bfloat16),
        in_specs=[smem] * 3 + [vmem] + [pl.BlockSpec(memory_space=pl.ANY)] * len(sources),
        out_specs=vmem,
        scratch_shapes=[
            pltpu.VMEM((len(pieces) * deep, length, width), jnp.bfloat16),
            pltpu.VMEM((2 * GROUP, length, length), jnp.float32),
            pltpu.VMEM((length, padded), jnp.float32),
            pltpu.VMEM((padded + 8, length), jnp.float32),
            pltpu.VMEM((2, 1, 1), jnp.float32),
            pltpu.SemaphoreType.DMA((len(pieces),)),
        ],
        compiler_params=pltpu.CompilerParams(vmem_limit_bytes=56 * 1024 * 1024),
        cost_estimate=pl.CostEstimate(flops=work, bytes_accessed=0, transcendentals=0),
    )(count, slots, views, before, *sources)


def gather_small_slice(features, pairs, moves):
    send = lambda x, name: lax.ppermute(x, "owner", moves[name])
    tie = lax.optimization_barrier
    near, high = send(features, "near"), send(features, "high")
    flat = pairs.T.reshape(1, -1)
    flat = jnp.concatenate([flat, send(flat, "side")])
    own, flat = tie((features, flat))
    side = send(own, "side")
    flat = jnp.concatenate([flat, send(flat, "core")])
    shift = lambda s: [(i, (i + 4 * s) % 16) for i in range(16)]
    flat = jnp.concatenate([flat] + [lax.ppermute(flat, "owner", shift(s)) for s in (1, 2, 3)])
    own_swapped = send(features, "core")
    flat, near, high, own_swapped = tie((flat, near, high, own_swapped))
    half = features.shape[0] // PIECES
    own, near, high = tie((features, near, high))
    far, cross = [send(own[:half], "far")], [send(own[:half], "cross")]
    swapped = [send(x, "core") for x in (near, high)]
    own, swapped[0], swapped[1] = tie((own, swapped[0], swapped[1]))
    far.append(send(own[half:], "far"))
    cross.append(send(own[half:], "cross"))
    swapped.append(send(side, "core"))
    everyone = flat.reshape(16, 2, -1).transpose(1, 0, 2).reshape(2, -1)
    return everyone, [features, near, high, side, far, cross, *swapped, [], own_swapped]


def local(features, pairs):
    owners = lax.axis_size("owner")
    views_dev, length, width = features.shape
    flows, phases, table, order = make_plan(owners)
    mine = jnp.asarray(table)[lax.axis_index("owner")]
    if owners == 16:
        everyone, buffers = gather_small_slice(features, pairs, small_slice_moves())
        lists = quick_lists(everyone, mine, order, views_dev)
    else:
        everyone = lax.all_gather(pairs, "owner", axis=0, tiled=True)
        buffers = [features] + [lax.ppermute(features, "owner", perm) for _, perm in flows]
        lists = pair_lists(everyone, mine, order, views_dev)
    deep = views_dev // PIECES
    padded = (owners * views_dev + LANES - 1) // LANES * LANES
    best = jnp.zeros((padded, length), jnp.bfloat16)
    for phase, (listed, wanted) in enumerate(zip(lists, phases)):
        if phase > 1:
            *far, best = lax.optimization_barrier((*buffers[4], best))
            buffers[LATE_BUFFER] = [lax.ppermute(x, "owner", small_slice_moves()["core"]) for x in far]
        sources, pieces = [], []
        for k, piece in wanted:
            cut = isinstance(buffers[k], list)
            part = buffers[k][piece] if cut else buffers[k]
            if not any(part is x for x in sources):
                sources.append(part)
            pieces.append(([part is x for x in sources].index(True), 0 if cut else piece * deep))
        best = confidences(listed, best, sources, tuple(pieces), deep, 10.0 / width, 10**8)
    outgoing = best[: owners * views_dev].reshape(owners, views_dev, length)
    returned = lax.all_to_all(outgoing, "owner", split_axis=0, concat_axis=0, tiled=True)
    return jnp.max(returned, axis=0)


def solution(mesh):
    placed = (P(("groups", "owner"), None, None), P(("groups", "owner"), None))
    return jax.shard_map(
        local, mesh=mesh, in_specs=placed, out_specs=P(("groups", "owner"), None), check_vma=False
    )
```

```python
import functools
import math

import jax
import jax.numpy as jnp
import numpy as np
from jax import lax
from jax.experimental import pallas as pl
from jax.experimental.pallas import tpu as pltpu
from jax.sharding import PartitionSpec as P

LANES = 128
SUM_LOW, SUM_HIGH = 1e-28, 1e36


PIECES = 2
GROUP = 2


def small_slice_moves():
    at = lambda z, y, c: (z * 2 + y) * 2 + c
    yc = [(y, c) for y in range(2) for c in range(2)]
    step = lambda z, t: [(at(z, y, c), at(t, y, c)) for y, c in yc]
    return dict(
        near=step(1, 2) + step(0, 1),
        high=step(3, 2) + step(2, 3),
        side=[(at(z, y, c), at(z, 1 - y, c)) for z in range(4) for y, c in yc],
        far=step(0, 2),
        cross=[(at(3, 1 - y, c), at(2, y, c)) for y, c in yc],
        core=[(i, i ^ 1) for i in range(16)],
    )


SMALL_FLOWS = [
    (0, "near"),
    (0, "high"),
    (0, "side"),
    (0, "far"),
    (0, "cross"),
    (1, "core"),
    (2, "core"),
    (3, "core"),
    (4, "core"),
    (0, "core"),
]
LATE_BUFFER = 9
EARLY = [(k, piece) for k in (0, 10, 3, 8, 2, 7, 1, 6) for piece in range(PIECES)]
SMALL_PHASES = [
    EARLY,
    [(4, 0)] + EARLY + [(5, 0)],
    [(4, 1)] + EARLY + [(5, 0), (5, 1), (4, 0), (9, 0), (9, 1)],
]


def cyclic_distances(owners):
    step = max(1, math.isqrt(owners // 2))
    reach = set(range(step))
    top = step - 1
    while top < owners // 2:
        top += step
        reach.add(top)
    return sorted({d % owners for d in reach} - {0})


@functools.lru_cache(None)
def make_plan(owners):
    if owners == 16:
        moves = small_slice_moves()
        flows = [(source, moves[name]) for source, name in SMALL_FLOWS]
        phases = SMALL_PHASES
    else:
        flows = [(0, [((i + d) % owners, i) for i in range(owners)]) for d in cyclic_distances(owners)]
        phases = [[(k, piece) for k in range(len(flows) + 1) for piece in range(PIECES)]]
    held = [[d] for d in range(owners)]
    for source, perm in flows:
        arrived = {t: held[s][source] for s, t in perm}
        for d in range(owners):
            held[d].append(arrived.get(d, -1))
    first = [{} for _ in range(owners)]
    for d in range(owners):
        for k, o in enumerate(held[d]):
            if o >= 0:
                first[d].setdefault(o, k)
    table = np.zeros((owners, owners, owners), np.int32)
    load = np.zeros(owners)
    choices = []
    for a in range(owners):
        for b in range(a, owners):
            at = [d for d in range(owners) if a in first[d] and b in first[d]]
            assert at
            choices.append((len(at), a, b, at))
    for _, a, b, at in sorted(choices):
        late = lambda d: owners == 16 and LATE_BUFFER in (first[d][a], first[d][b])
        d = min(at, key=lambda d: (late(d), load[d], d))
        load[d] += 1 if a == b else 2
        table[d, a, b] = first[d][a] * 64 + first[d][b] + 1
        table[d, b, a] = first[d][b] * 64 + first[d][a] + 1
    order = np.full((len(phases), (len(flows) + 1) * PIECES), -1, np.int32)
    for phase, pieces in enumerate(phases):
        for place, (k, piece) in enumerate(pieces):
            order[phase, k * PIECES + piece] = place
    return flows, phases, table, order


def pair_lists(pairs, mine, order, views_dev):
    count, owners = pairs.shape[0], mine.shape[0]
    left, right = pairs[:, 0], pairs[:, 1]
    is_left = (left // views_dev)[:, None] == jnp.arange(owners)[None, :]
    is_right = (right // views_dev)[:, None] == jnp.arange(owners)[None, :]
    row = jnp.dot(is_left.astype(jnp.float32), mine.astype(jnp.float32), precision=lax.Precision.HIGHEST)
    found = jnp.sum(jnp.where(is_right, row, 0.0), axis=1).astype(jnp.int32)
    buffers = jnp.maximum(found - 1, 0)
    deep = views_dev // PIECES
    left_piece = (buffers // 64) * PIECES + (left % views_dev) // deep
    right_piece = (buffers % 64) * PIECES + (right % views_dev) // deep
    place = jnp.arange(count)
    free = found > 0
    lists = []
    for phase in range(order.shape[0]):
        where = jnp.asarray(order[phase])[None, :]
        names = jnp.arange(order.shape[1])[None, :]
        left_at = jnp.sum(jnp.where(left_piece[:, None] == names, where, 0), axis=1)
        right_at = jnp.sum(jnp.where(right_piece[:, None] == names, where, 0), axis=1)
        chosen = free & (left_at >= 0) & (right_at >= 0)
        free = free & jnp.logical_not(chosen)
        key = jnp.maximum(left_at, right_at) * count + place
        rank = jnp.sum((key[None, :] < key[:, None]) & chosen[None, :], axis=1)
        picker = (rank[None, :] == place[:, None]) & chosen[None, :]
        slots = (left_at * deep + left % deep) * 1024 + right_at * deep + right % deep
        slots = jnp.sum(jnp.where(picker, slots[None, :], 0), axis=1)
        views = jnp.sum(jnp.where(picker, (left * 1024 + right)[None, :], 0), axis=1)
        used = ((left_at[:, None] == names) | (right_at[:, None] == names)) & chosen[:, None]
        counts = jnp.concatenate([jnp.sum(chosen.astype(jnp.int32)).reshape(1), jnp.any(used, axis=0).astype(jnp.int32)])
        lists += [jnp.pad(counts, (0, count - counts.shape[0])), slots, views]
    return jnp.stack(lists)


def list_kernel(order, views_dev, mine_ref, pairs_ref, out_ref):
    owners, count = mine_ref.shape[0], pairs_ref.shape[1]
    deep = views_dev // PIECES
    far_off = float(2**23)
    place = lax.broadcasted_iota(jnp.int32, (1, count), 1).astype(jnp.float32)
    steps = lambda x, width, most: sum((x >= k * width).astype(jnp.int32) for k in range(1, most))
    left, right = pairs_ref[0:1, :], pairs_ref[1:2, :]
    left_owner, right_owner = steps(left, views_dev, owners), steps(right, views_dev, owners)
    right_is = [right_owner == b for b in range(owners)]
    found = jnp.zeros((1, count), jnp.int32)
    for a in range(owners):
        row = jnp.zeros((1, count), jnp.int32)
        for b in range(owners):
            row = jnp.where(right_is[b], mine_ref[a, b], row)
        found = jnp.where(left_owner == a, row, found)
    buffers = jnp.maximum(found - 1, 0)
    left_view, right_view = left - left_owner * views_dev, right - right_owner * views_dev
    left_part, right_part = steps(left_view, deep, PIECES), steps(right_view, deep, PIECES)
    left_piece = lax.shift_right_logical(buffers, 6) * PIECES + left_part
    right_piece = lax.bitwise_and(buffers, 63) * PIECES + right_part
    column = lambda x: jnp.broadcast_to(x, (LANES, count)).T[:, 0:1]
    views = column((left * 1024 + right).astype(jnp.float32))
    free = found > 0
    for phase, where in enumerate(order):
        left_at, right_at = jnp.full((1, count), -1, jnp.int32), jnp.full((1, count), -1, jnp.int32)
        for name, at in enumerate(where):
            if at >= 0:
                left_at = jnp.where(left_piece == name, at, left_at)
                right_at = jnp.where(right_piece == name, at, right_at)
        chosen = free & (left_at >= 0) & (right_at >= 0)
        free = free & jnp.logical_not(chosen)
        key = jnp.where(chosen, jnp.maximum(left_at, right_at).astype(jnp.float32) * count + place, far_off)
        slots = (left_at * deep + left_view - left_part * deep) * 1024
        slots = (slots + right_at * deep + right_view - right_part * deep).astype(jnp.float32)
        own_key = column(key)
        rank = jnp.sum(jnp.where(key < own_key, 1.0, 0.0), axis=1, keepdims=True)
        rank = jnp.where(own_key < far_off, rank, -1.0)
        hit = rank == place
        out_ref[3 * phase + 1 : 3 * phase + 2, :] = jnp.sum(jnp.where(hit, column(slots), 0.0), axis=0, keepdims=True).astype(jnp.int32)
        out_ref[3 * phase + 2 : 3 * phase + 3, :] = jnp.sum(jnp.where(hit, views, 0.0), axis=0, keepdims=True).astype(jnp.int32)
        picked = jnp.where(chosen, 1.0, 0.0)
        lane = lax.broadcasted_iota(jnp.int32, (1, LANES), 1)
        counts = jnp.where(lane == 0, jnp.sum(picked, axis=1, keepdims=True), 0.0)
        for at in range(sum(x >= 0 for x in where)):
            uses = jnp.where((left_at == at) | (right_at == at), picked, 0.0)
            counts = jnp.where(lane == at + 1, jnp.max(uses, axis=1, keepdims=True), counts)
        out_ref[3 * phase : 3 * phase + 1, 0:LANES] = counts.astype(jnp.int32)


def quick_lists(pairs, mine, order, views_dev):
    count = pairs.shape[1]
    vmem = pl.BlockSpec(memory_space=pltpu.VMEM)
    return pl.pallas_call(
        functools.partial(list_kernel, order.tolist(), views_dev),
        out_shape=jax.ShapeDtypeStruct((3 * len(order), count), jnp.int32),
        in_specs=[pl.BlockSpec(memory_space=pltpu.SMEM), vmem],
        out_specs=vmem,
        compiler_params=pltpu.CompilerParams(vmem_limit_bytes=32 * 1024 * 1024),
        cost_estimate=pl.CostEstimate(flops=1, bytes_accessed=0, transcendentals=0),
    )(mine, pairs)


def kernel(pieces, row, score_scale, lists_ref, before_ref, *refs):
    sources = refs[:-7]
    out_ref, arena, held, by_row, by_col, bounds, sems = refs[-7:]
    length = arena.shape[1]
    deep = arena.shape[0] // len(pieces)
    total = lists_ref[row, 0]
    limit = lists_ref.shape[1] - 1

    def slots_of(p):
        packed = lists_ref[row + 1, jnp.minimum(p, limit)]
        return lax.shift_right_logical(packed, 10), lax.bitwise_and(packed, 1023)

    def wait_until(needed, waited):
        def wait(k, carry):
            part = arena.at[pl.ds(0, deep)]
            pl.when(lists_ref[row, k + 1] > 0)(lambda: pltpu.make_async_copy(part, part, sems.at[k]).wait())
            return carry

        lax.fori_loop(waited, needed, wait, 0)
        return jnp.maximum(waited, needed)

    def product(p):
        left, right = slots_of(p)
        return lax.dot_general(
            arena[left], arena[right], (((1,), (1,)), ((), ())), preferred_element_type=jnp.float32
        )

    def record(p, row_conf, col_conf):
        packed = lists_ref[row + 2, jnp.minimum(p, limit)]
        real = p < total
        left = jnp.where(real, lax.shift_right_logical(packed, 10), -1)
        right = jnp.where(real, lax.bitwise_and(packed, 1023), by_row.shape[1])
        for tile in range(by_row.shape[1] // LANES):
            lane = lax.broadcasted_iota(jnp.int32, (length, LANES), 1) + tile * LANES
            at = (slice(None), slice(tile * LANES, (tile + 1) * LANES))
            by_row[at] = jnp.maximum(by_row[at], jnp.where(lane == left, row_conf, 0.0))
        by_col[pl.ds(right, 1), :] = jnp.maximum(by_col[pl.ds(right, 1), :], col_conf)

    def plain(p, scores):
        weight = jnp.exp2(scores[...] * (score_scale / math.log(2.0)))
        row_sum = jnp.sum(weight, axis=1, keepdims=True)
        col_sum = jnp.sum(weight, axis=0, keepdims=True)
        least = jnp.minimum(jnp.min(row_sum, axis=0, keepdims=True), jnp.min(col_sum, axis=1, keepdims=True))
        most = jnp.maximum(jnp.max(row_sum, axis=0, keepdims=True), jnp.max(col_sum, axis=1, keepdims=True))
        bounds[0] = jnp.minimum(bounds[0], jnp.where(p < total, least, 1.0))
        bounds[1] = jnp.maximum(bounds[1], jnp.where(p < total, most, 1.0))
        row_inv, col_inv = lax.rsqrt(row_sum), lax.rsqrt(col_sum)
        row_top = jnp.max(weight * col_inv, axis=1, keepdims=True) * row_inv
        col_top = jnp.max(weight * row_inv, axis=0, keepdims=True) * col_inv
        record(p, row_top * row_top, col_top * col_top)

    def shifted(p, carry):
        held[0] = product(p) * score_scale
        value = held[0]
        row_peak = jnp.max(value, axis=1, keepdims=True)
        row_total = row_peak + jnp.log(jnp.sum(jnp.exp(value - row_peak), axis=1, keepdims=True))
        col_peak = jnp.max(value, axis=0, keepdims=True)
        col_total = col_peak + jnp.log(jnp.sum(jnp.exp(value - col_peak), axis=0, keepdims=True))
        value = (value - row_total) + (value - col_total)
        record(p, jnp.exp(jnp.max(value, axis=1, keepdims=True)), jnp.exp(jnp.max(value, axis=0, keepdims=True)))
        return carry

    def clear():
        by_row[...] = jnp.zeros_like(by_row)
        by_col[...] = jnp.zeros_like(by_col)

    for place, (source, first) in enumerate(pieces):
        piece = pltpu.make_async_copy(
            sources[source].at[pl.ds(first, deep)], arena.at[pl.ds(place * deep, deep)], sems.at[place]
        )
        pl.when(lists_ref[row, place + 1] > 0)(piece.start)
    clear()
    bounds[...] = jnp.ones_like(bounds)

    def load(first, at, waited):
        needed = 1
        for g in range(GROUP):
            left, right = slots_of(first + g)
            needed = jnp.maximum(needed, lax.div(jnp.maximum(left, right), deep) + 1)
        waited = wait_until(needed, waited)
        for g in range(GROUP):
            held[at * GROUP + g] = product(first + g)
        return waited

    def rounds(k, waited):
        first = 2 * GROUP * k
        for at in range(2):
            waited = load(first + (at + 1) * GROUP, 1 - at, waited)
            for g in range(GROUP):
                plain(first + at * GROUP + g, held.at[at * GROUP + g])
        return waited

    @pl.when(total > 0)
    def all_pairs():
        waited = load(0, 0, jnp.int32(0))
        waited = lax.fori_loop(0, lax.div(total + 2 * GROUP - 1, 2 * GROUP), rounds, waited)
        wait_until(jnp.int32(len(pieces)), waited)

    fine = (jnp.min(bounds[0]) >= SUM_LOW) & (jnp.max(bounds[1]) <= SUM_HIGH)

    @pl.when(jnp.logical_not(fine))
    def again():
        clear()
        lax.fori_loop(0, total, shifted, 0)

    result = jnp.maximum(by_row[...].T, by_col[: by_row.shape[1], :]).astype(jnp.bfloat16)
    out_ref[...] = jnp.maximum(result, before_ref[...])


def confidences(lists, phase, before, sources, pieces, deep, score_scale, work):
    padded, length = before.shape
    width = sources[0].shape[2]
    smem = pl.BlockSpec(memory_space=pltpu.SMEM)
    vmem = pl.BlockSpec(memory_space=pltpu.VMEM)
    return pl.pallas_call(
        functools.partial(kernel, pieces, 3 * phase, score_scale),
        out_shape=jax.ShapeDtypeStruct(before.shape, jnp.bfloat16),
        in_specs=[smem, vmem] + [pl.BlockSpec(memory_space=pl.ANY)] * len(sources),
        out_specs=vmem,
        scratch_shapes=[
            pltpu.VMEM((len(pieces) * deep, length, width), jnp.bfloat16),
            pltpu.VMEM((2 * GROUP, length, length), jnp.float32),
            pltpu.VMEM((length, padded), jnp.float32),
            pltpu.VMEM((padded + 8, length), jnp.float32),
            pltpu.VMEM((2, 1, 1), jnp.float32),
            pltpu.SemaphoreType.DMA((len(pieces),)),
        ],
        compiler_params=pltpu.CompilerParams(vmem_limit_bytes=56 * 1024 * 1024),
        cost_estimate=pl.CostEstimate(flops=work, bytes_accessed=0, transcendentals=0),
    )(lists, before, *sources)


def gather_small_slice(features, pairs, moves, make_lists):
    send = lambda x, name: lax.ppermute(x, "owner", moves[name])
    tie = lax.optimization_barrier
    flat = pairs.T.reshape(1, -1)
    shift = lambda s: [(i, (i + 4 * s) % 16) for i in range(16)]
    flat = jnp.concatenate([flat] + [lax.ppermute(flat, "owner", shift(s)) for s in (1, 2, 3)])
    own, flat = tie((features, flat))
    near, high = send(own, "near"), send(own, "high")
    flat = jnp.concatenate([flat, send(flat, "side")])
    own, flat = tie((features, flat))
    side = send(own, "side")
    flat = jnp.concatenate([flat, send(flat, "core")])
    lists = make_lists(flat.reshape(16, 2, -1).transpose(1, 0, 2).reshape(2, -1))
    half = features.shape[0] // PIECES
    halves = [features[:half], features[half:]]
    own_swapped = send(features, "core")
    near, high, lists, own_swapped, *halves = tie((near, high, lists, own_swapped, *halves))
    far, cross = [send(halves[0], "far")], [send(halves[0], "cross")]
    swapped = [send(x, "core") for x in (near, high)]
    second, swapped[0] = tie((halves[1], swapped[0]))
    far.append(send(second, "far"))
    cross.append(send(second, "cross"))
    swapped.append(send(side, "core"))
    return lists, [features, near, high, side, far, cross, *swapped, [], own_swapped]


def local(features, pairs):
    owners = lax.axis_size("owner")
    views_dev, length, width = features.shape
    flows, phases, table, order = make_plan(owners)
    mine = jnp.asarray(table)[lax.axis_index("owner")]
    if owners == 16:
        make_lists = lambda everyone: quick_lists(everyone, mine, order, views_dev)
        lists, buffers = gather_small_slice(features, pairs, small_slice_moves(), make_lists)
    else:
        everyone = lax.all_gather(pairs, "owner", axis=0, tiled=True)
        buffers = [features] + [lax.ppermute(features, "owner", perm) for _, perm in flows]
        lists = pair_lists(everyone, mine, order, views_dev)
    deep = views_dev // PIECES
    padded = (owners * views_dev + LANES - 1) // LANES * LANES
    best = jnp.zeros((padded, length), jnp.bfloat16)
    for phase, wanted in enumerate(phases):
        if phase > 1:
            *far, best = lax.optimization_barrier((*buffers[4], best))
            buffers[LATE_BUFFER] = [lax.ppermute(x, "owner", small_slice_moves()["core"]) for x in far]
        sources, pieces = [], []
        for k, piece in wanted:
            cut = isinstance(buffers[k], list)
            part = buffers[k][piece] if cut else buffers[k]
            if not any(part is x for x in sources):
                sources.append(part)
            pieces.append(([part is x for x in sources].index(True), 0 if cut else piece * deep))
        best = confidences(lists, phase, best, sources, tuple(pieces), deep, 10.0 / width, 10**8)
    outgoing = best[: owners * views_dev].reshape(owners, views_dev, length)
    returned = lax.all_to_all(outgoing, "owner", split_axis=0, concat_axis=0, tiled=True)
    return jnp.max(returned, axis=0)


def solution(mesh):
    placed = (P(("groups", "owner"), None, None), P(("groups", "owner"), None))
    return jax.shard_map(
        local, mesh=mesh, in_specs=placed, out_specs=P(("groups", "owner"), None), check_vma=False
    )
```

```python
import functools
import math

import jax
import jax.numpy as jnp
import numpy as np
from jax import lax
from jax.experimental import pallas as pl
from jax.experimental.pallas import tpu as pltpu
from jax.sharding import PartitionSpec as P

LANES = 128
SUM_LOW, SUM_HIGH = 1e-28, 1e35


PIECES = 2
GROUP = 2


def small_slice_moves():
    at = lambda z, y, c: (z * 2 + y) * 2 + c
    yc = [(y, c) for y in range(2) for c in range(2)]
    step = lambda z, t: [(at(z, y, c), at(t, y, c)) for y, c in yc]
    return dict(
        near=step(1, 2) + step(0, 1),
        high=step(3, 2) + step(2, 3),
        side=[(at(z, y, c), at(z, 1 - y, c)) for z in range(4) for y, c in yc],
        far=step(0, 2),
        cross=[(at(3, 1 - y, c), at(2, y, c)) for y, c in yc],
        core=[(i, i ^ 1) for i in range(16)],
    )


SMALL_FLOWS = [
    (0, "near"),
    (0, "high"),
    (0, "side"),
    (0, "far"),
    (0, "cross"),
    (1, "core"),
    (2, "core"),
    (3, "core"),
    (4, "core"),
    (0, "core"),
]
LATE_BUFFER = 9
EARLY = [(k, piece) for k in (0, 10, 3, 8, 2, 7, 1, 6) for piece in range(PIECES)]
SMALL_PHASES = [
    EARLY,
    [(4, 0)] + EARLY + [(5, 0)],
    [(4, 1)] + EARLY + [(5, 0), (5, 1), (4, 0), (9, 0), (9, 1)],
]


def cyclic_distances(owners):
    step = max(1, math.isqrt(owners // 2))
    reach = set(range(step))
    top = step - 1
    while top < owners // 2:
        top += step
        reach.add(top)
    return sorted({d % owners for d in reach} - {0})


@functools.lru_cache(None)
def make_plan(owners):
    if owners == 16:
        moves = small_slice_moves()
        flows = [(source, moves[name]) for source, name in SMALL_FLOWS]
        phases = SMALL_PHASES
    else:
        flows = [(0, [((i + d) % owners, i) for i in range(owners)]) for d in cyclic_distances(owners)]
        phases = [[(k, piece) for k in range(len(flows) + 1) for piece in range(PIECES)]]
    held = [[d] for d in range(owners)]
    for source, perm in flows:
        arrived = {t: held[s][source] for s, t in perm}
        for d in range(owners):
            held[d].append(arrived.get(d, -1))
    first = [{} for _ in range(owners)]
    for d in range(owners):
        for k, o in enumerate(held[d]):
            if o >= 0:
                first[d].setdefault(o, k)
    table = np.zeros((owners, owners, owners), np.int32)
    load = np.zeros(owners)
    choices = []
    for a in range(owners):
        for b in range(a, owners):
            at = [d for d in range(owners) if a in first[d] and b in first[d]]
            assert at
            choices.append((len(at), a, b, at))
    for _, a, b, at in sorted(choices):
        late = lambda d: owners == 16 and LATE_BUFFER in (first[d][a], first[d][b])
        d = min(at, key=lambda d: (late(d), load[d], d))
        load[d] += 1 if a == b else 2
        table[d, a, b] = first[d][a] * 64 + first[d][b] + 1
        table[d, b, a] = first[d][b] * 64 + first[d][a] + 1
    order = np.full((len(phases), (len(flows) + 1) * PIECES), -1, np.int32)
    for phase, pieces in enumerate(phases):
        for place, (k, piece) in enumerate(pieces):
            order[phase, k * PIECES + piece] = place
    return flows, phases, table, order


def pair_lists(pairs, mine, order, views_dev):
    count, owners = pairs.shape[0], mine.shape[0]
    left, right = pairs[:, 0], pairs[:, 1]
    is_left = (left // views_dev)[:, None] == jnp.arange(owners)[None, :]
    is_right = (right // views_dev)[:, None] == jnp.arange(owners)[None, :]
    row = jnp.dot(is_left.astype(jnp.float32), mine.astype(jnp.float32), precision=lax.Precision.HIGHEST)
    found = jnp.sum(jnp.where(is_right, row, 0.0), axis=1).astype(jnp.int32)
    buffers = jnp.maximum(found - 1, 0)
    deep = views_dev // PIECES
    left_piece = (buffers // 64) * PIECES + (left % views_dev) // deep
    right_piece = (buffers % 64) * PIECES + (right % views_dev) // deep
    place = jnp.arange(count)
    free = found > 0
    lists = []
    for phase in range(order.shape[0]):
        where = jnp.asarray(order[phase])[None, :]
        names = jnp.arange(order.shape[1])[None, :]
        left_at = jnp.sum(jnp.where(left_piece[:, None] == names, where, 0), axis=1)
        right_at = jnp.sum(jnp.where(right_piece[:, None] == names, where, 0), axis=1)
        chosen = free & (left_at >= 0) & (right_at >= 0)
        free = free & jnp.logical_not(chosen)
        key = jnp.maximum(left_at, right_at) * count + place
        rank = jnp.sum((key[None, :] < key[:, None]) & chosen[None, :], axis=1)
        picker = (rank[None, :] == place[:, None]) & chosen[None, :]
        slots = (left_at * deep + left % deep) * 1024 + right_at * deep + right % deep
        slots = jnp.sum(jnp.where(picker, slots[None, :], 0), axis=1)
        views = jnp.sum(jnp.where(picker, (left * 1024 + right)[None, :], 0), axis=1)
        used = ((left_at[:, None] == names) | (right_at[:, None] == names)) & chosen[:, None]
        counts = jnp.concatenate([jnp.sum(chosen.astype(jnp.int32)).reshape(1), jnp.any(used, axis=0).astype(jnp.int32)])
        lists += [jnp.pad(counts, (0, count - counts.shape[0])), slots, views]
    return jnp.stack(lists)


def list_kernel(order, views_dev, mine_ref, pairs_ref, out_ref):
    owners, count = mine_ref.shape[0], pairs_ref.shape[1]
    deep = views_dev // PIECES
    far_off = float(2**23)
    place = lax.broadcasted_iota(jnp.int32, (1, count), 1).astype(jnp.float32)
    steps = lambda x, width, most: sum((x >= k * width).astype(jnp.int32) for k in range(1, most))
    left, right = pairs_ref[0:1, :], pairs_ref[1:2, :]
    left_owner, right_owner = steps(left, views_dev, owners), steps(right, views_dev, owners)
    right_is = [right_owner == b for b in range(owners)]
    found = jnp.zeros((1, count), jnp.int32)
    for a in range(owners):
        row = jnp.zeros((1, count), jnp.int32)
        for b in range(owners):
            row = jnp.where(right_is[b], mine_ref[a, b], row)
        found = jnp.where(left_owner == a, row, found)
    buffers = jnp.maximum(found - 1, 0)
    left_view, right_view = left - left_owner * views_dev, right - right_owner * views_dev
    left_part, right_part = steps(left_view, deep, PIECES), steps(right_view, deep, PIECES)
    left_piece = lax.shift_right_logical(buffers, 6) * PIECES + left_part
    right_piece = lax.bitwise_and(buffers, 63) * PIECES + right_part
    column = lambda x: jnp.broadcast_to(x, (LANES, count)).T[:, 0:1]
    views = column((left * 1024 + right).astype(jnp.float32))
    free = found > 0
    for phase, where in enumerate(order):
        left_at, right_at = jnp.full((1, count), -1, jnp.int32), jnp.full((1, count), -1, jnp.int32)
        for name, at in enumerate(where):
            if at >= 0:
                left_at = jnp.where(left_piece == name, at, left_at)
                right_at = jnp.where(right_piece == name, at, right_at)
        chosen = free & (left_at >= 0) & (right_at >= 0)
        free = free & jnp.logical_not(chosen)
        key = jnp.where(chosen, jnp.maximum(left_at, right_at).astype(jnp.float32) * count + place, far_off)
        slots = (left_at * deep + left_view - left_part * deep) * 1024
        slots = (slots + right_at * deep + right_view - right_part * deep).astype(jnp.float32)
        own_key = column(key)
        rank = jnp.sum(jnp.where(key < own_key, 1.0, 0.0), axis=1, keepdims=True)
        rank = jnp.where(own_key < far_off, rank, -1.0)
        hit = rank == place
        out_ref[3 * phase + 1 : 3 * phase + 2, :] = jnp.sum(jnp.where(hit, column(slots), 0.0), axis=0, keepdims=True).astype(jnp.int32)
        out_ref[3 * phase + 2 : 3 * phase + 3, :] = jnp.sum(jnp.where(hit, views, 0.0), axis=0, keepdims=True).astype(jnp.int32)
        picked = jnp.where(chosen, 1.0, 0.0)
        lane = lax.broadcasted_iota(jnp.int32, (1, LANES), 1)
        counts = jnp.where(lane == 0, jnp.sum(picked, axis=1, keepdims=True), 0.0)
        for at in range(sum(x >= 0 for x in where)):
            uses = jnp.where((left_at == at) | (right_at == at), picked, 0.0)
            counts = jnp.where(lane == at + 1, jnp.max(uses, axis=1, keepdims=True), counts)
        out_ref[3 * phase : 3 * phase + 1, 0:LANES] = counts.astype(jnp.int32)


def quick_lists(pairs, mine, order, views_dev):
    count = pairs.shape[1]
    vmem = pl.BlockSpec(memory_space=pltpu.VMEM)
    return pl.pallas_call(
        functools.partial(list_kernel, order.tolist(), views_dev),
        out_shape=jax.ShapeDtypeStruct((3 * len(order), count), jnp.int32),
        in_specs=[pl.BlockSpec(memory_space=pltpu.SMEM), vmem],
        out_specs=vmem,
        compiler_params=pltpu.CompilerParams(vmem_limit_bytes=32 * 1024 * 1024),
        cost_estimate=pl.CostEstimate(flops=1, bytes_accessed=0, transcendentals=0),
    )(mine, pairs)


def kernel(pieces, row, score_scale, lists_ref, before_ref, *refs):
    sources = refs[:-7]
    out_ref, arena, held, by_row, by_col, bounds, sems = refs[-7:]
    length = arena.shape[1]
    deep = arena.shape[0] // len(pieces)
    total = lists_ref[row, 0]
    limit = lists_ref.shape[1] - 1

    def slots_of(p):
        packed = lists_ref[row + 1, jnp.minimum(p, limit)]
        return lax.shift_right_logical(packed, 10), lax.bitwise_and(packed, 1023)

    def wait_until(needed, waited):
        def wait(k, carry):
            part = arena.at[pl.ds(0, deep)]
            pl.when(lists_ref[row, k + 1] > 0)(lambda: pltpu.make_async_copy(part, part, sems.at[k]).wait())
            return carry

        lax.fori_loop(waited, needed, wait, 0)
        return jnp.maximum(waited, needed)

    def product(p):
        left, right = slots_of(p)
        return lax.dot_general(
            arena[left], arena[right], (((1,), (1,)), ((), ())), preferred_element_type=jnp.float32
        )

    def record(p, row_conf, col_conf):
        packed = lists_ref[row + 2, jnp.minimum(p, limit)]
        real = p < total
        left = jnp.where(real, lax.shift_right_logical(packed, 10), -1)
        right = jnp.where(real, lax.bitwise_and(packed, 1023), by_row.shape[1])
        for tile in range(by_row.shape[1] // LANES):
            lane = lax.broadcasted_iota(jnp.int32, (length, LANES), 1) + tile * LANES
            at = (slice(None), slice(tile * LANES, (tile + 1) * LANES))
            by_row[at] = jnp.maximum(by_row[at], jnp.where(lane == left, row_conf, 0.0))
        by_col[pl.ds(right, 1), :] = jnp.maximum(by_col[pl.ds(right, 1), :], col_conf)

    def plain(p, scores):
        weight = jnp.exp2(scores[...] * (score_scale / math.log(2.0)))
        row_sum = jnp.sum(weight, axis=1, keepdims=True)
        col_sum = jnp.sum(weight, axis=0, keepdims=True)
        least = jnp.minimum(jnp.min(row_sum, axis=0, keepdims=True), jnp.min(col_sum, axis=1, keepdims=True))
        most = jnp.max(col_sum, axis=1, keepdims=True)
        bounds[0] = jnp.minimum(bounds[0], jnp.where(p < total, least, 1.0))
        bounds[1] = jnp.maximum(bounds[1], jnp.where(p < total, most, 1.0))
        row_inv, col_inv = lax.rsqrt(row_sum), lax.rsqrt(col_sum)
        row_top = jnp.max(weight * col_inv, axis=1, keepdims=True) * row_inv
        col_top = jnp.max(weight * row_inv, axis=0, keepdims=True) * col_inv
        record(p, row_top * row_top, col_top * col_top)

    def shifted(p, carry):
        held[0] = product(p) * score_scale
        value = held[0]
        row_peak = jnp.max(value, axis=1, keepdims=True)
        row_total = row_peak + jnp.log(jnp.sum(jnp.exp(value - row_peak), axis=1, keepdims=True))
        col_peak = jnp.max(value, axis=0, keepdims=True)
        col_total = col_peak + jnp.log(jnp.sum(jnp.exp(value - col_peak), axis=0, keepdims=True))
        value = (value - row_total) + (value - col_total)
        record(p, jnp.exp(jnp.max(value, axis=1, keepdims=True)), jnp.exp(jnp.max(value, axis=0, keepdims=True)))
        return carry

    def clear():
        by_row[...] = jnp.zeros_like(by_row)
        by_col[...] = jnp.zeros_like(by_col)

    for place, (source, first) in enumerate(pieces):
        piece = pltpu.make_async_copy(
            sources[source].at[pl.ds(first, deep)], arena.at[pl.ds(place * deep, deep)], sems.at[place]
        )
        pl.when(lists_ref[row, place + 1] > 0)(piece.start)
    clear()
    bounds[...] = jnp.ones_like(bounds)

    def load(first, at, waited):
        needed = 1
        for g in range(GROUP):
            left, right = slots_of(first + g)
            needed = jnp.maximum(needed, lax.div(jnp.maximum(left, right), deep) + 1)
        waited = wait_until(needed, waited)
        for g in range(GROUP):
            held[at * GROUP + g] = product(first + g)
        return waited

    def rounds(k, waited):
        first = 2 * GROUP * k
        for at in range(2):
            waited = load(first + (at + 1) * GROUP, 1 - at, waited)
            for g in range(GROUP):
                plain(first + at * GROUP + g, held.at[at * GROUP + g])
        return waited

    @pl.when(total > 0)
    def all_pairs():
        waited = load(0, 0, jnp.int32(0))
        waited = lax.fori_loop(0, lax.div(total + 2 * GROUP - 1, 2 * GROUP), rounds, waited)
        wait_until(jnp.int32(len(pieces)), waited)

    fine = (jnp.min(bounds[0]) >= SUM_LOW) & (jnp.max(bounds[1]) <= SUM_HIGH)

    @pl.when(jnp.logical_not(fine))
    def again():
        clear()
        lax.fori_loop(0, total, shifted, 0)

    result = jnp.maximum(by_row[...].T, by_col[: by_row.shape[1], :]).astype(jnp.bfloat16)
    out_ref[...] = jnp.maximum(result, before_ref[...])


def confidences(lists, phase, before, sources, pieces, deep, score_scale, work):
    padded, length = before.shape
    width = sources[0].shape[2]
    smem = pl.BlockSpec(memory_space=pltpu.SMEM)
    vmem = pl.BlockSpec(memory_space=pltpu.VMEM)
    return pl.pallas_call(
        functools.partial(kernel, pieces, 3 * phase, score_scale),
        out_shape=jax.ShapeDtypeStruct(before.shape, jnp.bfloat16),
        in_specs=[smem, vmem] + [pl.BlockSpec(memory_space=pl.ANY)] * len(sources),
        out_specs=vmem,
        scratch_shapes=[
            pltpu.VMEM((len(pieces) * deep, length, width), jnp.bfloat16),
            pltpu.VMEM((2 * GROUP, length, length), jnp.float32),
            pltpu.VMEM((length, padded), jnp.float32),
            pltpu.VMEM((padded + 8, length), jnp.float32),
            pltpu.VMEM((2, 1, 1), jnp.float32),
            pltpu.SemaphoreType.DMA((len(pieces),)),
        ],
        compiler_params=pltpu.CompilerParams(vmem_limit_bytes=56 * 1024 * 1024),
        cost_estimate=pl.CostEstimate(flops=work, bytes_accessed=0, transcendentals=0),
    )(lists, before, *sources)


def gather_small_slice(features, pairs, moves, make_lists):
    send = lambda x, name: lax.ppermute(x, "owner", moves[name])
    tie = lax.optimization_barrier
    flat = pairs.reshape(1, -1)
    shift = lambda s: [(i, (i + 4 * s) % 16) for i in range(16)]
    flat = jnp.concatenate([flat] + [lax.ppermute(flat, "owner", shift(s)) for s in (1, 2, 3)])
    own, flat = tie((features, flat))
    near, high = send(own, "near"), send(own, "high")
    flat = jnp.concatenate([flat, send(flat, "side")])
    own, flat = tie((features, flat))
    side, own_swapped = send(own, "side"), send(own, "core")
    flat = jnp.concatenate([flat, send(flat, "core")])
    lists = make_lists(flat.reshape(-1, 2).T)
    half = features.shape[0] // PIECES
    halves = [features[:half], features[half:]]
    near, high, lists, own_swapped, *halves = tie((near, high, lists, own_swapped, *halves))
    far, cross = [send(halves[0], "far")], [send(halves[0], "cross")]
    swapped = [send(x, "core") for x in (near, high)]
    second, swapped[0] = tie((halves[1], swapped[0]))
    far.append(send(second, "far"))
    cross.append(send(second, "cross"))
    swapped.append(send(side, "core"))
    return lists, [features, near, high, side, far, cross, *swapped, [], own_swapped]


def local(features, pairs):
    owners = lax.axis_size("owner")
    views_dev, length, width = features.shape
    flows, phases, table, order = make_plan(owners)
    mine = jnp.asarray(table)[lax.axis_index("owner")]
    if owners == 16:
        make_lists = lambda everyone: quick_lists(everyone, mine, order, views_dev)
        lists, buffers = gather_small_slice(features, pairs, small_slice_moves(), make_lists)
    else:
        everyone = lax.all_gather(pairs, "owner", axis=0, tiled=True)
        buffers = [features] + [lax.ppermute(features, "owner", perm) for _, perm in flows]
        lists = pair_lists(everyone, mine, order, views_dev)
    deep = views_dev // PIECES
    padded = (owners * views_dev + LANES - 1) // LANES * LANES
    best = jnp.zeros((padded, length), jnp.bfloat16)
    for phase, wanted in enumerate(phases):
        if phase > 1:
            *far, best = lax.optimization_barrier((*buffers[4], best))
            buffers[LATE_BUFFER] = [lax.ppermute(x, "owner", small_slice_moves()["core"]) for x in far]
        sources, pieces = [], []
        for k, piece in wanted:
            cut = isinstance(buffers[k], list)
            part = buffers[k][piece] if cut else buffers[k]
            if not any(part is x for x in sources):
                sources.append(part)
            pieces.append(([part is x for x in sources].index(True), 0 if cut else piece * deep))
        best = confidences(lists, phase, best, sources, tuple(pieces), deep, 10.0 / width, 10**8)
    outgoing = best[: owners * views_dev].reshape(owners, views_dev, length)
    returned = lax.all_to_all(outgoing, "owner", split_axis=0, concat_axis=0, tiled=True)
    return jnp.max(returned, axis=0)


def solution(mesh):
    placed = (P(("groups", "owner"), None, None), P(("groups", "owner"), None))
    return jax.shard_map(
        local, mesh=mesh, in_specs=placed, out_specs=P(("groups", "owner"), None), check_vma=False
    )
```

```python
import functools
import math

import jax
import jax.numpy as jnp
import numpy as np
from jax import lax
from jax.experimental import pallas as pl
from jax.experimental.pallas import tpu as pltpu
from jax.sharding import PartitionSpec as P

LANES = 128
SUM_LOW, SUM_HIGH = 1e-28, 1e36


PIECES = 2
GROUP = 2


def small_slice_moves():
    at = lambda z, y, c: (z * 2 + y) * 2 + c
    yc = [(y, c) for y in range(2) for c in range(2)]
    step = lambda z, t: [(at(z, y, c), at(t, y, c)) for y, c in yc]
    return dict(
        near=step(1, 2) + step(0, 1),
        high=step(3, 2) + step(2, 3),
        side=[(at(z, y, c), at(z, 1 - y, c)) for z in range(4) for y, c in yc],
        far=step(0, 2),
        cross=[(at(3, 1 - y, c), at(2, y, c)) for y, c in yc],
        core=[(i, i ^ 1) for i in range(16)],
    )


SMALL_FLOWS = [
    (0, "near"),
    (0, "high"),
    (0, "side"),
    (0, "far"),
    (0, "cross"),
    (1, "core"),
    (2, "core"),
    (3, "core"),
    (4, "core"),
    (0, "core"),
]
LATE_BUFFER = 9
whole = lambda *names: [(k, piece) for k in names for piece in range(PIECES)]
EARLY = whole(0, 10, 3, 2, 1, 6)
SMALL_PHASES = [
    EARLY,
    [(4, 0)] + EARLY + whole(8, 7) + [(5, 0)],
    [(4, 1)] + EARLY + whole(8, 7) + [(5, 0), (5, 1), (4, 0), (9, 0), (9, 1)],
]


def cyclic_distances(owners):
    step = max(1, math.isqrt(owners // 2))
    reach = set(range(step))
    top = step - 1
    while top < owners // 2:
        top += step
        reach.add(top)
    return sorted({d % owners for d in reach} - {0})


@functools.lru_cache(None)
def make_plan(owners):
    if owners == 16:
        moves = small_slice_moves()
        flows = [(source, moves[name]) for source, name in SMALL_FLOWS]
        phases = SMALL_PHASES
    else:
        flows = [(0, [((i + d) % owners, i) for i in range(owners)]) for d in cyclic_distances(owners)]
        phases = [[(k, piece) for k in range(len(flows) + 1) for piece in range(PIECES)]]
    held = [[d] for d in range(owners)]
    for source, perm in flows:
        arrived = {t: held[s][source] for s, t in perm}
        for d in range(owners):
            held[d].append(arrived.get(d, -1))
    first = [{} for _ in range(owners)]
    for d in range(owners):
        for k, o in enumerate(held[d]):
            if o >= 0:
                first[d].setdefault(o, k)
    table = np.zeros((owners, owners, owners), np.int32)
    load = np.zeros(owners)
    choices = []
    for a in range(owners):
        for b in range(a, owners):
            at = [d for d in range(owners) if a in first[d] and b in first[d]]
            assert at
            choices.append((len(at), a, b, at))
    for _, a, b, at in sorted(choices):
        used = lambda d: {first[d][a], first[d][b]}
        late = lambda d: owners == 16 and (2 * (LATE_BUFFER in used(d)) + (1 in used(d) and bool(used(d) & {7, 8})))
        d = min(at, key=lambda d: (late(d), load[d], d))
        load[d] += 1 if a == b else 2
        table[d, a, b] = first[d][a] * 64 + first[d][b] + 1
        table[d, b, a] = first[d][b] * 64 + first[d][a] + 1
    order = np.full((len(phases), (len(flows) + 1) * PIECES), -1, np.int32)
    for phase, pieces in enumerate(phases):
        for place, (k, piece) in enumerate(pieces):
            order[phase, k * PIECES + piece] = place
    return flows, phases, table, order


def pair_lists(pairs, mine, order, views_dev):
    count, owners = pairs.shape[0], mine.shape[0]
    left, right = pairs[:, 0], pairs[:, 1]
    is_left = (left // views_dev)[:, None] == jnp.arange(owners)[None, :]
    is_right = (right // views_dev)[:, None] == jnp.arange(owners)[None, :]
    row = jnp.dot(is_left.astype(jnp.float32), mine.astype(jnp.float32), precision=lax.Precision.HIGHEST)
    found = jnp.sum(jnp.where(is_right, row, 0.0), axis=1).astype(jnp.int32)
    buffers = jnp.maximum(found - 1, 0)
    deep = views_dev // PIECES
    left_piece = (buffers // 64) * PIECES + (left % views_dev) // deep
    right_piece = (buffers % 64) * PIECES + (right % views_dev) // deep
    place = jnp.arange(count)
    free = found > 0
    lists = []
    for phase in range(order.shape[0]):
        where = jnp.asarray(order[phase])[None, :]
        names = jnp.arange(order.shape[1])[None, :]
        left_at = jnp.sum(jnp.where(left_piece[:, None] == names, where, 0), axis=1)
        right_at = jnp.sum(jnp.where(right_piece[:, None] == names, where, 0), axis=1)
        chosen = free & (left_at >= 0) & (right_at >= 0)
        free = free & jnp.logical_not(chosen)
        key = jnp.maximum(left_at, right_at) * count + place
        rank = jnp.sum((key[None, :] < key[:, None]) & chosen[None, :], axis=1)
        picker = (rank[None, :] == place[:, None]) & chosen[None, :]
        slots = (left_at * deep + left % deep) * 1024 + right_at * deep + right % deep
        slots = jnp.sum(jnp.where(picker, slots[None, :], 0), axis=1)
        views = jnp.sum(jnp.where(picker, (left * 1024 + right)[None, :], 0), axis=1)
        used = ((left_at[:, None] == names) | (right_at[:, None] == names)) & chosen[:, None]
        counts = jnp.concatenate([jnp.sum(chosen.astype(jnp.int32)).reshape(1), jnp.any(used, axis=0).astype(jnp.int32)])
        lists += [jnp.pad(counts, (0, count - counts.shape[0])), slots, views]
    return jnp.stack(lists)


def list_kernel(order, views_dev, mine_ref, pairs_ref, out_ref):
    owners, count = mine_ref.shape[0], pairs_ref.shape[1]
    deep = views_dev // PIECES
    far_off = float(2**23)
    place = lax.broadcasted_iota(jnp.int32, (1, count), 1).astype(jnp.float32)
    steps = lambda x, width, most: sum((x >= k * width).astype(jnp.int32) for k in range(1, most))
    left, right = pairs_ref[0:1, :], pairs_ref[1:2, :]
    left_owner, right_owner = steps(left, views_dev, owners), steps(right, views_dev, owners)
    right_is = [right_owner == b for b in range(owners)]
    found = jnp.zeros((1, count), jnp.int32)
    for a in range(owners):
        row = jnp.zeros((1, count), jnp.int32)
        for b in range(owners):
            row = jnp.where(right_is[b], mine_ref[a, b], row)
        found = jnp.where(left_owner == a, row, found)
    buffers = jnp.maximum(found - 1, 0)
    left_view, right_view = left - left_owner * views_dev, right - right_owner * views_dev
    left_part, right_part = steps(left_view, deep, PIECES), steps(right_view, deep, PIECES)
    left_piece = lax.shift_right_logical(buffers, 6) * PIECES + left_part
    right_piece = lax.bitwise_and(buffers, 63) * PIECES + right_part
    column = lambda x: jnp.broadcast_to(x, (LANES, count)).T[:, 0:1]
    views = column((left * 1024 + right).astype(jnp.float32))
    free = found > 0
    for phase, where in enumerate(order):
        left_at, right_at = jnp.full((1, count), -1, jnp.int32), jnp.full((1, count), -1, jnp.int32)
        for name, at in enumerate(where):
            if at >= 0:
                left_at = jnp.where(left_piece == name, at, left_at)
                right_at = jnp.where(right_piece == name, at, right_at)
        chosen = free & (left_at >= 0) & (right_at >= 0)
        free = free & jnp.logical_not(chosen)
        key = jnp.where(chosen, jnp.maximum(left_at, right_at).astype(jnp.float32) * count + place, far_off)
        slots = (left_at * deep + left_view - left_part * deep) * 1024
        slots = (slots + right_at * deep + right_view - right_part * deep).astype(jnp.float32)
        own_key = column(key)
        rank = jnp.sum(jnp.where(key < own_key, 1.0, 0.0), axis=1, keepdims=True)
        rank = jnp.where(own_key < far_off, rank, -1.0)
        hit = rank == place
        out_ref[3 * phase + 1 : 3 * phase + 2, :] = jnp.sum(jnp.where(hit, column(slots), 0.0), axis=0, keepdims=True).astype(jnp.int32)
        out_ref[3 * phase + 2 : 3 * phase + 3, :] = jnp.sum(jnp.where(hit, views, 0.0), axis=0, keepdims=True).astype(jnp.int32)
        picked = jnp.where(chosen, 1.0, 0.0)
        lane = lax.broadcasted_iota(jnp.int32, (1, LANES), 1)
        counts = jnp.where(lane == 0, jnp.sum(picked, axis=1, keepdims=True), 0.0)
        for at in range(sum(x >= 0 for x in where)):
            uses = jnp.where((left_at == at) | (right_at == at), picked, 0.0)
            counts = jnp.where(lane == at + 1, jnp.max(uses, axis=1, keepdims=True), counts)
        out_ref[3 * phase : 3 * phase + 1, 0:LANES] = counts.astype(jnp.int32)


def quick_lists(pairs, mine, order, views_dev):
    count = pairs.shape[1]
    vmem = pl.BlockSpec(memory_space=pltpu.VMEM)
    return pl.pallas_call(
        functools.partial(list_kernel, order.tolist(), views_dev),
        out_shape=jax.ShapeDtypeStruct((3 * len(order), count), jnp.int32),
        in_specs=[pl.BlockSpec(memory_space=pltpu.SMEM), vmem],
        out_specs=vmem,
        compiler_params=pltpu.CompilerParams(vmem_limit_bytes=32 * 1024 * 1024),
        cost_estimate=pl.CostEstimate(flops=1, bytes_accessed=0, transcendentals=0),
    )(mine, pairs)


def kernel(pieces, row, score_scale, lists_ref, before_ref, *refs):
    sources = refs[:-7]
    out_ref, arena, held, by_row, by_col, bounds, sems = refs[-7:]
    length = arena.shape[1]
    deep = arena.shape[0] // len(pieces)
    total = lists_ref[row, 0]
    limit = lists_ref.shape[1] - 1

    def slots_of(p):
        packed = lists_ref[row + 1, jnp.minimum(p, limit)]
        return lax.shift_right_logical(packed, 10), lax.bitwise_and(packed, 1023)

    def wait_until(needed, waited):
        def wait(k, carry):
            part = arena.at[pl.ds(0, deep)]
            pl.when(lists_ref[row, k + 1] > 0)(lambda: pltpu.make_async_copy(part, part, sems.at[k]).wait())
            return carry

        lax.fori_loop(waited, needed, wait, 0)
        return jnp.maximum(waited, needed)

    def product(p):
        left, right = slots_of(p)
        return lax.dot_general(
            arena[left], arena[right], (((1,), (1,)), ((), ())), preferred_element_type=jnp.float32
        )

    def record(p, row_conf, col_conf):
        packed = lists_ref[row + 2, jnp.minimum(p, limit)]
        real = p < total
        left = jnp.where(real, lax.shift_right_logical(packed, 10), -1)
        right = jnp.where(real, lax.bitwise_and(packed, 1023), by_row.shape[1])
        for tile in range(by_row.shape[1] // LANES):
            lane = lax.broadcasted_iota(jnp.int32, (length, LANES), 1) + tile * LANES
            at = (slice(None), slice(tile * LANES, (tile + 1) * LANES))
            by_row[at] = jnp.maximum(by_row[at], jnp.where(lane == left, row_conf, 0.0))
        by_col[pl.ds(right, 1), :] = jnp.maximum(by_col[pl.ds(right, 1), :], col_conf)

    def plain(p, scores):
        weight = jnp.exp2(scores[...] * (score_scale / math.log(2.0)))
        row_sum = jnp.sum(weight, axis=1, keepdims=True)
        col_sum = jnp.sum(weight, axis=0, keepdims=True)
        least = jnp.minimum(jnp.min(row_sum, axis=0, keepdims=True), jnp.min(col_sum, axis=1, keepdims=True))
        most = jnp.maximum(jnp.max(row_sum, axis=0, keepdims=True), jnp.max(col_sum, axis=1, keepdims=True))
        bounds[0] = jnp.minimum(bounds[0], jnp.where(p < total, least, 1.0))
        bounds[1] = jnp.maximum(bounds[1], jnp.where(p < total, most, 1.0))
        row_inv, col_inv = lax.rsqrt(row_sum), lax.rsqrt(col_sum)
        row_top = jnp.max(weight * col_inv, axis=1, keepdims=True) * row_inv
        col_top = jnp.max(weight * row_inv, axis=0, keepdims=True) * col_inv
        record(p, row_top * row_top, col_top * col_top)

    def shifted(p, carry):
        held[0] = product(p) * score_scale
        value = held[0]
        row_peak = jnp.max(value, axis=1, keepdims=True)
        row_total = row_peak + jnp.log(jnp.sum(jnp.exp(value - row_peak), axis=1, keepdims=True))
        col_peak = jnp.max(value, axis=0, keepdims=True)
        col_total = col_peak + jnp.log(jnp.sum(jnp.exp(value - col_peak), axis=0, keepdims=True))
        value = (value - row_total) + (value - col_total)
        record(p, jnp.exp(jnp.max(value, axis=1, keepdims=True)), jnp.exp(jnp.max(value, axis=0, keepdims=True)))
        return carry

    def clear():
        by_row[...] = jnp.zeros_like(by_row)
        by_col[...] = jnp.zeros_like(by_col)

    for place, (source, first) in enumerate(pieces):
        piece = pltpu.make_async_copy(
            sources[source].at[pl.ds(first, deep)], arena.at[pl.ds(place * deep, deep)], sems.at[place]
        )
        pl.when(lists_ref[row, place + 1] > 0)(piece.start)
    clear()
    bounds[...] = jnp.ones_like(bounds)

    def load(first, at, waited):
        needed = 1
        for g in range(GROUP):
            left, right = slots_of(first + g)
            needed = jnp.maximum(needed, lax.div(jnp.maximum(left, right), deep) + 1)
        waited = wait_until(needed, waited)
        for g in range(GROUP):
            held[at * GROUP + g] = product(first + g)
        return waited

    def rounds(k, waited):
        first = 2 * GROUP * k
        for at in range(2):
            waited = load(first + (at + 1) * GROUP, 1 - at, waited)
            for g in range(GROUP):
                plain(first + at * GROUP + g, held.at[at * GROUP + g])
        return waited

    @pl.when(total > 0)
    def all_pairs():
        waited = load(0, 0, jnp.int32(0))
        waited = lax.fori_loop(0, lax.div(total + 2 * GROUP - 1, 2 * GROUP), rounds, waited)
        wait_until(jnp.int32(len(pieces)), waited)

    fine = (jnp.min(bounds[0]) >= SUM_LOW) & (jnp.max(bounds[1]) <= SUM_HIGH)

    @pl.when(jnp.logical_not(fine))
    def again():
        clear()
        lax.fori_loop(0, total, shifted, 0)

    result = jnp.maximum(by_row[...].T, by_col[: by_row.shape[1], :]).astype(jnp.bfloat16)
    out_ref[...] = jnp.maximum(result, before_ref[...])


def confidences(lists, phase, before, sources, pieces, deep, score_scale, work):
    padded, length = before.shape
    width = sources[0].shape[2]
    smem = pl.BlockSpec(memory_space=pltpu.SMEM)
    vmem = pl.BlockSpec(memory_space=pltpu.VMEM)
    return pl.pallas_call(
        functools.partial(kernel, pieces, 3 * phase, score_scale),
        out_shape=jax.ShapeDtypeStruct(before.shape, jnp.bfloat16),
        in_specs=[smem, vmem] + [pl.BlockSpec(memory_space=pl.ANY)] * len(sources),
        out_specs=vmem,
        scratch_shapes=[
            pltpu.VMEM((len(pieces) * deep, length, width), jnp.bfloat16),
            pltpu.VMEM((2 * GROUP, length, length), jnp.float32),
            pltpu.VMEM((length, padded), jnp.float32),
            pltpu.VMEM((padded + 8, length), jnp.float32),
            pltpu.VMEM((2, 1, 1), jnp.float32),
            pltpu.SemaphoreType.DMA((len(pieces),)),
        ],
        compiler_params=pltpu.CompilerParams(vmem_limit_bytes=56 * 1024 * 1024),
        cost_estimate=pl.CostEstimate(flops=work, bytes_accessed=0, transcendentals=0),
    )(lists, before, *sources)


def gather_small_slice(features, pairs, moves, make_lists):
    send = lambda x, name: lax.ppermute(x, "owner", moves[name])
    tie = lax.optimization_barrier
    flat = pairs.T.reshape(1, -1)
    shift = lambda s: [(i, (i + 4 * s) % 16) for i in range(16)]
    flat = jnp.concatenate([flat] + [lax.ppermute(flat, "owner", shift(s)) for s in (1, 2, 3)])
    own, flat = tie((features, flat))
    near, high = send(own, "near"), send(own, "high")
    flat = jnp.concatenate([flat, send(flat, "side")])
    own, flat = tie((features, flat))
    side = send(own, "side")
    flat = jnp.concatenate([flat, send(flat, "core")])
    lists = make_lists(flat.reshape(16, 2, -1).transpose(1, 0, 2).reshape(2, -1))
    half = features.shape[0] // PIECES
    halves = [features[:half], features[half:]]
    own_swapped = send(features, "core")
    near, high, lists, own_swapped, *halves = tie((near, high, lists, own_swapped, *halves))
    far, cross = [send(halves[0], "far")], [send(halves[0], "cross")]
    swapped = [send(x, "core") for x in (near, high)]
    second, swapped[0] = tie((halves[1], swapped[0]))
    far.append(send(second, "far"))
    cross.append(send(second, "cross"))
    swapped.append(send(side, "core"))
    return lists, [features, near, high, side, far, cross, *swapped, [], own_swapped]


def local(features, pairs):
    owners = lax.axis_size("owner")
    views_dev, length, width = features.shape
    flows, phases, table, order = make_plan(owners)
    mine = jnp.asarray(table)[lax.axis_index("owner")]
    if owners == 16:
        make_lists = lambda everyone: quick_lists(everyone, mine, order, views_dev)
        lists, buffers = gather_small_slice(features, pairs, small_slice_moves(), make_lists)
    else:
        everyone = lax.all_gather(pairs, "owner", axis=0, tiled=True)
        buffers = [features] + [lax.ppermute(features, "owner", perm) for _, perm in flows]
        lists = pair_lists(everyone, mine, order, views_dev)
    deep = views_dev // PIECES
    padded = (owners * views_dev + LANES - 1) // LANES * LANES
    best = jnp.zeros((padded, length), jnp.bfloat16)
    for phase, wanted in enumerate(phases):
        if phase > 1:
            *far, best = lax.optimization_barrier((*buffers[4], best))
            buffers[LATE_BUFFER] = [lax.ppermute(x, "owner", small_slice_moves()["core"]) for x in far]
        sources, pieces = [], []
        for k, piece in wanted:
            cut = isinstance(buffers[k], list)
            part = buffers[k][piece] if cut else buffers[k]
            if not any(part is x for x in sources):
                sources.append(part)
            pieces.append(([part is x for x in sources].index(True), 0 if cut else piece * deep))
        best = confidences(lists, phase, best, sources, tuple(pieces), deep, 10.0 / width, 10**8)
    outgoing = best[: owners * views_dev].reshape(owners, views_dev, length)
    returned = lax.all_to_all(outgoing, "owner", split_axis=0, concat_axis=0, tiled=True)
    return jnp.max(returned, axis=0)


def solution(mesh):
    placed = (P(("groups", "owner"), None, None), P(("groups", "owner"), None))
    return jax.shard_map(
        local, mesh=mesh, in_specs=placed, out_specs=P(("groups", "owner"), None), check_vma=False
    )
```

```python
import functools
import math

import jax
import jax.numpy as jnp
import numpy as np
from jax import lax
from jax.experimental import pallas as pl
from jax.experimental.pallas import tpu as pltpu
from jax.sharding import PartitionSpec as P

LANES = 128
SUM_LOW, SUM_HIGH = 1e-28, 1e36


PIECES = 2
GROUP = 2


def small_slice_moves():
    at = lambda z, y, c: (z * 2 + y) * 2 + c
    yc = [(y, c) for y in range(2) for c in range(2)]
    step = lambda z, t: [(at(z, y, c), at(t, y, c)) for y, c in yc]
    return dict(
        near=step(1, 2) + step(0, 1),
        high=step(3, 2) + step(2, 3),
        side=[(at(z, y, c), at(z, 1 - y, c)) for z in range(4) for y, c in yc],
        far=step(0, 2),
        cross=[(at(3, 1 - y, c), at(2, y, c)) for y, c in yc],
        core=[(i, i ^ 1) for i in range(16)],
    )


SMALL_FLOWS = [
    (0, "near"),
    (0, "high"),
    (0, "side"),
    (0, "far"),
    (0, "cross"),
    (1, "core"),
    (2, "core"),
    (3, "core"),
    (4, "core"),
    (0, "core"),
]
LATE_BUFFER = 9
EARLY = [(k, piece) for k in (0, 10, 3, 8, 2, 7, 1, 6) for piece in range(PIECES)]
SMALL_PHASES = [
    EARLY,
    [(4, 0)] + EARLY + [(5, 0)],
    [(4, 1)] + EARLY + [(5, 0), (5, 1), (4, 0), (9, 0), (9, 1)],
]


def cyclic_distances(owners):
    step = max(1, math.isqrt(owners // 2))
    reach = set(range(step))
    top = step - 1
    while top < owners // 2:
        top += step
        reach.add(top)
    return sorted({d % owners for d in reach} - {0})


@functools.lru_cache(None)
def make_plan(owners):
    if owners == 16:
        moves = small_slice_moves()
        flows = [(source, moves[name]) for source, name in SMALL_FLOWS]
        phases = SMALL_PHASES
    else:
        flows = [(0, [((i + d) % owners, i) for i in range(owners)]) for d in cyclic_distances(owners)]
        phases = [[(k, piece) for k in range(len(flows) + 1) for piece in range(PIECES)]]
    held = [[d] for d in range(owners)]
    for source, perm in flows:
        arrived = {t: held[s][source] for s, t in perm}
        for d in range(owners):
            held[d].append(arrived.get(d, -1))
    first = [{} for _ in range(owners)]
    for d in range(owners):
        for k, o in enumerate(held[d]):
            if o >= 0:
                first[d].setdefault(o, k)
    table = np.zeros((owners, owners, owners), np.int32)
    load = np.zeros(owners)
    choices = []
    for a in range(owners):
        for b in range(a, owners):
            at = [d for d in range(owners) if a in first[d] and b in first[d]]
            assert at
            choices.append((len(at), a, b, at))
    for _, a, b, at in sorted(choices):
        late = lambda d: owners == 16 and LATE_BUFFER in (first[d][a], first[d][b])
        d = min(at, key=lambda d: (late(d), load[d], d))
        load[d] += 1 if a == b else 2
        table[d, a, b] = first[d][a] * 64 + first[d][b] + 1
        table[d, b, a] = first[d][b] * 64 + first[d][a] + 1
    order = np.full((len(phases), (len(flows) + 1) * PIECES), -1, np.int32)
    for phase, pieces in enumerate(phases):
        for place, (k, piece) in enumerate(pieces):
            order[phase, k * PIECES + piece] = place
    return flows, phases, table, order


def pair_lists(pairs, mine, order, views_dev):
    count, owners = pairs.shape[0], mine.shape[0]
    left, right = pairs[:, 0], pairs[:, 1]
    is_left = (left // views_dev)[:, None] == jnp.arange(owners)[None, :]
    is_right = (right // views_dev)[:, None] == jnp.arange(owners)[None, :]
    row = jnp.dot(is_left.astype(jnp.float32), mine.astype(jnp.float32), precision=lax.Precision.HIGHEST)
    found = jnp.sum(jnp.where(is_right, row, 0.0), axis=1).astype(jnp.int32)
    buffers = jnp.maximum(found - 1, 0)
    deep = views_dev // PIECES
    left_piece = (buffers // 64) * PIECES + (left % views_dev) // deep
    right_piece = (buffers % 64) * PIECES + (right % views_dev) // deep
    place = jnp.arange(count)
    free = found > 0
    lists = []
    for phase in range(order.shape[0]):
        where = jnp.asarray(order[phase])[None, :]
        names = jnp.arange(order.shape[1])[None, :]
        left_at = jnp.sum(jnp.where(left_piece[:, None] == names, where, 0), axis=1)
        right_at = jnp.sum(jnp.where(right_piece[:, None] == names, where, 0), axis=1)
        chosen = free & (left_at >= 0) & (right_at >= 0)
        free = free & jnp.logical_not(chosen)
        key = jnp.maximum(left_at, right_at) * count + place
        rank = jnp.sum((key[None, :] < key[:, None]) & chosen[None, :], axis=1)
        picker = (rank[None, :] == place[:, None]) & chosen[None, :]
        slots = (left_at * deep + left % deep) * 1024 + right_at * deep + right % deep
        slots = jnp.sum(jnp.where(picker, slots[None, :], 0), axis=1)
        views = jnp.sum(jnp.where(picker, (left * 1024 + right)[None, :], 0), axis=1)
        used = ((left_at[:, None] == names) | (right_at[:, None] == names)) & chosen[:, None]
        counts = jnp.concatenate([jnp.sum(chosen.astype(jnp.int32)).reshape(1), jnp.any(used, axis=0).astype(jnp.int32)])
        lists += [jnp.pad(counts, (0, count - counts.shape[0])), slots, views]
    return jnp.stack(lists)


def list_kernel(order, views_dev, mine_ref, pairs_ref, out_ref):
    owners, count = mine_ref.shape[0], pairs_ref.shape[1]
    deep = views_dev // PIECES
    far_off = float(2**23)
    place = lax.broadcasted_iota(jnp.int32, (1, count), 1).astype(jnp.float32)
    steps = lambda x, width, most: sum((x >= k * width).astype(jnp.int32) for k in range(1, most))
    left, right = pairs_ref[0:1, :], pairs_ref[1:2, :]
    left_owner, right_owner = steps(left, views_dev, owners), steps(right, views_dev, owners)
    right_is = [right_owner == b for b in range(owners)]
    found = jnp.zeros((1, count), jnp.int32)
    for a in range(owners):
        row = jnp.zeros((1, count), jnp.int32)
        for b in range(owners):
            row = jnp.where(right_is[b], mine_ref[a, b], row)
        found = jnp.where(left_owner == a, row, found)
    buffers = jnp.maximum(found - 1, 0)
    left_view, right_view = left - left_owner * views_dev, right - right_owner * views_dev
    left_part, right_part = steps(left_view, deep, PIECES), steps(right_view, deep, PIECES)
    left_piece = lax.shift_right_logical(buffers, 6) * PIECES + left_part
    right_piece = lax.bitwise_and(buffers, 63) * PIECES + right_part
    column = lambda x: jnp.broadcast_to(x, (LANES, count)).T[:, 0:1]
    views = column((left * 1024 + right).astype(jnp.float32))
    free = found > 0
    for phase, where in enumerate(order):
        left_at, right_at = jnp.full((1, count), -1, jnp.int32), jnp.full((1, count), -1, jnp.int32)
        for name, at in enumerate(where):
            if at >= 0:
                left_at = jnp.where(left_piece == name, at, left_at)
                right_at = jnp.where(right_piece == name, at, right_at)
        chosen = free & (left_at >= 0) & (right_at >= 0)
        free = free & jnp.logical_not(chosen)
        key = jnp.where(chosen, jnp.maximum(left_at, right_at).astype(jnp.float32) * count + place, far_off)
        slots = (left_at * deep + left_view - left_part * deep) * 1024
        slots = (slots + right_at * deep + right_view - right_part * deep).astype(jnp.float32)
        own_key = column(key)
        rank = jnp.sum(jnp.where(key < own_key, 1.0, 0.0), axis=1, keepdims=True)
        rank = jnp.where(own_key < far_off, rank, -1.0)
        hit = rank == place
        out_ref[3 * phase + 1 : 3 * phase + 2, :] = jnp.sum(jnp.where(hit, column(slots), 0.0), axis=0, keepdims=True).astype(jnp.int32)
        out_ref[3 * phase + 2 : 3 * phase + 3, :] = jnp.sum(jnp.where(hit, views, 0.0), axis=0, keepdims=True).astype(jnp.int32)
        picked = jnp.where(chosen, 1.0, 0.0)
        lane = lax.broadcasted_iota(jnp.int32, (1, LANES), 1)
        counts = jnp.where(lane == 0, jnp.sum(picked, axis=1, keepdims=True), 0.0)
        for at in range(sum(x >= 0 for x in where)):
            uses = jnp.where((left_at == at) | (right_at == at), picked, 0.0)
            counts = jnp.where(lane == at + 1, jnp.max(uses, axis=1, keepdims=True), counts)
        out_ref[3 * phase : 3 * phase + 1, 0:LANES] = counts.astype(jnp.int32)


def quick_lists(pairs, mine, order, views_dev):
    count = pairs.shape[1]
    vmem = pl.BlockSpec(memory_space=pltpu.VMEM)
    return pl.pallas_call(
        functools.partial(list_kernel, order.tolist(), views_dev),
        out_shape=jax.ShapeDtypeStruct((3 * len(order), count), jnp.int32),
        in_specs=[pl.BlockSpec(memory_space=pltpu.SMEM), vmem],
        out_specs=vmem,
        compiler_params=pltpu.CompilerParams(vmem_limit_bytes=32 * 1024 * 1024),
        cost_estimate=pl.CostEstimate(flops=1, bytes_accessed=0, transcendentals=0),
    )(mine, pairs)


def kernel(pieces, row, score_scale, lists_ref, before_ref, *refs):
    sources = refs[:-7]
    out_ref, arena, held, by_row, by_col, bounds, sems = refs[-7:]
    length = arena.shape[1]
    deep = arena.shape[0] // len(pieces)
    total = lists_ref[row, 0]
    limit = lists_ref.shape[1] - 1

    def slots_of(p):
        packed = lists_ref[row + 1, jnp.minimum(p, limit)]
        return lax.shift_right_logical(packed, 10), lax.bitwise_and(packed, 1023)

    def wait_until(needed, waited):
        def wait(k, carry):
            part = arena.at[pl.ds(0, deep)]
            pl.when(lists_ref[row, k + 1] > 0)(lambda: pltpu.make_async_copy(part, part, sems.at[k]).wait())
            return carry

        lax.fori_loop(waited, needed, wait, 0)
        return jnp.maximum(waited, needed)

    def product(p):
        left, right = slots_of(p)
        return lax.dot_general(
            arena[left], arena[right], (((1,), (1,)), ((), ())), preferred_element_type=jnp.float32
        )

    def record(p, row_conf, col_conf):
        packed = lists_ref[row + 2, jnp.minimum(p, limit)]
        real = p < total
        left = jnp.where(real, lax.shift_right_logical(packed, 10), -1)
        right = jnp.where(real, lax.bitwise_and(packed, 1023), by_row.shape[1])
        for tile in range(by_row.shape[1] // LANES):
            lane = lax.broadcasted_iota(jnp.int32, (length, LANES), 1) + tile * LANES
            at = (slice(None), slice(tile * LANES, (tile + 1) * LANES))
            by_row[at] = jnp.maximum(by_row[at], jnp.where(lane == left, row_conf, 0.0))
        by_col[pl.ds(right, 1), :] = jnp.maximum(by_col[pl.ds(right, 1), :], col_conf)

    def plain(p, scores):
        weight = jnp.exp2(scores[...] * (score_scale / math.log(2.0)))
        row_sum = jnp.sum(weight, axis=1, keepdims=True)
        col_sum = jnp.sum(weight, axis=0, keepdims=True)
        least = jnp.minimum(jnp.min(row_sum, axis=0, keepdims=True), jnp.min(col_sum, axis=1, keepdims=True))
        most = jnp.maximum(jnp.max(row_sum, axis=0, keepdims=True), jnp.max(col_sum, axis=1, keepdims=True))
        bounds[0] = jnp.minimum(bounds[0], jnp.where(p < total, least, 1.0))
        bounds[1] = jnp.maximum(bounds[1], jnp.where(p < total, most, 1.0))
        row_inv, col_inv = lax.rsqrt(row_sum), lax.rsqrt(col_sum)
        row_top = jnp.max(weight * col_inv, axis=1, keepdims=True) * row_inv
        col_top = jnp.max(weight * row_inv, axis=0, keepdims=True) * col_inv
        record(p, row_top * row_top, col_top * col_top)

    def shifted(p, carry):
        held[0] = product(p) * score_scale
        value = held[0]
        row_peak = jnp.max(value, axis=1, keepdims=True)
        row_total = row_peak + jnp.log(jnp.sum(jnp.exp(value - row_peak), axis=1, keepdims=True))
        col_peak = jnp.max(value, axis=0, keepdims=True)
        col_total = col_peak + jnp.log(jnp.sum(jnp.exp(value - col_peak), axis=0, keepdims=True))
        value = (value - row_total) + (value - col_total)
        record(p, jnp.exp(jnp.max(value, axis=1, keepdims=True)), jnp.exp(jnp.max(value, axis=0, keepdims=True)))
        return carry

    def clear():
        by_row[...] = jnp.zeros_like(by_row)
        by_col[...] = jnp.zeros_like(by_col)

    for place, (source, first) in enumerate(pieces):
        piece = pltpu.make_async_copy(
            sources[source].at[pl.ds(first, deep)], arena.at[pl.ds(place * deep, deep)], sems.at[place]
        )
        pl.when(lists_ref[row, place + 1] > 0)(piece.start)
    clear()
    bounds[...] = jnp.ones_like(bounds)

    def load(first, at, waited):
        needed = 1
        for g in range(GROUP):
            left, right = slots_of(first + g)
            needed = jnp.maximum(needed, lax.div(jnp.maximum(left, right), deep) + 1)
        waited = wait_until(needed, waited)
        for g in range(GROUP):
            held[at * GROUP + g] = product(first + g)
        return waited

    def rounds(k, waited):
        first = 2 * GROUP * k
        for at in range(2):
            waited = load(first + (at + 1) * GROUP, 1 - at, waited)
            for g in range(GROUP):
                plain(first + at * GROUP + g, held.at[at * GROUP + g])
        return waited

    @pl.when(total > 0)
    def all_pairs():
        waited = load(0, 0, jnp.int32(0))
        waited = lax.fori_loop(0, lax.div(total + 2 * GROUP - 1, 2 * GROUP), rounds, waited)
        wait_until(jnp.int32(len(pieces)), waited)

    fine = (jnp.min(bounds[0]) >= SUM_LOW) & (jnp.max(bounds[1]) <= SUM_HIGH)

    @pl.when(jnp.logical_not(fine))
    def again():
        clear()
        lax.fori_loop(0, total, shifted, 0)

    result = jnp.maximum(by_row[...].T, by_col[: by_row.shape[1], :]).astype(jnp.bfloat16)
    out_ref[...] = jnp.maximum(result, before_ref[...])


def confidences(lists, phase, before, sources, pieces, deep, score_scale, work):
    padded, length = before.shape
    width = sources[0].shape[2]
    smem = pl.BlockSpec(memory_space=pltpu.SMEM)
    vmem = pl.BlockSpec(memory_space=pltpu.VMEM)
    return pl.pallas_call(
        functools.partial(kernel, pieces, 3 * phase, score_scale),
        out_shape=jax.ShapeDtypeStruct(before.shape, jnp.bfloat16),
        in_specs=[smem, vmem] + [pl.BlockSpec(memory_space=pl.ANY)] * len(sources),
        out_specs=vmem,
        scratch_shapes=[
            pltpu.VMEM((len(pieces) * deep, length, width), jnp.bfloat16),
            pltpu.VMEM((2 * GROUP, length, length), jnp.float32),
            pltpu.VMEM((length, padded), jnp.float32),
            pltpu.VMEM((padded + 8, length), jnp.float32),
            pltpu.VMEM((2, 1, 1), jnp.float32),
            pltpu.SemaphoreType.DMA((len(pieces),)),
        ],
        compiler_params=pltpu.CompilerParams(vmem_limit_bytes=56 * 1024 * 1024),
        cost_estimate=pl.CostEstimate(flops=work, bytes_accessed=0, transcendentals=0),
    )(lists, before, *sources)


def gather_small_slice(features, pairs, moves, make_lists):
    send = lambda x, name: lax.ppermute(x, "owner", moves[name])
    tie = lax.optimization_barrier
    flat = pairs.T.reshape(1, -1)
    shift = lambda s: [(i, (i + 4 * s) % 16) for i in range(16)]
    flat = jnp.concatenate([flat] + [lax.ppermute(flat, "owner", shift(s)) for s in (1, 2, 3)])
    own, flat = tie((features, flat))
    near, high = send(own, "near"), send(own, "high")
    flat = jnp.concatenate([flat, send(flat, "side")])
    own, flat = tie((features, flat))
    side = send(own, "side")
    flat = jnp.concatenate([flat, send(flat, "core")])
    lists = make_lists(flat.reshape(16, 2, -1).transpose(1, 0, 2).reshape(2, -1))
    half = features.shape[0] // PIECES
    halves = [features[:half], features[half:]]
    own_swapped = send(features, "core")
    near, high, lists, own_swapped, *halves = tie((near, high, lists, own_swapped, *halves))
    far, cross = [send(halves[0], "far")], [send(halves[0], "cross")]
    swapped = [send(x, "core") for x in (near, high)]
    second, swapped[0] = tie((halves[1], swapped[0]))
    far.append(send(second, "far"))
    cross.append(send(second, "cross"))
    swapped.append(send(side, "core"))
    return lists, [features, near, high, side, far, cross, *swapped, [], own_swapped]


def local(features, pairs):
    owners = lax.axis_size("owner")
    views_dev, length, width = features.shape
    flows, phases, table, order = make_plan(owners)
    mine = jnp.asarray(table)[lax.axis_index("owner")]
    if owners == 16:
        make_lists = lambda everyone: quick_lists(everyone, mine, order, views_dev)
        lists, buffers = gather_small_slice(features, pairs, small_slice_moves(), make_lists)
    else:
        everyone = lax.all_gather(pairs, "owner", axis=0, tiled=True)
        buffers = [features] + [lax.ppermute(features, "owner", perm) for _, perm in flows]
        lists = pair_lists(everyone, mine, order, views_dev)
    deep = views_dev // PIECES
    padded = (owners * views_dev + LANES - 1) // LANES * LANES
    best = jnp.zeros((padded, length), jnp.bfloat16)
    for phase, wanted in enumerate(phases):
        if phase > 0:
            far, best = lax.optimization_barrier((buffers[4][phase - 1], best))
            buffers[LATE_BUFFER].append(lax.ppermute(far, "owner", small_slice_moves()["core"]))
        sources, pieces = [], []
        for k, piece in wanted:
            cut = isinstance(buffers[k], list)
            part = buffers[k][piece] if cut else buffers[k]
            if not any(part is x for x in sources):
                sources.append(part)
            pieces.append(([part is x for x in sources].index(True), 0 if cut else piece * deep))
        best = confidences(lists, phase, best, sources, tuple(pieces), deep, 10.0 / width, 10**8)
    outgoing = best[: owners * views_dev].reshape(owners, views_dev, length)
    returned = lax.all_to_all(outgoing, "owner", split_axis=0, concat_axis=0, tiled=True)
    return jnp.max(returned, axis=0)


def solution(mesh):
    placed = (P(("groups", "owner"), None, None), P(("groups", "owner"), None))
    return jax.shard_map(
        local, mesh=mesh, in_specs=placed, out_specs=P(("groups", "owner"), None), check_vma=False
    )
```

```python
import functools
import math

import jax
import jax.numpy as jnp
import numpy as np
from jax import lax
from jax.experimental import pallas as pl
from jax.experimental.pallas import tpu as pltpu
from jax.sharding import PartitionSpec as P

LANES = 128
SUM_LOW, SUM_HIGH = 1e-28, 1e35


PIECES = 2
GROUP = 2


def small_slice_moves():
    at = lambda z, y, c: (z * 2 + y) * 2 + c
    yc = [(y, c) for y in range(2) for c in range(2)]
    step = lambda z, t: [(at(z, y, c), at(t, y, c)) for y, c in yc]
    return dict(
        near=step(1, 2) + step(0, 1),
        high=step(3, 2) + step(2, 3),
        side=[(at(z, y, c), at(z, 1 - y, c)) for z in range(4) for y, c in yc],
        far=step(0, 2),
        cross=[(at(3, 1 - y, c), at(2, y, c)) for y, c in yc],
        core=[(i, i ^ 1) for i in range(16)],
    )


SMALL_FLOWS = [
    (0, "near"),
    (0, "high"),
    (0, "side"),
    (0, "far"),
    (0, "cross"),
    (1, "core"),
    (2, "core"),
    (3, "core"),
    (4, "core"),
    (0, "core"),
]
LATE_BUFFER = 9
EARLY = [(k, piece) for k in (0, 10, 3, 8, 2, 7, 1, 6) for piece in range(PIECES)]
SMALL_PHASES = [
    EARLY,
    [(4, 0)] + EARLY + [(5, 0)],
    [(4, 1)] + EARLY + [(5, 0), (5, 1), (4, 0), (9, 0), (9, 1)],
]


def cyclic_distances(owners):
    step = max(1, math.isqrt(owners // 2))
    reach = set(range(step))
    top = step - 1
    while top < owners // 2:
        top += step
        reach.add(top)
    return sorted({d % owners for d in reach} - {0})


@functools.lru_cache(None)
def make_plan(owners):
    if owners == 16:
        moves = small_slice_moves()
        flows = [(source, moves[name]) for source, name in SMALL_FLOWS]
        phases = SMALL_PHASES
    else:
        flows = [(0, [((i + d) % owners, i) for i in range(owners)]) for d in cyclic_distances(owners)]
        phases = [[(k, piece) for k in range(len(flows) + 1) for piece in range(PIECES)]]
    held = [[d] for d in range(owners)]
    for source, perm in flows:
        arrived = {t: held[s][source] for s, t in perm}
        for d in range(owners):
            held[d].append(arrived.get(d, -1))
    first = [{} for _ in range(owners)]
    for d in range(owners):
        for k, o in enumerate(held[d]):
            if o >= 0:
                first[d].setdefault(o, k)
    table = np.zeros((owners, owners, owners), np.int32)
    load = np.zeros(owners)
    choices = []
    for a in range(owners):
        for b in range(a, owners):
            at = [d for d in range(owners) if a in first[d] and b in first[d]]
            assert at
            choices.append((len(at), a, b, at))
    for _, a, b, at in sorted(choices):
        late = lambda d: owners == 16 and LATE_BUFFER in (first[d][a], first[d][b])
        d = min(at, key=lambda d: (late(d), load[d], d))
        load[d] += 1 if a == b else 2
        table[d, a, b] = first[d][a] * 64 + first[d][b] + 1
        table[d, b, a] = first[d][b] * 64 + first[d][a] + 1
    order = np.full((len(phases), (len(flows) + 1) * PIECES), -1, np.int32)
    for phase, pieces in enumerate(phases):
        for place, (k, piece) in enumerate(pieces):
            order[phase, k * PIECES + piece] = place
    return flows, phases, table, order


def pair_lists(pairs, mine, order, views_dev):
    count, owners = pairs.shape[0], mine.shape[0]
    left, right = pairs[:, 0], pairs[:, 1]
    is_left = (left // views_dev)[:, None] == jnp.arange(owners)[None, :]
    is_right = (right // views_dev)[:, None] == jnp.arange(owners)[None, :]
    row = jnp.dot(is_left.astype(jnp.float32), mine.astype(jnp.float32), precision=lax.Precision.HIGHEST)
    found = jnp.sum(jnp.where(is_right, row, 0.0), axis=1).astype(jnp.int32)
    buffers = jnp.maximum(found - 1, 0)
    deep = views_dev // PIECES
    left_piece = (buffers // 64) * PIECES + (left % views_dev) // deep
    right_piece = (buffers % 64) * PIECES + (right % views_dev) // deep
    place = jnp.arange(count)
    free = found > 0
    lists = []
    for phase in range(order.shape[0]):
        where = jnp.asarray(order[phase])[None, :]
        names = jnp.arange(order.shape[1])[None, :]
        left_at = jnp.sum(jnp.where(left_piece[:, None] == names, where, 0), axis=1)
        right_at = jnp.sum(jnp.where(right_piece[:, None] == names, where, 0), axis=1)
        chosen = free & (left_at >= 0) & (right_at >= 0)
        free = free & jnp.logical_not(chosen)
        key = jnp.maximum(left_at, right_at) * count + place
        rank = jnp.sum((key[None, :] < key[:, None]) & chosen[None, :], axis=1)
        picker = (rank[None, :] == place[:, None]) & chosen[None, :]
        slots = (left_at * deep + left % deep) * 1024 + right_at * deep + right % deep
        slots = jnp.sum(jnp.where(picker, slots[None, :], 0), axis=1)
        views = jnp.sum(jnp.where(picker, (left * 1024 + right)[None, :], 0), axis=1)
        used = ((left_at[:, None] == names) | (right_at[:, None] == names)) & chosen[:, None]
        counts = jnp.concatenate([jnp.sum(chosen.astype(jnp.int32)).reshape(1), jnp.any(used, axis=0).astype(jnp.int32)])
        lists += [jnp.pad(counts, (0, count - counts.shape[0])), slots, views]
    return jnp.stack(lists)


def list_kernel(order, views_dev, mine_ref, pairs_ref, out_ref):
    owners, count = mine_ref.shape[0], pairs_ref.shape[1]
    deep = views_dev // PIECES
    far_off = float(2**23)
    place = lax.broadcasted_iota(jnp.int32, (1, count), 1).astype(jnp.float32)
    steps = lambda x, width, most: sum((x >= k * width).astype(jnp.int32) for k in range(1, most))
    left, right = pairs_ref[0:1, :], pairs_ref[1:2, :]
    left_owner, right_owner = steps(left, views_dev, owners), steps(right, views_dev, owners)
    right_is = [right_owner == b for b in range(owners)]
    found = jnp.zeros((1, count), jnp.int32)
    for a in range(owners):
        row = jnp.zeros((1, count), jnp.int32)
        for b in range(owners):
            row = jnp.where(right_is[b], mine_ref[a, b], row)
        found = jnp.where(left_owner == a, row, found)
    buffers = jnp.maximum(found - 1, 0)
    left_view, right_view = left - left_owner * views_dev, right - right_owner * views_dev
    left_part, right_part = steps(left_view, deep, PIECES), steps(right_view, deep, PIECES)
    left_piece = lax.shift_right_logical(buffers, 6) * PIECES + left_part
    right_piece = lax.bitwise_and(buffers, 63) * PIECES + right_part
    column = lambda x: jnp.broadcast_to(x, (LANES, count)).T[:, 0:1]
    views = column((left * 1024 + right).astype(jnp.float32))
    free = found > 0
    for phase, where in enumerate(order):
        left_at, right_at = jnp.full((1, count), -1, jnp.int32), jnp.full((1, count), -1, jnp.int32)
        for name, at in enumerate(where):
            if at >= 0:
                left_at = jnp.where(left_piece == name, at, left_at)
                right_at = jnp.where(right_piece == name, at, right_at)
        chosen = free & (left_at >= 0) & (right_at >= 0)
        free = free & jnp.logical_not(chosen)
        key = jnp.where(chosen, jnp.maximum(left_at, right_at).astype(jnp.float32) * count + place, far_off)
        slots = (left_at * deep + left_view - left_part * deep) * 1024
        slots = (slots + right_at * deep + right_view - right_part * deep).astype(jnp.float32)
        own_key = column(key)
        rank = jnp.sum(jnp.where(key < own_key, 1.0, 0.0), axis=1, keepdims=True)
        rank = jnp.where(own_key < far_off, rank, -1.0)
        hit = rank == place
        out_ref[3 * phase + 1 : 3 * phase + 2, :] = jnp.sum(jnp.where(hit, column(slots), 0.0), axis=0, keepdims=True).astype(jnp.int32)
        out_ref[3 * phase + 2 : 3 * phase + 3, :] = jnp.sum(jnp.where(hit, views, 0.0), axis=0, keepdims=True).astype(jnp.int32)
        picked = jnp.where(chosen, 1.0, 0.0)
        lane = lax.broadcasted_iota(jnp.int32, (1, LANES), 1)
        counts = jnp.where(lane == 0, jnp.sum(picked, axis=1, keepdims=True), 0.0)
        for at in range(sum(x >= 0 for x in where)):
            uses = jnp.where((left_at == at) | (right_at == at), picked, 0.0)
            counts = jnp.where(lane == at + 1, jnp.max(uses, axis=1, keepdims=True), counts)
        out_ref[3 * phase : 3 * phase + 1, 0:LANES] = counts.astype(jnp.int32)


def quick_lists(pairs, mine, order, views_dev):
    count = pairs.shape[1]
    vmem = pl.BlockSpec(memory_space=pltpu.VMEM)
    return pl.pallas_call(
        functools.partial(list_kernel, order.tolist(), views_dev),
        out_shape=jax.ShapeDtypeStruct((3 * len(order), count), jnp.int32),
        in_specs=[pl.BlockSpec(memory_space=pltpu.SMEM), vmem],
        out_specs=vmem,
        compiler_params=pltpu.CompilerParams(vmem_limit_bytes=32 * 1024 * 1024),
        cost_estimate=pl.CostEstimate(flops=1, bytes_accessed=0, transcendentals=0),
    )(mine, pairs)


def kernel(pieces, row, score_scale, lists_ref, before_ref, *refs):
    sources = refs[:-7]
    out_ref, arena, held, by_row, by_col, bounds, sems = refs[-7:]
    length = arena.shape[1]
    deep = arena.shape[0] // len(pieces)
    total = lists_ref[row, 0]
    limit = lists_ref.shape[1] - 1

    def slots_of(p):
        packed = lists_ref[row + 1, jnp.minimum(p, limit)]
        return lax.shift_right_logical(packed, 10), lax.bitwise_and(packed, 1023)

    def wait_until(needed, waited):
        def wait(k, carry):
            part = arena.at[pl.ds(0, deep)]
            pl.when(lists_ref[row, k + 1] > 0)(lambda: pltpu.make_async_copy(part, part, sems.at[k]).wait())
            return carry

        lax.fori_loop(waited, needed, wait, 0)
        return jnp.maximum(waited, needed)

    def product(p):
        left, right = slots_of(p)
        return lax.dot_general(
            arena[left], arena[right], (((1,), (1,)), ((), ())), preferred_element_type=jnp.float32
        )

    def record(p, row_conf, col_conf):
        packed = lists_ref[row + 2, jnp.minimum(p, limit)]
        real = p < total
        left = jnp.where(real, lax.shift_right_logical(packed, 10), -1)
        right = jnp.where(real, lax.bitwise_and(packed, 1023), by_row.shape[1])
        for tile in range(by_row.shape[1] // LANES):
            lane = lax.broadcasted_iota(jnp.int32, (length, LANES), 1) + tile * LANES
            at = (slice(None), slice(tile * LANES, (tile + 1) * LANES))
            by_row[at] = jnp.maximum(by_row[at], jnp.where(lane == left, row_conf, 0.0))
        by_col[pl.ds(right, 1), :] = jnp.maximum(by_col[pl.ds(right, 1), :], col_conf)

    def plain(p, scores):
        weight = jnp.exp2(scores[...] * (score_scale / math.log(2.0)))
        row_sum = jnp.sum(weight, axis=1, keepdims=True)
        col_sum = jnp.sum(weight, axis=0, keepdims=True)
        least = jnp.minimum(jnp.min(row_sum, axis=0, keepdims=True), jnp.min(col_sum, axis=1, keepdims=True))
        most = jnp.max(col_sum, axis=1, keepdims=True)
        bounds[0] = jnp.minimum(bounds[0], jnp.where(p < total, least, 1.0))
        bounds[1] = jnp.maximum(bounds[1], jnp.where(p < total, most, 1.0))
        row_inv, col_inv = lax.rsqrt(row_sum), lax.rsqrt(col_sum)
        row_top = jnp.max(weight * col_inv, axis=1, keepdims=True) * row_inv
        col_top = jnp.max(weight * row_inv, axis=0, keepdims=True) * col_inv
        record(p, row_top * row_top, col_top * col_top)

    def shifted(p, carry):
        held[0] = product(p) * score_scale
        value = held[0]
        row_peak = jnp.max(value, axis=1, keepdims=True)
        row_total = row_peak + jnp.log(jnp.sum(jnp.exp(value - row_peak), axis=1, keepdims=True))
        col_peak = jnp.max(value, axis=0, keepdims=True)
        col_total = col_peak + jnp.log(jnp.sum(jnp.exp(value - col_peak), axis=0, keepdims=True))
        value = (value - row_total) + (value - col_total)
        record(p, jnp.exp(jnp.max(value, axis=1, keepdims=True)), jnp.exp(jnp.max(value, axis=0, keepdims=True)))
        return carry

    def clear():
        by_row[...] = jnp.zeros_like(by_row)
        by_col[...] = jnp.zeros_like(by_col)

    for place, (source, first) in enumerate(pieces):
        piece = pltpu.make_async_copy(
            sources[source].at[pl.ds(first, deep)], arena.at[pl.ds(place * deep, deep)], sems.at[place]
        )
        pl.when(lists_ref[row, place + 1] > 0)(piece.start)
    clear()
    bounds[...] = jnp.ones_like(bounds)

    def load(first, at, waited):
        needed = 1
        for g in range(GROUP):
            left, right = slots_of(first + g)
            needed = jnp.maximum(needed, lax.div(jnp.maximum(left, right), deep) + 1)
        waited = wait_until(needed, waited)
        for g in range(GROUP):
            held[at * GROUP + g] = product(first + g)
        return waited

    def rounds(k, waited):
        first = 2 * GROUP * k
        for at in range(2):
            waited = load(first + (at + 1) * GROUP, 1 - at, waited)
            for g in range(GROUP):
                plain(first + at * GROUP + g, held.at[at * GROUP + g])
        return waited

    @pl.when(total > 0)
    def all_pairs():
        waited = load(0, 0, jnp.int32(0))
        waited = lax.fori_loop(0, lax.div(total + 2 * GROUP - 1, 2 * GROUP), rounds, waited)
        wait_until(jnp.int32(len(pieces)), waited)

    fine = (jnp.min(bounds[0]) >= SUM_LOW) & (jnp.max(bounds[1]) <= SUM_HIGH)

    @pl.when(jnp.logical_not(fine))
    def again():
        clear()
        lax.fori_loop(0, total, shifted, 0)

    result = jnp.maximum(by_row[...].T, by_col[: by_row.shape[1], :]).astype(jnp.bfloat16)
    out_ref[...] = jnp.maximum(result, before_ref[...])


def confidences(lists, phase, before, sources, pieces, deep, score_scale, work):
    padded, length = before.shape
    width = sources[0].shape[2]
    smem = pl.BlockSpec(memory_space=pltpu.SMEM)
    vmem = pl.BlockSpec(memory_space=pltpu.VMEM)
    return pl.pallas_call(
        functools.partial(kernel, pieces, 3 * phase, score_scale),
        out_shape=jax.ShapeDtypeStruct(before.shape, jnp.bfloat16),
        in_specs=[smem, vmem] + [pl.BlockSpec(memory_space=pl.ANY)] * len(sources),
        out_specs=vmem,
        scratch_shapes=[
            pltpu.VMEM((len(pieces) * deep, length, width), jnp.bfloat16),
            pltpu.VMEM((2 * GROUP, length, length), jnp.float32),
            pltpu.VMEM((length, padded), jnp.float32),
            pltpu.VMEM((padded + 8, length), jnp.float32),
            pltpu.VMEM((2, 1, 1), jnp.float32),
            pltpu.SemaphoreType.DMA((len(pieces),)),
        ],
        compiler_params=pltpu.CompilerParams(vmem_limit_bytes=56 * 1024 * 1024),
        cost_estimate=pl.CostEstimate(flops=work, bytes_accessed=0, transcendentals=0),
    )(lists, before, *sources)


def gather_small_slice(features, pairs, moves, make_lists):
    send = lambda x, name: lax.ppermute(x, "owner", moves[name])
    tie = lax.optimization_barrier
    flat = pairs.T.reshape(1, -1)
    shift = lambda s: [(i, (i + 4 * s) % 16) for i in range(16)]
    flat = jnp.concatenate([flat] + [lax.ppermute(flat, "owner", shift(s)) for s in (1, 2, 3)])
    own, flat = tie((features, flat))
    near, high = send(own, "near"), send(own, "high")
    flat = jnp.concatenate([flat, send(flat, "side")])
    own, flat = tie((features, flat))
    side = send(own, "side")
    flat = jnp.concatenate([flat, send(flat, "core")])
    lists = make_lists(flat.reshape(16, 2, -1).transpose(1, 0, 2).reshape(2, -1))
    half = features.shape[0] // PIECES
    halves = [features[:half], features[half:]]
    own_swapped = send(features, "core")
    near, high, lists, own_swapped, *halves = tie((near, high, lists, own_swapped, *halves))
    far, cross = [send(halves[0], "far")], [send(halves[0], "cross")]
    swapped = [send(x, "core") for x in (near, high)]
    second, swapped[0] = tie((halves[1], swapped[0]))
    far.append(send(second, "far"))
    cross.append(send(second, "cross"))
    swapped.append(send(side, "core"))
    return lists, [features, near, high, side, far, cross, *swapped, [], own_swapped]


def local(features, pairs):
    owners = lax.axis_size("owner")
    views_dev, length, width = features.shape
    flows, phases, table, order = make_plan(owners)
    mine = jnp.asarray(table)[lax.axis_index("owner")]
    if owners == 16:
        make_lists = lambda everyone: quick_lists(everyone, mine, order, views_dev)
        lists, buffers = gather_small_slice(features, pairs, small_slice_moves(), make_lists)
    else:
        everyone = lax.all_gather(pairs, "owner", axis=0, tiled=True)
        buffers = [features] + [lax.ppermute(features, "owner", perm) for _, perm in flows]
        lists = pair_lists(everyone, mine, order, views_dev)
    deep = views_dev // PIECES
    padded = (owners * views_dev + LANES - 1) // LANES * LANES
    best = jnp.zeros((padded, length), jnp.bfloat16)
    for phase, wanted in enumerate(phases):
        if phase > 0:
            far, best = lax.optimization_barrier((buffers[4][phase - 1], best))
            buffers[LATE_BUFFER].append(lax.ppermute(far, "owner", small_slice_moves()["core"]))
        sources, pieces = [], []
        for k, piece in wanted:
            cut = isinstance(buffers[k], list)
            part = buffers[k][piece] if cut else buffers[k]
            if not any(part is x for x in sources):
                sources.append(part)
            pieces.append(([part is x for x in sources].index(True), 0 if cut else piece * deep))
        best = confidences(lists, phase, best, sources, tuple(pieces), deep, 10.0 / width, 10**8)
    outgoing = best[: owners * views_dev].reshape(owners, views_dev, length)
    returned = lax.all_to_all(outgoing, "owner", split_axis=0, concat_axis=0, tiled=True)
    return jnp.max(returned, axis=0)


def solution(mesh):
    placed = (P(("groups", "owner"), None, None), P(("groups", "owner"), None))
    return jax.shard_map(
        local, mesh=mesh, in_specs=placed, out_specs=P(("groups", "owner"), None), check_vma=False
    )
```

```python
import functools
import math

import jax
import jax.numpy as jnp
import numpy as np
from jax import lax
from jax.experimental import pallas as pl
from jax.experimental.pallas import tpu as pltpu
from jax.sharding import PartitionSpec as P

LANES = 128
SUM_LOW, SUM_HIGH = 1e-28, 1e35


PIECES = 2
GROUP = 2


def small_slice_moves():
    at = lambda z, y, c: (z * 2 + y) * 2 + c
    yc = [(y, c) for y in range(2) for c in range(2)]
    step = lambda z, t: [(at(z, y, c), at(t, y, c)) for y, c in yc]
    return dict(
        near=step(1, 2) + step(0, 1),
        high=step(3, 2) + step(2, 3),
        side=[(at(z, y, c), at(z, 1 - y, c)) for z in range(4) for y, c in yc],
        far=step(0, 2),
        cross=[(at(3, 1 - y, c), at(2, y, c)) for y, c in yc],
        core=[(i, i ^ 1) for i in range(16)],
    )


SMALL_FLOWS = [
    (0, "near"),
    (0, "high"),
    (0, "side"),
    (0, "far"),
    (0, "cross"),
    (1, "core"),
    (2, "core"),
    (3, "core"),
    (4, "core"),
    (0, "core"),
]
LATE_BUFFER = 9
EARLY = [(k, piece) for k in (0, 10, 3, 8, 2, 7, 1, 6) for piece in range(PIECES)]
SMALL_PHASES = [
    EARLY,
    [(4, 0)] + EARLY + [(5, 0)],
    [(4, 1)] + EARLY + [(5, 0), (5, 1), (4, 0), (9, 0), (9, 1)],
]


def cyclic_distances(owners):
    step = max(1, math.isqrt(owners // 2))
    reach = set(range(step))
    top = step - 1
    while top < owners // 2:
        top += step
        reach.add(top)
    return sorted({d % owners for d in reach} - {0})


@functools.lru_cache(None)
def make_plan(owners):
    if owners == 16:
        moves = small_slice_moves()
        flows = [(source, moves[name]) for source, name in SMALL_FLOWS]
        phases = SMALL_PHASES
    else:
        flows = [(0, [((i + d) % owners, i) for i in range(owners)]) for d in cyclic_distances(owners)]
        phases = [[(k, piece) for k in range(len(flows) + 1) for piece in range(PIECES)]]
    held = [[d] for d in range(owners)]
    for source, perm in flows:
        arrived = {t: held[s][source] for s, t in perm}
        for d in range(owners):
            held[d].append(arrived.get(d, -1))
    first = [{} for _ in range(owners)]
    for d in range(owners):
        for k, o in enumerate(held[d]):
            if o >= 0:
                first[d].setdefault(o, k)
    table = np.zeros((owners, owners, owners), np.int32)
    load = np.zeros(owners)
    choices = []
    for a in range(owners):
        for b in range(a, owners):
            at = [d for d in range(owners) if a in first[d] and b in first[d]]
            assert at
            choices.append((len(at), a, b, at))
    for _, a, b, at in sorted(choices):
        late = lambda d: owners == 16 and LATE_BUFFER in (first[d][a], first[d][b])
        d = min(at, key=lambda d: (late(d), load[d], d))
        load[d] += 1 if a == b else 2
        table[d, a, b] = first[d][a] * 64 + first[d][b] + 1
        table[d, b, a] = first[d][b] * 64 + first[d][a] + 1
    order = np.full((len(phases), (len(flows) + 1) * PIECES), -1, np.int32)
    for phase, pieces in enumerate(phases):
        for place, (k, piece) in enumerate(pieces):
            order[phase, k * PIECES + piece] = place
    return flows, phases, table, order


def pair_lists(pairs, mine, order, views_dev):
    count, owners = pairs.shape[0], mine.shape[0]
    left, right = pairs[:, 0], pairs[:, 1]
    is_left = (left // views_dev)[:, None] == jnp.arange(owners)[None, :]
    is_right = (right // views_dev)[:, None] == jnp.arange(owners)[None, :]
    row = jnp.dot(is_left.astype(jnp.float32), mine.astype(jnp.float32), precision=lax.Precision.HIGHEST)
    found = jnp.sum(jnp.where(is_right, row, 0.0), axis=1).astype(jnp.int32)
    buffers = jnp.maximum(found - 1, 0)
    deep = views_dev // PIECES
    left_piece = (buffers // 64) * PIECES + (left % views_dev) // deep
    right_piece = (buffers % 64) * PIECES + (right % views_dev) // deep
    place = jnp.arange(count)
    free = found > 0
    lists = []
    for phase in range(order.shape[0]):
        where = jnp.asarray(order[phase])[None, :]
        names = jnp.arange(order.shape[1])[None, :]
        left_at = jnp.sum(jnp.where(left_piece[:, None] == names, where, 0), axis=1)
        right_at = jnp.sum(jnp.where(right_piece[:, None] == names, where, 0), axis=1)
        chosen = free & (left_at >= 0) & (right_at >= 0)
        free = free & jnp.logical_not(chosen)
        key = jnp.maximum(left_at, right_at) * count + place
        rank = jnp.sum((key[None, :] < key[:, None]) & chosen[None, :], axis=1)
        picker = (rank[None, :] == place[:, None]) & chosen[None, :]
        slots = (left_at * deep + left % deep) * 1024 + right_at * deep + right % deep
        slots = jnp.sum(jnp.where(picker, slots[None, :], 0), axis=1)
        views = jnp.sum(jnp.where(picker, (left * 1024 + right)[None, :], 0), axis=1)
        used = ((left_at[:, None] == names) | (right_at[:, None] == names)) & chosen[:, None]
        counts = jnp.concatenate([jnp.sum(chosen.astype(jnp.int32)).reshape(1), jnp.any(used, axis=0).astype(jnp.int32)])
        lists += [jnp.pad(counts, (0, count - counts.shape[0])), slots, views]
    return jnp.stack(lists)


def list_kernel(order, views_dev, mine_ref, pairs_ref, out_ref):
    owners, count = mine_ref.shape[0], pairs_ref.shape[1]
    deep = views_dev // PIECES
    far_off = float(2**23)
    place = lax.broadcasted_iota(jnp.int32, (1, count), 1).astype(jnp.float32)
    steps = lambda x, width, most: sum((x >= k * width).astype(jnp.int32) for k in range(1, most))
    left, right = pairs_ref[0:1, :], pairs_ref[1:2, :]
    left_owner, right_owner = steps(left, views_dev, owners), steps(right, views_dev, owners)
    right_is = [right_owner == b for b in range(owners)]
    found = jnp.zeros((1, count), jnp.int32)
    for a in range(owners):
        row = jnp.zeros((1, count), jnp.int32)
        for b in range(owners):
            row = jnp.where(right_is[b], mine_ref[a, b], row)
        found = jnp.where(left_owner == a, row, found)
    buffers = jnp.maximum(found - 1, 0)
    left_view, right_view = left - left_owner * views_dev, right - right_owner * views_dev
    left_part, right_part = steps(left_view, deep, PIECES), steps(right_view, deep, PIECES)
    left_piece = lax.shift_right_logical(buffers, 6) * PIECES + left_part
    right_piece = lax.bitwise_and(buffers, 63) * PIECES + right_part
    column = lambda x: jnp.broadcast_to(x, (LANES, count)).T[:, 0:1]
    views = column((left * 1024 + right).astype(jnp.float32))
    free = found > 0
    for phase, where in enumerate(order):
        left_at, right_at = jnp.full((1, count), -1, jnp.int32), jnp.full((1, count), -1, jnp.int32)
        for name, at in enumerate(where):
            if at >= 0:
                left_at = jnp.where(left_piece == name, at, left_at)
                right_at = jnp.where(right_piece == name, at, right_at)
        chosen = free & (left_at >= 0) & (right_at >= 0)
        free = free & jnp.logical_not(chosen)
        key = jnp.where(chosen, jnp.maximum(left_at, right_at).astype(jnp.float32) * count + place, far_off)
        slots = (left_at * deep + left_view - left_part * deep) * 1024
        slots = (slots + right_at * deep + right_view - right_part * deep).astype(jnp.float32)
        own_key = column(key)
        rank = jnp.sum(jnp.where(key < own_key, 1.0, 0.0), axis=1, keepdims=True)
        rank = jnp.where(own_key < far_off, rank, -1.0)
        hit = rank == place
        out_ref[3 * phase + 1 : 3 * phase + 2, :] = jnp.sum(jnp.where(hit, column(slots), 0.0), axis=0, keepdims=True).astype(jnp.int32)
        out_ref[3 * phase + 2 : 3 * phase + 3, :] = jnp.sum(jnp.where(hit, views, 0.0), axis=0, keepdims=True).astype(jnp.int32)
        picked = jnp.where(chosen, 1.0, 0.0)
        lane = lax.broadcasted_iota(jnp.int32, (1, LANES), 1)
        counts = jnp.where(lane == 0, jnp.sum(picked, axis=1, keepdims=True), 0.0)
        for at in range(sum(x >= 0 for x in where)):
            uses = jnp.where((left_at == at) | (right_at == at), picked, 0.0)
            counts = jnp.where(lane == at + 1, jnp.max(uses, axis=1, keepdims=True), counts)
        out_ref[3 * phase : 3 * phase + 1, 0:LANES] = counts.astype(jnp.int32)


def quick_lists(pairs, mine, order, views_dev):
    count = pairs.shape[1]
    vmem = pl.BlockSpec(memory_space=pltpu.VMEM)
    return pl.pallas_call(
        functools.partial(list_kernel, order.tolist(), views_dev),
        out_shape=jax.ShapeDtypeStruct((3 * len(order), count), jnp.int32),
        in_specs=[pl.BlockSpec(memory_space=pltpu.SMEM), vmem],
        out_specs=vmem,
        compiler_params=pltpu.CompilerParams(vmem_limit_bytes=32 * 1024 * 1024),
        cost_estimate=pl.CostEstimate(flops=1, bytes_accessed=0, transcendentals=0),
    )(mine, pairs)


def kernel(pieces, row, score_scale, lists_ref, before_ref, *refs):
    sources = refs[:-7]
    out_ref, arena, held, by_row, by_col, bounds, sems = refs[-7:]
    length = arena.shape[1]
    deep = arena.shape[0] // len(pieces)
    total = lists_ref[row, 0]
    limit = lists_ref.shape[1] - 1

    def slots_of(p):
        packed = lists_ref[row + 1, jnp.minimum(p, limit)]
        return lax.shift_right_logical(packed, 10), lax.bitwise_and(packed, 1023)

    def wait_until(needed, waited):
        def wait(k, carry):
            part = arena.at[pl.ds(0, deep)]
            pl.when(lists_ref[row, k + 1] > 0)(lambda: pltpu.make_async_copy(part, part, sems.at[k]).wait())
            return carry

        lax.fori_loop(waited, needed, wait, 0)
        return jnp.maximum(waited, needed)

    def product(p):
        left, right = slots_of(p)
        return lax.dot_general(
            arena[left], arena[right], (((1,), (1,)), ((), ())), preferred_element_type=jnp.float32
        )

    def record(p, row_conf, col_conf):
        packed = lists_ref[row + 2, jnp.minimum(p, limit)]
        real = p < total
        left = jnp.where(real, lax.shift_right_logical(packed, 10), -1)
        right = jnp.where(real, lax.bitwise_and(packed, 1023), by_row.shape[1])
        for tile in range(by_row.shape[1] // LANES):
            lane = lax.broadcasted_iota(jnp.int32, (length, LANES), 1) + tile * LANES
            at = (slice(None), slice(tile * LANES, (tile + 1) * LANES))
            by_row[at] = jnp.maximum(by_row[at], jnp.where(lane == left, row_conf, 0.0))
        by_col[pl.ds(right, 1), :] = jnp.maximum(by_col[pl.ds(right, 1), :], col_conf)

    def plain(p, scores):
        weight = jnp.exp2(scores[...] * (score_scale / math.log(2.0)))
        row_sum = jnp.sum(weight, axis=1, keepdims=True)
        col_sum = jnp.sum(weight, axis=0, keepdims=True)
        least = jnp.minimum(jnp.min(row_sum, axis=0, keepdims=True), jnp.min(col_sum, axis=1, keepdims=True))
        most = jnp.max(col_sum, axis=1, keepdims=True)
        bounds[0] = jnp.minimum(bounds[0], jnp.where(p < total, least, 1.0))
        bounds[1] = jnp.maximum(bounds[1], jnp.where(p < total, most, 1.0))
        row_inv, col_inv = lax.rsqrt(row_sum), lax.rsqrt(col_sum)
        row_top = jnp.max(weight * col_inv, axis=1, keepdims=True) * row_inv
        col_top = jnp.max(weight * row_inv, axis=0, keepdims=True) * col_inv
        record(p, row_top * row_top, col_top * col_top)

    def shifted(p, carry):
        held[0] = product(p) * score_scale
        value = held[0]
        row_peak = jnp.max(value, axis=1, keepdims=True)
        row_total = row_peak + jnp.log(jnp.sum(jnp.exp(value - row_peak), axis=1, keepdims=True))
        col_peak = jnp.max(value, axis=0, keepdims=True)
        col_total = col_peak + jnp.log(jnp.sum(jnp.exp(value - col_peak), axis=0, keepdims=True))
        value = (value - row_total) + (value - col_total)
        record(p, jnp.exp(jnp.max(value, axis=1, keepdims=True)), jnp.exp(jnp.max(value, axis=0, keepdims=True)))
        return carry

    def clear():
        by_row[...] = jnp.zeros_like(by_row)
        by_col[...] = jnp.zeros_like(by_col)

    for place, (source, first) in enumerate(pieces):
        piece = pltpu.make_async_copy(
            sources[source].at[pl.ds(first, deep)], arena.at[pl.ds(place * deep, deep)], sems.at[place]
        )
        pl.when(lists_ref[row, place + 1] > 0)(piece.start)
    clear()
    bounds[...] = jnp.ones_like(bounds)

    def load(first, at, waited):
        needed = 1
        for g in range(GROUP):
            left, right = slots_of(first + g)
            needed = jnp.maximum(needed, lax.div(jnp.maximum(left, right), deep) + 1)
        waited = wait_until(needed, waited)
        for g in range(GROUP):
            held[at * GROUP + g] = product(first + g)
        return waited

    def rounds(k, waited):
        first = 2 * GROUP * k
        for at in range(2):
            waited = load(first + (at + 1) * GROUP, 1 - at, waited)
            for g in range(GROUP):
                plain(first + at * GROUP + g, held.at[at * GROUP + g])
        return waited

    @pl.when(total > 0)
    def all_pairs():
        waited = load(0, 0, jnp.int32(0))
        waited = lax.fori_loop(0, lax.div(total + 2 * GROUP - 1, 2 * GROUP), rounds, waited)
        wait_until(jnp.int32(len(pieces)), waited)

    fine = (jnp.min(bounds[0]) >= SUM_LOW) & (jnp.max(bounds[1]) <= SUM_HIGH)

    @pl.when(jnp.logical_not(fine))
    def again():
        clear()
        lax.fori_loop(0, total, shifted, 0)

    result = jnp.maximum(by_row[...].T, by_col[: by_row.shape[1], :]).astype(jnp.bfloat16)
    out_ref[...] = jnp.maximum(result, before_ref[...])


def confidences(lists, phase, before, sources, pieces, deep, score_scale, work):
    padded, length = before.shape
    width = sources[0].shape[2]
    smem = pl.BlockSpec(memory_space=pltpu.SMEM)
    vmem = pl.BlockSpec(memory_space=pltpu.VMEM)
    return pl.pallas_call(
        functools.partial(kernel, pieces, 3 * phase, score_scale),
        out_shape=jax.ShapeDtypeStruct(before.shape, jnp.bfloat16),
        in_specs=[smem, vmem] + [pl.BlockSpec(memory_space=pl.ANY)] * len(sources),
        out_specs=vmem,
        scratch_shapes=[
            pltpu.VMEM((len(pieces) * deep, length, width), jnp.bfloat16),
            pltpu.VMEM((2 * GROUP, length, length), jnp.float32),
            pltpu.VMEM((length, padded), jnp.float32),
            pltpu.VMEM((padded + 8, length), jnp.float32),
            pltpu.VMEM((2, 1, 1), jnp.float32),
            pltpu.SemaphoreType.DMA((len(pieces),)),
        ],
        compiler_params=pltpu.CompilerParams(vmem_limit_bytes=56 * 1024 * 1024),
        cost_estimate=pl.CostEstimate(flops=work, bytes_accessed=0, transcendentals=0),
    )(lists, before, *sources)


def gather_small_slice(features, pairs, moves, make_lists):
    send = lambda x, name: lax.ppermute(x, "owner", moves[name])
    tie = lax.optimization_barrier
    flat = pairs.reshape(1, -1)
    shift = lambda s: [(i, (i + 4 * s) % 16) for i in range(16)]
    flat = jnp.concatenate([flat] + [lax.ppermute(flat, "owner", shift(s)) for s in (1, 2, 3)])
    own, flat = tie((features, flat))
    near, high = send(own, "near"), send(own, "high")
    flat = jnp.concatenate([flat, send(flat, "side")])
    own, flat = tie((features, flat))
    side = send(own, "side")
    flat = jnp.concatenate([flat, send(flat, "core")])
    lists = make_lists(flat.reshape(-1, 2).T)
    half = features.shape[0] // PIECES
    halves = [features[:half], features[half:]]
    own_swapped = send(features, "core")
    near, high, lists, own_swapped, *halves = tie((near, high, lists, own_swapped, *halves))
    far, cross = [send(halves[0], "far")], [send(halves[0], "cross")]
    swapped = [send(x, "core") for x in (near, high)]
    second, swapped[0] = tie((halves[1], swapped[0]))
    far.append(send(second, "far"))
    cross.append(send(second, "cross"))
    swapped.append(send(side, "core"))
    return lists, [features, near, high, side, far, cross, *swapped, [], own_swapped]


def local(features, pairs):
    owners = lax.axis_size("owner")
    views_dev, length, width = features.shape
    flows, phases, table, order = make_plan(owners)
    mine = jnp.asarray(table)[lax.axis_index("owner")]
    if owners == 16:
        make_lists = lambda everyone: quick_lists(everyone, mine, order, views_dev)
        lists, buffers = gather_small_slice(features, pairs, small_slice_moves(), make_lists)
    else:
        everyone = lax.all_gather(pairs, "owner", axis=0, tiled=True)
        buffers = [features] + [lax.ppermute(features, "owner", perm) for _, perm in flows]
        lists = pair_lists(everyone, mine, order, views_dev)
    deep = views_dev // PIECES
    padded = (owners * views_dev + LANES - 1) // LANES * LANES
    best = jnp.zeros((padded, length), jnp.bfloat16)
    for phase, wanted in enumerate(phases):
        if phase > 0:
            far, best = lax.optimization_barrier((buffers[4][phase - 1], best))
            buffers[LATE_BUFFER].append(lax.ppermute(far, "owner", small_slice_moves()["core"]))
        sources, pieces = [], []
        for k, piece in wanted:
            cut = isinstance(buffers[k], list)
            part = buffers[k][piece] if cut else buffers[k]
            if not any(part is x for x in sources):
                sources.append(part)
            pieces.append(([part is x for x in sources].index(True), 0 if cut else piece * deep))
        best = confidences(lists, phase, best, sources, tuple(pieces), deep, 10.0 / width, 10**8)
    outgoing = best[: owners * views_dev].reshape(owners, views_dev, length)
    returned = lax.all_to_all(outgoing, "owner", split_axis=0, concat_axis=0, tiled=True)
    return jnp.max(returned, axis=0)


def solution(mesh):
    placed = (P(("groups", "owner"), None, None), P(("groups", "owner"), None))
    return jax.shard_map(
        local, mesh=mesh, in_specs=placed, out_specs=P(("groups", "owner"), None), check_vma=False
    )
```
